32 devices in a mesh: seq: 8 (over y, x, core), slot: 4 (over z).
Axes of the slice: x: 2, y: 2, z: 4, core: 2. Of those that a mesh axis runs over, the one named last changes fastest.
Arguments:
- tokens: bfloat16 [4, 1024, 1024], P('slot', 'seq'), may hold values from -6 to 6
- lengths: int32 [4], P('slot'), may hold values from 897 to 1024, as said below
- query_weight: bfloat16 [1024, 1024], P('seq'), may hold values from -0.1875 to 0.1875
- key_weight: bfloat16 [1024, 512], P('seq'), may hold values from -0.1875 to 0.1875
- value_weight: bfloat16 [1024, 512], P('seq'), may hold values from -0.1875 to 0.1875
- out_weight: bfloat16 [1024, 1024], P('seq'), may hold values from -1.5 to 1.5
- gate_weight: bfloat16 [1024, 4608], P('seq'), may hold values from -0.1875 to 0.1875
- up_weight: bfloat16 [1024, 4608], P('seq'), may hold values from -0.1875 to 0.1875
- down_weight: bfloat16 [1024, 4608], P('seq'), may hold values from -0.09375 to 0.09375
- attn_norm: float32 [1024], replicated, may hold values from 0.5 to 1.5
- query_norm: float32 [64], replicated, may hold values from 0.1 to 1.9
- key_norm: float32 [64], replicated, may hold values from 0.1 to 1.9
- ffn_norm: float32 [1024], replicated, may hold values from 0.5 to 1.5
- out_grad: bfloat16 [4, 1024, 1024], P('slot', 'seq'), may hold values from -6 to 6
Outputs:
- mixed: bfloat16 [4, 1024, 1024], P('slot', 'seq')
- input_grad: bfloat16 [4, 1024, 1024], P('slot', 'seq')
- query_weight_grad: float32 [1024, 1024], P('seq')
- key_weight_grad: float32 [1024, 512], P('seq')
- value_weight_grad: float32 [1024, 512], P('seq')
- out_weight_grad: float32 [1024, 1024], P('seq')
- gate_weight_grad: float32 [1024, 4608], P('seq')
- up_weight_grad: float32 [1024, 4608], P('seq')
- down_weight_grad: float32 [1024, 4608], P('seq')
- attn_norm_grad: float32 [1024], replicated
- query_norm_grad: float32 [64], replicated
- key_norm_grad: float32 [64], replicated
- ffn_norm_grad: float32 [1024], replicated
The draws below stay inside these ranges and needn't reach their ends.
Inputs may be any that keep to these rules, and one draw needn't show every extreme that they name: `lengths`: each slot's true length is more than 896; some slot's length is exactly 1024.
All inputs are finite; a program needn't handle non-finite values.
Results may differ from the reference program's by a relative error of at most 0.035.
Values may be sent and summed in bfloat16 or wider, within the bound.
No kernel may reach another device: no remote copies, remote signals or barrier semaphores. Data moves between devices by JAX's collectives and lax.ppermute only.
A program may use at most 320 MiB of HBM per device.

```python
import jax
import jax.numpy as jnp
from jax import lax

D = 1024
FF = 4608
HEADS = 16
KV_HEADS = 8
HEAD_DIM = 64
TOK_DEV = 128
SEQLEN = 1024
SLOTS = 4


def draw_lengths(key, part):
    key = jax.random.fold_in(key, 7)
    length_key, pick_key = jax.random.split(key)
    drawn = jax.random.randint(length_key, (SLOTS,), SEQLEN - TOK_DEV + 1, SEQLEN + 1)
    chosen = jax.random.randint(pick_key, (), 0, SLOTS)
    return jnp.where(jnp.arange(SLOTS) == chosen, SEQLEN, drawn).astype(jnp.int32)


def levels(key, dims, shards, smallest, largest):
    loudness, own = 1.0, jax.random.fold_in(key, 6)
    for dim, parts in shards:
        heights = jnp.exp(jax.random.uniform(jax.random.fold_in(own, dim), (parts,), jnp.float32, smallest / len(shards), largest / len(shards)))
        loudness = loudness * jnp.repeat(heights, dims[dim] // parts).reshape([-1 if axis == dim else 1 for axis in range(len(dims))])
    return loudness


def centred(stream_key, dims, width, bound, shards=(), kind=jnp.bfloat16):
    loudness = levels(stream_key, dims, shards, -0.22, 0.18) if shards else 1.0
    values = jax.random.normal(stream_key, dims, jnp.float32) * width * loudness
    return jnp.minimum(jnp.maximum(values, -bound), bound).astype(kind)


def setup_inputs(seed: int = 0) -> dict:
    streams_of = jax.random.split(jax.random.key(seed), 15)
    tokens = centred(streams_of[0], (SLOTS, SEQLEN, D), 1.0, 6.0, ((0, 4), (1, 8)))
    lengths = draw_lengths(jax.random.fold_in(streams_of[14], 71), 0)
    query_weight = centred(streams_of[2], (D, HEADS * HEAD_DIM), D ** -0.5, 0.1875, ((0, 8),))
    key_weight = centred(streams_of[3], (D, KV_HEADS * HEAD_DIM), D ** -0.5, 0.1875, ((0, 8),))
    value_weight = centred(streams_of[4], (D, KV_HEADS * HEAD_DIM), D ** -0.5, 0.1875, ((0, 8),))
    out_weight = centred(streams_of[5], (D, HEADS * HEAD_DIM), 16 ** -0.5, 1.5, ((0, 8),))
    gate_weight = centred(streams_of[6], (D, FF), D ** -0.5, 0.1875, ((0, 8),))
    up_weight = centred(streams_of[7], (D, FF), D ** -0.5, 0.1875, ((0, 8),))
    down_weight = centred(streams_of[8], (D, FF), FF ** -0.5, 0.09375, ((0, 8),))
    attn_norm = jnp.clip(1.0 + 0.1 * jax.random.normal(streams_of[9], (D,), jnp.float32), 0.5, 1.5)
    query_norm = jnp.clip(1.0 + 0.18 * jax.random.normal(streams_of[10], (HEAD_DIM,), jnp.float32), 0.1, 1.9)
    key_norm = jnp.clip(1.0 + 0.18 * jax.random.normal(streams_of[11], (HEAD_DIM,), jnp.float32), 0.1, 1.9)
    ffn_norm = jnp.clip(1.0 + 0.1 * jax.random.normal(streams_of[12], (D,), jnp.float32), 0.5, 1.5)
    out_grad = centred(streams_of[13], (SLOTS, SEQLEN, D), 1.0, 6.0, ((0, 4), (1, 8)))
    return {"tokens": tokens, "lengths": lengths, "query_weight": query_weight, "key_weight": key_weight, "value_weight": value_weight, "out_weight": out_weight, "gate_weight": gate_weight, "up_weight": up_weight, "down_weight": down_weight, "attn_norm": attn_norm, "query_norm": query_norm, "key_norm": key_norm, "ffn_norm": ffn_norm, "out_grad": out_grad}


EPSILON = 1e-05
THETA_BASE = 1000000.0
MASK_FILL = -1e+30
HIGHEST = lax.Precision.HIGHEST

@jax.custom_vjp
def low(v):
    return lax.optimization_barrier(v.astype(jnp.bfloat16)).astype(jnp.float32)

@jax.custom_vjp
def low_back(v):
    return v

def low_keep(v):
    return (low(v), None)

def low_pass(kept, grad):
    return (grad,)

def back_keep(v):
    return (v, None)

def back_low(kept, grad):
    return (low(grad),)
low.defvjp(low_keep, low_pass)
low_back.defvjp(back_keep, back_low)

def rms_norm(values, gain_vec):
    factor = lax.rsqrt(lax.optimization_barrier(jnp.mean(values * values, axis=-1, keepdims=True)) + EPSILON)
    return values * factor * gain_vec

def rotary_tables(position):
    exponent = jnp.arange(HEAD_DIM // 2, dtype=jnp.float32) * (2.0 / HEAD_DIM)
    inverse = THETA_BASE ** (-exponent)
    angles = position.astype(jnp.float32)[:, None] * inverse[None, :]
    cosine = jnp.concatenate([jnp.cos(angles), jnp.cos(angles)], axis=-1)
    sine_tab = jnp.concatenate([jnp.sin(angles), jnp.sin(angles)], axis=-1)
    return (cosine, sine_tab)

def rotate(values, cosine, sine_tab):
    half_dim = values.shape[-1] // 2
    turned = jnp.concatenate([-values[..., half_dim:], values[..., :half_dim]], axis=-1)
    return values * cosine[:, None, :] + turned * sine_tab[:, None, :]

def attend(queries, keys_all, values_all, length):
    seq_total = queries.shape[0]
    block_rows = min(512, seq_total)
    key_place = jnp.arange(seq_total, dtype=jnp.int32)

    def one_block(block_start):
        query_block = lax.dynamic_slice_in_dim(queries, block_start, block_rows, 0)
        scores = jnp.einsum('tgrd,ngd->grtn', query_block, keys_all, precision=HIGHEST) * HEAD_DIM ** (-0.5)
        scores = low_back(scores)
        query_place = block_start + jnp.arange(block_rows, dtype=jnp.int32)
        allowed = (key_place[None, :] <= query_place[:, None]) & (key_place[None, :] < length)
        masked = jnp.where(allowed, scores, MASK_FILL)
        top_score = lax.optimization_barrier(jnp.max(masked, axis=-1, keepdims=True))
        weights = jnp.where(allowed, jnp.exp(masked - top_score), 0.0)
        totals = lax.optimization_barrier(jnp.sum(weights, axis=-1))
        summed = jnp.einsum('grtn,ngd->tgrd', low(weights), values_all, precision=HIGHEST)
        return summed / jnp.transpose(totals, (2, 0, 1))[..., None]
    starts = jnp.arange(seq_total // block_rows, dtype=jnp.int32) * block_rows
    blocks = lax.map(jax.checkpoint(one_block), starts)
    return blocks.reshape(queries.shape)

def layer(params, tokens_slot, length):
    query_w, key_w, value_w, out_w, gate_w, up_w, down_w, attn_gain, query_gain, key_gain, ffn_gain = params
    seq_total = tokens_slot.shape[0]
    position = jnp.arange(seq_total, dtype=jnp.int32)
    cosine, sine_tab = rotary_tables(position)
    normed = low(rms_norm(tokens_slot, attn_gain))
    query_proj = low_back(jnp.dot(normed, query_w, precision=HIGHEST)).reshape(seq_total, HEADS, HEAD_DIM)
    key_proj = low_back(jnp.dot(normed, key_w, precision=HIGHEST)).reshape(seq_total, KV_HEADS, HEAD_DIM)
    value_proj = low(low_back(jnp.dot(normed, value_w, precision=HIGHEST))).reshape(seq_total, KV_HEADS, HEAD_DIM)
    queries = low(rotate(rms_norm(query_proj, query_gain), cosine, sine_tab))
    queries = queries.reshape(seq_total, KV_HEADS, HEADS // KV_HEADS, HEAD_DIM)
    keys_all = low(rotate(rms_norm(key_proj, key_gain), cosine, sine_tab))
    attended = attend(queries, keys_all, value_proj, length).reshape(seq_total, HEADS * HEAD_DIM)
    attended = low(low_back(attended))
    branch = low_back(jnp.dot(attended, out_w.T, precision=HIGHEST))
    residual = tokens_slot + branch
    normed_two = low(rms_norm(residual, ffn_gain))
    gate_val = low_back(jnp.dot(normed_two, gate_w, precision=HIGHEST))
    up_val = low_back(jnp.dot(normed_two, up_w, precision=HIGHEST))
    hidden = low(jax.nn.silu(gate_val) * up_val)
    result = residual + low_back(jnp.dot(hidden, down_w.T, precision=HIGHEST))
    return jnp.where((position < length)[:, None], result, 0.0)

def reference(tokens, lengths, query_weight, key_weight, value_weight, out_weight, gate_weight, up_weight, down_weight, attn_norm, query_norm, key_norm, ffn_norm, out_grad):
    params = tuple((item.astype(jnp.float32) for item in (query_weight, key_weight, value_weight, out_weight, gate_weight, up_weight, down_weight, attn_norm, query_norm, key_norm, ffn_norm)))
    outputs = []
    input_grads = []
    sums = tuple((jnp.zeros_like(item) for item in params))
    for slot_index in range(SLOTS):
        slot_length = lengths[slot_index]

        def run_slot(params_in, tokens_in):
            return layer(params_in, tokens_in, slot_length)
        result, pull = jax.vjp(run_slot, params, tokens[slot_index].astype(jnp.float32))
        param_grads, token_grad = pull(out_grad[slot_index].astype(jnp.float32))
        outputs.append(result)
        input_grads.append(token_grad)
        sums = tuple((total + piece_grad for total, piece_grad in zip(sums, param_grads)))
    return (jnp.stack(outputs).astype(jnp.bfloat16), jnp.stack(input_grads).astype(jnp.bfloat16), sums[0], sums[1], sums[2], sums[3], sums[4], sums[5], sums[6], sums[7], sums[8], sums[9], sums[10])
```

```python
import functools

import jax
import jax.numpy as jnp
from jax import lax
from jax.experimental import pallas as pl
from jax.experimental.pallas import tpu as pltpu
from jax.sharding import PartitionSpec as P

HEADS = 16
KV_HEADS = 8
HEAD_DIM = 64


EPSILON = 1e-05
THETA_BASE = 1000000.0
MASK_FILL = -1e30
HIGHEST = lax.Precision.HIGHEST


def rms_apply(values, gain_vec):
    factor = lax.rsqrt(jnp.mean(values * values, axis=-1, keepdims=True) + EPSILON)
    return (values * factor * gain_vec, factor)


def rms_back(values, factor, gain_vec, upstream):
    normal = values * factor
    weighted = upstream * gain_vec
    shared = jnp.mean(weighted * normal, axis=-1, keepdims=True)
    return (factor * (weighted - normal * shared), upstream * normal)


def rotary_tables(position):
    exponent = jnp.arange(HEAD_DIM // 2, dtype=jnp.float32) * (2.0 / HEAD_DIM)
    inverse = THETA_BASE ** (-exponent)
    angles = position.astype(jnp.float32)[:, None] * inverse[None, :]
    cosine = jnp.concatenate([jnp.cos(angles), jnp.cos(angles)], axis=-1)
    sine_tab = jnp.concatenate([jnp.sin(angles), jnp.sin(angles)], axis=-1)
    return (cosine, sine_tab)


def rotate(values, cosine, sine_tab):
    half_dim = values.shape[-1] // 2
    turned = jnp.concatenate([-values[..., half_dim:], values[..., :half_dim]], axis=-1)
    return values * cosine[:, None, :] + turned * sine_tab[:, None, :]


def rotate_back(upstream, cosine, sine_tab):
    half_dim = upstream.shape[-1] // 2
    scaled = upstream * sine_tab[:, None, :]
    turned = jnp.concatenate([scaled[..., half_dim:], -scaled[..., :half_dim]], axis=-1)
    return upstream * cosine[:, None, :] + turned


def contract_rows(left, right):
    return lax.dot_general(
        left, right, (((0,), (0,)), ((), ())), preferred_element_type=jnp.float32
    )


def contract_cols(left, right):
    return lax.dot_general(
        left, right, (((1,), (1,)), ((), ())), preferred_element_type=jnp.float32
    )


def general_body(
    tokens,
    lengths,
    query_weight,
    key_weight,
    value_weight,
    out_weight,
    gate_weight,
    up_weight,
    down_weight,
    attn_norm,
    query_norm,
    key_norm,
    ffn_norm,
    out_grad,
):
    tok_rows = tokens.shape[1]
    group_size = HEADS // KV_HEADS
    kv_width = KV_HEADS * HEAD_DIM
    score_scale = HEAD_DIM ** (-0.5)
    length = lengths[0]
    my_index = lax.axis_index("seq")
    position = my_index * tok_rows + jnp.arange(tok_rows, dtype=jnp.int32)
    row_valid = (position < length)[:, None]
    cosine, sine_tab = rotary_tables(position)
    inputs = tokens[0].astype(jnp.float32)
    query_full, key_full, value_full, out_full, gate_full, up_full, down_full = (
        lax.all_gather(query_weight, "seq", axis=0, tiled=True),
        lax.all_gather(key_weight, "seq", axis=0, tiled=True),
        lax.all_gather(value_weight, "seq", axis=0, tiled=True),
        lax.all_gather(out_weight, "seq", axis=0, tiled=True),
        lax.all_gather(gate_weight, "seq", axis=0, tiled=True),
        lax.all_gather(up_weight, "seq", axis=0, tiled=True),
        lax.all_gather(down_weight, "seq", axis=0, tiled=True),
    )
    normed_float, factor_one = rms_apply(inputs, attn_norm)
    normed = normed_float.astype(jnp.bfloat16)
    query_proj = jnp.dot(normed, query_full, preferred_element_type=jnp.float32).reshape(
        tok_rows, HEADS, HEAD_DIM
    )
    key_proj = jnp.dot(normed, key_full, preferred_element_type=jnp.float32).reshape(
        tok_rows, KV_HEADS, HEAD_DIM
    )
    value_low = jnp.dot(normed, value_full, preferred_element_type=jnp.float32).astype(jnp.bfloat16)
    query_unit, query_factor = rms_apply(query_proj, query_norm)
    key_unit, key_factor = rms_apply(key_proj, key_norm)
    query_low = (
        rotate(query_unit, cosine, sine_tab)
        .astype(jnp.bfloat16)
        .reshape(tok_rows, KV_HEADS, group_size, HEAD_DIM)
    )
    key_low = rotate(key_unit, cosine, sine_tab).astype(jnp.bfloat16).reshape(tok_rows, kv_width)

    def piece_scores(key_heads):
        key_count = key_heads.shape[0]
        scores = (
            jnp.einsum("tgrd,ngd->grtn", query_low, key_heads, preferred_element_type=jnp.float32)
            * score_scale
        )
        key_place = jnp.arange(key_count, dtype=jnp.int32)
        allowed = (key_place[None, :] <= position[:, None]) & (key_place[None, :] < length)
        return (scores, allowed)

    piece = (
        lax.all_gather(key_low, "seq", axis=0, tiled=True),
        lax.all_gather(value_low, "seq", axis=0, tiled=True),
    )
    forward_top_score = jnp.full((KV_HEADS, group_size, tok_rows), MASK_FILL, jnp.float32)
    key_heads = piece[0].reshape(-1, KV_HEADS, HEAD_DIM)
    value_heads = piece[1].reshape(-1, KV_HEADS, HEAD_DIM)
    scores, allowed = piece_scores(key_heads)
    masked = jnp.where(allowed, scores, MASK_FILL)
    new_top = jnp.maximum(forward_top_score, jnp.max(masked, axis=-1))
    weights = jnp.where(allowed, jnp.exp(masked - new_top[..., None]), 0.0)
    forward_weight_sum = jnp.sum(weights, axis=-1)
    added = jnp.einsum(
        "grtn,ngd->tgrd",
        weights.astype(jnp.bfloat16),
        value_heads,
        preferred_element_type=jnp.float32,
    )
    accum = added
    top_score, weight_sum, accum = (new_top, forward_weight_sum, accum)
    attn_heads = accum / jnp.transpose(weight_sum, (2, 0, 1))[..., None]
    attn_low = attn_heads.reshape(tok_rows, HEADS * HEAD_DIM).astype(jnp.bfloat16)
    residual = inputs + contract_cols(attn_low, out_full)
    normed_two_float, factor_two = rms_apply(residual, ffn_norm)
    normed_two = normed_two_float.astype(jnp.bfloat16)
    gate_val = jnp.dot(normed_two, gate_full, preferred_element_type=jnp.float32)
    up_val = jnp.dot(normed_two, up_full, preferred_element_type=jnp.float32)
    sigmoid_gate = jax.nn.sigmoid(gate_val)
    silu_gate = gate_val * sigmoid_gate
    hidden = (silu_gate * up_val).astype(jnp.bfloat16)
    result = residual + contract_cols(hidden, down_full)
    mixed = jnp.where(row_valid, result, 0.0).astype(jnp.bfloat16)[None]
    query_full, key_full, value_full, out_full, gate_full, up_full, down_full = (
        lax.all_gather(query_weight, "seq", axis=0, tiled=True),
        lax.all_gather(key_weight, "seq", axis=0, tiled=True),
        lax.all_gather(value_weight, "seq", axis=0, tiled=True),
        lax.all_gather(out_weight, "seq", axis=0, tiled=True),
        lax.all_gather(gate_weight, "seq", axis=0, tiled=True),
        lax.all_gather(up_weight, "seq", axis=0, tiled=True),
        lax.all_gather(down_weight, "seq", axis=0, tiled=True),
    )
    upstream = jnp.where(row_valid, out_grad[0].astype(jnp.float32), 0.0)
    branch_grad = upstream.astype(jnp.bfloat16)
    hidden_grad = jnp.dot(branch_grad, down_full, preferred_element_type=jnp.float32)
    down_w_grad = contract_rows(branch_grad, hidden)
    gate_grad_low = (
        hidden_grad * up_val * sigmoid_gate * (1.0 + gate_val * (1.0 - sigmoid_gate))
    ).astype(jnp.bfloat16)
    up_grad_low = (hidden_grad * silu_gate).astype(jnp.bfloat16)
    normed_two_grad = contract_cols(gate_grad_low, gate_full) + contract_cols(up_grad_low, up_full)
    gate_w_grad = contract_rows(normed_two, gate_grad_low)
    up_w_grad = contract_rows(normed_two, up_grad_low)
    residual_part, ffn_terms = rms_back(residual, factor_two, ffn_norm, normed_two_grad)
    residual_grad = upstream + residual_part
    attn_out_low = residual_grad.astype(jnp.bfloat16)
    out_w_grad = contract_rows(attn_out_low, attn_low)
    attn_grad_low = jnp.dot(attn_out_low, out_full, preferred_element_type=jnp.float32).astype(
        jnp.bfloat16
    )
    attn_grad_heads = attn_grad_low.reshape(tok_rows, KV_HEADS, group_size, HEAD_DIM)
    row_inner = jnp.transpose(
        jnp.sum(attn_grad_heads.astype(jnp.float32) * attn_heads, axis=-1), (1, 2, 0)
    )
    scaled_grad = (
        attn_grad_heads.astype(jnp.float32) / jnp.transpose(weight_sum, (2, 0, 1))[..., None]
    )
    piece = (
        lax.all_gather(key_low, "seq", axis=0, tiled=True),
        lax.all_gather(value_low, "seq", axis=0, tiled=True),
    )
    key_heads = piece[0].reshape(-1, KV_HEADS, HEAD_DIM)
    value_heads = piece[1].reshape(-1, KV_HEADS, HEAD_DIM)
    key_count = key_heads.shape[0]
    scores, allowed = piece_scores(key_heads)
    shifted = jnp.where(allowed, scores - top_score[..., None], MASK_FILL)
    exp_vals = jnp.where(allowed, jnp.exp(shifted), 0.0)
    probs = exp_vals / weight_sum[..., None]
    prob_grad = jnp.einsum(
        "tgrd,ngd->grtn", attn_grad_heads, value_heads, preferred_element_type=jnp.float32
    )
    score_grad = (probs * (prob_grad - row_inner[..., None])).astype(jnp.bfloat16)
    backward_query_acc = (
        jnp.einsum("grtn,ngd->tgrd", score_grad, key_heads, preferred_element_type=jnp.float32)
        * score_scale
    )
    key_part = (
        jnp.einsum("grtn,tgrd->ngd", score_grad, query_low, preferred_element_type=jnp.float32)
        * score_scale
    )
    exp_low = exp_vals.astype(jnp.bfloat16).astype(jnp.float32)
    value_part = jnp.einsum(
        "grtn,tgrd->ngd",
        exp_low,
        scaled_grad,
        precision=HIGHEST,
        preferred_element_type=jnp.float32,
    )
    update = jnp.concatenate(
        [key_part.reshape(key_count, kv_width), value_part.reshape(key_count, kv_width)], axis=1
    )
    query_acc, update = (backward_query_acc, update)
    key_buffer = update
    query_acc, key_buffer = (query_acc, key_buffer)
    key_value_grad = lax.psum_scatter(key_buffer, "seq", scatter_dimension=0, tiled=True)
    key_rot_grad = key_value_grad[:, :kv_width].reshape(tok_rows, KV_HEADS, HEAD_DIM)
    value_grad_low = key_value_grad[:, kv_width:].astype(jnp.bfloat16)
    query_rot_grad = query_acc.reshape(tok_rows, HEADS, HEAD_DIM)
    query_proj_grad, query_terms = rms_back(
        query_proj, query_factor, query_norm, rotate_back(query_rot_grad, cosine, sine_tab)
    )
    key_proj_grad, key_terms = rms_back(
        key_proj, key_factor, key_norm, rotate_back(key_rot_grad, cosine, sine_tab)
    )
    query_grad_low = query_proj_grad.reshape(tok_rows, HEADS * HEAD_DIM).astype(jnp.bfloat16)
    key_grad_low = key_proj_grad.reshape(tok_rows, kv_width).astype(jnp.bfloat16)
    normed_grad = (
        contract_cols(query_grad_low, query_full)
        + contract_cols(key_grad_low, key_full)
        + contract_cols(value_grad_low, value_full)
    )
    query_w_grad = contract_rows(normed, query_grad_low)
    key_w_grad = contract_rows(normed, key_grad_low)
    value_w_grad = contract_rows(normed, value_grad_low)
    input_part, attn_terms = rms_back(inputs, factor_one, attn_norm, normed_grad)
    input_grad = (residual_grad + input_part).astype(jnp.bfloat16)[None]
    attn_gain_grad, query_gain_grad, key_gain_grad, ffn_gain_grad = lax.psum(
        (
            jnp.sum(attn_terms, axis=0),
            jnp.sum(query_terms, axis=(0, 1)),
            jnp.sum(key_terms, axis=(0, 1)),
            jnp.sum(ffn_terms, axis=0),
        ),
        ("seq", "slot"),
    )
    query_share, key_share, value_share, out_share, gate_share, up_share, down_share = (
        lax.psum_scatter(query_w_grad, "seq", scatter_dimension=0, tiled=True),
        lax.psum_scatter(key_w_grad, "seq", scatter_dimension=0, tiled=True),
        lax.psum_scatter(value_w_grad, "seq", scatter_dimension=0, tiled=True),
        lax.psum_scatter(out_w_grad, "seq", scatter_dimension=0, tiled=True),
        lax.psum_scatter(gate_w_grad, "seq", scatter_dimension=0, tiled=True),
        lax.psum_scatter(up_w_grad, "seq", scatter_dimension=0, tiled=True),
        lax.psum_scatter(down_w_grad, "seq", scatter_dimension=0, tiled=True),
    )
    query_share, key_share, value_share, out_share, gate_share, up_share, down_share = (
        lax.psum(query_share.astype(jnp.bfloat16), "slot").astype(jnp.float32),
        lax.psum(key_share.astype(jnp.bfloat16), "slot").astype(jnp.float32),
        lax.psum(value_share.astype(jnp.bfloat16), "slot").astype(jnp.float32),
        lax.psum(out_share.astype(jnp.bfloat16), "slot").astype(jnp.float32),
        lax.psum(gate_share.astype(jnp.bfloat16), "slot").astype(jnp.float32),
        lax.psum(up_share.astype(jnp.bfloat16), "slot").astype(jnp.float32),
        lax.psum(down_share.astype(jnp.bfloat16), "slot").astype(jnp.float32),
    )
    return (
        mixed,
        input_grad,
        query_share,
        key_share,
        value_share,
        out_share,
        gate_share,
        up_share,
        down_share,
        attn_gain_grad,
        query_gain_grad,
        key_gain_grad,
        ffn_gain_grad,
    )


SLOTS_BY_HEADS = 4
LANES = 2 * HEAD_DIM
VMEM_LIMIT = 60 * 1024 * 1024


def dot_nn(left, right):
    return lax.dot_general(left, right, (((1,), (0,)), ((), ())), preferred_element_type=jnp.float32)


def dot_nt(left, right):
    return lax.dot_general(left, right, (((1,), (1,)), ((), ())), preferred_element_type=jnp.float32)


def dot_tn(left, right):
    return lax.dot_general(left, right, (((0,), (0,)), ((), ())), preferred_element_type=jnp.float32)


def lane_is_low(shape):
    return lax.broadcasted_iota(jnp.int32, shape, len(shape) - 1) < HEAD_DIM


def pair_mean(values):
    low = lane_is_low(values.shape)
    first = jnp.sum(jnp.where(low, values, 0.0), axis=-1, keepdims=True)
    second = jnp.sum(jnp.where(low, 0.0, values), axis=-1, keepdims=True)
    return jnp.where(low, first, second) * (1.0 / HEAD_DIM)


def pair_turn(values, cosine, sine_signed):
    lane = lax.broadcasted_iota(jnp.int32, values.shape, 1)
    near = lax.rem(lane, HEAD_DIM) < HEAD_DIM // 2
    half = HEAD_DIM // 2
    turned = jnp.where(near, pltpu.roll(values, LANES - half, 1), pltpu.roll(values, half, 1))
    return values * cosine + turned * sine_signed


def call(kernel, out_shape, scratch_shapes=(), flops=0, moved=0):
    vmem = pl.BlockSpec(memory_space=pltpu.VMEM)

    def apply(*operands, smem=0):
        in_specs = [pl.BlockSpec(memory_space=pltpu.SMEM)] * smem + [vmem] * (len(operands) - smem)
        return pl.pallas_call(
            kernel,
            out_shape=out_shape,
            in_specs=in_specs,
            out_specs=jax.tree.map(lambda _: vmem, out_shape),
            scratch_shapes=scratch_shapes,
            compiler_params=pltpu.CompilerParams(vmem_limit_bytes=VMEM_LIMIT),
            cost_estimate=pl.CostEstimate(flops=flops, bytes_accessed=moved, transcendentals=0),
        )(*operands)

    return apply


ROW_BLOCK = 256


def attention_forward_kernel(
    length_ref, x_ref, weight_ref, gain_ref, q_gain_ref, k_gain_ref, cos_q_ref, sin_q_ref, cos_k_ref, sin_k_ref,
    normed_ref, q_proj_ref, kv_proj_ref, q_low_ref, k_pair_ref, v_pair_ref, attn_ref, attn_low_ref, weight_inv_ref,
):
    total = x_ref.shape[0]
    length = length_ref[0]
    low = lane_is_low((ROW_BLOCK, LANES))
    for start in range(0, total, ROW_BLOCK):
        rows = pl.ds(start, ROW_BLOCK)
        x = x_ref[rows, :].astype(jnp.float32)
        factor = lax.rsqrt(jnp.mean(x * x, axis=-1, keepdims=True) + EPSILON)
        normed = (x * factor * gain_ref[...]).astype(jnp.bfloat16)
        normed_ref[rows, :] = normed
        proj = dot_nn(normed, weight_ref[...])
        q_proj = proj[:, :LANES]
        kv_proj = proj[:, LANES:]
        q_proj_ref[rows, :] = q_proj
        kv_proj_ref[rows, :] = kv_proj
        q_factor = lax.rsqrt(pair_mean(q_proj * q_proj) + EPSILON)
        q_low_ref[rows, :] = pair_turn(
            q_proj * q_factor * q_gain_ref[...], cos_q_ref[rows, :], sin_q_ref[rows, :]
        ).astype(jnp.bfloat16)
        k_factor = jnp.where(low, lax.rsqrt(pair_mean(kv_proj * kv_proj) + EPSILON), 1.0)
        kv = pair_turn(kv_proj * k_factor * k_gain_ref[...], cos_k_ref[rows, :], sin_k_ref[rows, :])
        swapped = pltpu.roll(kv, HEAD_DIM, 1)
        k_pair_ref[rows, :] = jnp.where(low, kv, swapped).astype(jnp.bfloat16)
        v_pair_ref[rows, :] = jnp.where(low, swapped, kv).astype(jnp.bfloat16)

    scale = HEAD_DIM ** (-0.5)
    for start in range(0, total, ROW_BLOCK):
        rows = pl.ds(start, ROW_BLOCK)
        q = q_low_ref[rows, :]
        zero = jnp.zeros_like(q)
        heads = (jnp.where(low, q, zero), jnp.where(low, zero, q))
        results = []
        for q_head in heads:
            weight_sum = jnp.zeros((ROW_BLOCK, 1), jnp.float32)
            summed = jnp.zeros((ROW_BLOCK, LANES), jnp.float32)
            if start > 0:
                past = pl.ds(0, start)
                exp_vals = jnp.exp(dot_nt(q_head, k_pair_ref[past, :]) * scale)
                weight_sum += jnp.sum(exp_vals, axis=-1, keepdims=True)
                summed += dot_nn(exp_vals.astype(jnp.bfloat16), v_pair_ref[past, :])
            scores = dot_nt(q_head, k_pair_ref[rows, :]) * scale
            query = lax.broadcasted_iota(jnp.int32, scores.shape, 0)
            key = lax.broadcasted_iota(jnp.int32, scores.shape, 1)
            allowed = (key <= query) & (key + start < length)
            exp_vals = jnp.where(allowed, jnp.exp(scores), 0.0)
            weight_sum += jnp.sum(exp_vals, axis=-1, keepdims=True)
            summed += dot_nn(exp_vals.astype(jnp.bfloat16), v_pair_ref[rows, :])
            inverse = 1.0 / weight_sum
            results.append((summed * inverse, inverse))
        attn = jnp.where(low, results[0][0], results[1][0])
        attn_ref[rows, :] = attn
        attn_low_ref[rows, :] = attn.astype(jnp.bfloat16)
        weight_inv_ref[rows, :] = jnp.where(low, results[0][1], results[1][1])


def attention_backward_kernel(
    length_ref, dattn_ref, normed_ref, weight_ref, q_gain_ref, k_gain_ref, cos_q_ref, sin_q_ref, cos_k_ref, sin_k_ref,
    q_proj_ref, kv_proj_ref, q_low_ref, k_pair_ref, v_pair_ref, attn_ref, weight_inv_ref,
    dnormed_ref, dproj_ref, terms_ref, dq_acc, dk_acc, dv_acc,
):
    total = dattn_ref.shape[0]
    length = length_ref[0]
    low = lane_is_low((ROW_BLOCK, LANES))
    scale = HEAD_DIM ** (-0.5)
    dk_acc[...] = jnp.zeros_like(dk_acc)
    dv_acc[...] = jnp.zeros_like(dv_acc)
    for start in range(0, total, ROW_BLOCK):
        rows = pl.ds(start, ROW_BLOCK)
        q = q_low_ref[rows, :]
        dattn = dattn_ref[rows, :]
        zero = jnp.zeros_like(q)
        inner = dattn.astype(jnp.float32) * attn_ref[rows, :]
        inverses = weight_inv_ref[rows, :]
        dq_heads = []
        for head in range(2):
            mine = low if head == 0 else jnp.logical_not(low)
            q_head = jnp.where(mine, q, zero)
            dattn_head = jnp.where(mine, dattn, zero)
            delta = jnp.sum(jnp.where(mine, inner, 0.0), axis=-1, keepdims=True)
            inverse = inverses[:, head * HEAD_DIM : head * HEAD_DIM + 1]
            dq = jnp.zeros((ROW_BLOCK, LANES), jnp.float32)
            spans = ([(0, start)] if start > 0 else []) + [(start, ROW_BLOCK)]
            for key_start, key_count in spans:
                keys = pl.ds(key_start, key_count)
                k_pair = k_pair_ref[keys, :]
                probs = jnp.exp(dot_nt(q_head, k_pair) * scale) * inverse
                if key_start == start:
                    query = lax.broadcasted_iota(jnp.int32, probs.shape, 0)
                    key = lax.broadcasted_iota(jnp.int32, probs.shape, 1)
                    allowed = (key <= query) & (key + start < length)
                    probs = jnp.where(allowed, probs, 0.0)
                dprobs = dot_nt(dattn_head, v_pair_ref[keys, :])
                dscores = (probs * (dprobs - delta)).astype(jnp.bfloat16)
                dq += dot_nn(dscores, k_pair)
                dk_acc[keys, :] += dot_tn(dscores, q_head)
                dv_acc[keys, :] += dot_tn(probs.astype(jnp.bfloat16), dattn_head)
            dq_heads.append(dq)
        dq_acc[rows, :] = jnp.where(low, dq_heads[0], dq_heads[1]) * scale

    q_terms = jnp.zeros((1, LANES), jnp.float32)
    k_terms = jnp.zeros((1, LANES), jnp.float32)
    for start in range(0, total, ROW_BLOCK):
        rows = pl.ds(start, ROW_BLOCK)
        q_proj = q_proj_ref[rows, :]
        upstream = pair_turn(dq_acc[rows, :], cos_q_ref[rows, :], -sin_q_ref[rows, :])
        factor = lax.rsqrt(pair_mean(q_proj * q_proj) + EPSILON)
        normal = q_proj * factor
        weighted = upstream * q_gain_ref[...]
        dq_proj = factor * (weighted - normal * pair_mean(weighted * normal))
        q_terms += jnp.sum(upstream * normal, axis=0, keepdims=True)

        dk = dk_acc[rows, :] * scale
        dv = dv_acc[rows, :]
        dk = dk + pltpu.roll(dk, HEAD_DIM, 1)
        dv = dv + pltpu.roll(dv, HEAD_DIM, 1)
        kv_proj = kv_proj_ref[rows, :]
        upstream = pair_turn(jnp.where(low, dk, 0.0), cos_k_ref[rows, :], -sin_k_ref[rows, :])
        factor = lax.rsqrt(pair_mean(kv_proj * kv_proj) + EPSILON)
        normal = kv_proj * factor
        weighted = upstream * k_gain_ref[...]
        dk_proj = factor * (weighted - normal * pair_mean(weighted * normal))
        k_terms += jnp.sum(upstream * normal, axis=0, keepdims=True)
        dkv_proj = jnp.where(low, dk_proj, dv)
        dproj = jnp.concatenate([dq_proj, dkv_proj], axis=1).astype(jnp.bfloat16)
        dproj_ref[rows, :] = dproj
        dnormed_ref[rows, :] = dot_nt(dproj, weight_ref[...]).astype(jnp.bfloat16)
    terms_ref[0:1, :] = q_terms
    terms_ref[1:2, :] = k_terms


def feed_forward_kernel(
    x_ref, attn_ref, out_weight_ref, gain_ref, gate_up_ref, down_ref, dout_ref,
    residual_ref, normed_ref, hidden_ref, dgate_up_ref, dnormed_ref, mixed_ref,
):
    low = lane_is_low((x_ref.shape[0], LANES))
    attn = jnp.concatenate([attn_ref[i] for i in range(attn_ref.shape[0])], axis=1)
    residual = x_ref[...].astype(jnp.float32) + dot_nt(attn, out_weight_ref[...])
    residual_ref[...] = residual
    factor = lax.rsqrt(jnp.mean(residual * residual, axis=-1, keepdims=True) + EPSILON)
    normed = (residual * factor * gain_ref[...]).astype(jnp.bfloat16)
    normed_ref[...] = normed
    both = dot_nn(normed, gate_up_ref[...])
    dhidden = dot_nn(dout_ref[...], down_ref[...])
    whole = (both.shape[1] - LANES) // 2
    tail = both[:, 2 * whole :]
    tail_swapped = pltpu.roll(tail, HEAD_DIM, 1)

    def share(gate, up, upstream):
        sigmoid = jax.nn.sigmoid(gate)
        silu = gate * sigmoid
        dgate = upstream * up * sigmoid * (1.0 + gate * (1.0 - sigmoid))
        return silu * up, dgate, upstream * silu

    hidden, dgate, dup = share(both[:, :whole], both[:, whole : 2 * whole], dhidden[:, :whole])
    hidden_tail, dgate_tail, dup_tail = share(
        jnp.where(low, tail, tail_swapped), jnp.where(low, tail_swapped, tail), dhidden[:, whole:]
    )
    hidden_low = jnp.concatenate([hidden, jnp.where(low, hidden_tail, 0.0)], axis=1).astype(jnp.bfloat16)
    dgate_up = jnp.concatenate([dgate, dup, jnp.where(low, dgate_tail, dup_tail)], axis=1).astype(jnp.bfloat16)
    hidden_ref[...] = hidden_low
    dgate_up_ref[...] = dgate_up
    dnormed_ref[...] = dot_nt(dgate_up, gate_up_ref[...]).astype(jnp.bfloat16)
    mixed_ref[...] = dot_nt(hidden_low, down_ref[...]).astype(jnp.bfloat16)


def rotary_pair_tables(total):
    position = jnp.arange(total, dtype=jnp.int32)
    cosine, sine = rotary_tables(position)
    half = HEAD_DIM // 2
    signed = jnp.concatenate([-sine[:, :half], sine[:, half:]], axis=1)
    return (
        jnp.concatenate([cosine, cosine], axis=1),
        jnp.concatenate([signed, signed], axis=1),
        jnp.concatenate([cosine, jnp.ones_like(cosine)], axis=1),
        jnp.concatenate([signed, jnp.zeros_like(signed)], axis=1),
    )


def heads_body(
    tokens, lengths, query_weight, key_weight, value_weight, out_weight, gate_weight, up_weight, down_weight,
    attn_norm, query_norm, key_norm, ffn_norm, out_grad,
):
    count = KV_HEADS
    tok_rows, width = tokens.shape[1:]
    depth = query_weight.shape[0]
    total = tok_rows * count
    hidden_width = gate_weight.shape[1]
    whole = hidden_width // count // LANES * LANES
    rest = hidden_width // count - whole
    length = lengths[0]
    me = lax.axis_index("seq")
    position = me * tok_rows + jnp.arange(tok_rows, dtype=jnp.int32)
    row_valid = (position < length)[:, None]

    def gather(block):
        return lax.all_gather(block, "seq", axis=0, tiled=True)

    def swap(blocks):
        return lax.all_to_all(blocks, "seq", 0, 0, tiled=True)

    def by_owner(weight):
        return jnp.transpose(weight.reshape(depth, count, -1), (1, 0, 2))

    def sum_swapped(partial):
        return jnp.sum(swap(partial.reshape(count, tok_rows, width)).astype(jnp.float32), axis=0)

    x_all = gather(tokens[0])
    attn_weight = swap(
        jnp.concatenate([by_owner(query_weight), by_owner(key_weight), by_owner(value_weight)], axis=2)
    ).reshape(width, 2 * LANES)
    cut = whole * count
    ffn_weight = swap(
        jnp.concatenate(
            [
                by_owner(gate_weight[:, :cut]),
                by_owner(up_weight[:, :cut]),
                by_owner(gate_weight[:, cut:]),
                by_owner(up_weight[:, cut:]),
                by_owner(down_weight[:, :cut]),
                by_owner(down_weight[:, cut:]),
            ],
            axis=2,
        )
    ).reshape(width, -1)
    gate_up = ffn_weight[:, : 2 * whole + 2 * rest]
    down = jnp.concatenate([ffn_weight[:, 2 * whole + 2 * rest :], ffn_weight[:, -rest:]], axis=1)
    out_full = gather(out_weight)
    upstream = jnp.where(row_valid, out_grad[0].astype(jnp.float32), 0.0)
    dout_all = gather(upstream.astype(jnp.bfloat16))
    tables = rotary_pair_tables(total)
    q_gain = jnp.concatenate([query_norm, query_norm])[None]
    k_gain = jnp.concatenate([key_norm, jnp.ones_like(key_norm)])[None]

    def array(kind, *shape):
        return jax.ShapeDtypeStruct(shape, kind)

    f32, bf16 = jnp.float32, jnp.bfloat16
    normed, q_proj, kv_proj, q_low, k_pair, v_pair, attn, attn_low, weight_inv = call(
        attention_forward_kernel,
        (
            array(bf16, total, width), array(f32, total, LANES), array(f32, total, LANES), array(bf16, total, LANES),
            array(bf16, total, LANES), array(bf16, total, LANES), array(f32, total, LANES), array(bf16, total, LANES),
            array(f32, total, LANES),
        ),
        flops=2_000_000_000,
        moved=8_000_000,
    )(lengths, x_all, attn_weight, attn_norm[None], q_gain, k_gain, *tables, smem=1)

    attn_all = lax.all_gather(attn_low, "seq", axis=0)

    blocks = total // ROW_BLOCK
    units = whole + rest
    row_spec = lambda size: pl.BlockSpec((ROW_BLOCK, size), lambda i: (i, 0))
    full_spec = lambda *shape: pl.BlockSpec(shape, lambda i: (0,) * len(shape))
    residual, normed_two, hidden, dgate_up, dnormed_two, mixed_part = pl.pallas_call(
        feed_forward_kernel,
        grid=(blocks,),
        out_shape=(
            array(f32, total, width), array(bf16, total, width), array(bf16, total, whole + LANES),
            array(bf16, total, 2 * units), array(bf16, total, width), array(bf16, total, width),
        ),
        in_specs=[
            row_spec(width),
            pl.BlockSpec((count, ROW_BLOCK, LANES), lambda i: (0, i, 0)),
            full_spec(width, width),
            full_spec(1, width),
            full_spec(width, 2 * units),
            full_spec(width, whole + LANES),
            row_spec(width),
        ],
        out_specs=(
            row_spec(width), row_spec(width), row_spec(whole + LANES), row_spec(2 * units), row_spec(width),
            row_spec(width),
        ),
        compiler_params=pltpu.CompilerParams(vmem_limit_bytes=VMEM_LIMIT),
        cost_estimate=pl.CostEstimate(flops=9_000_000_000, bytes_accessed=25_000_000, transcendentals=0),
    )(x_all, attn_all, out_full, ffn_norm[None], gate_up, down, dout_all)

    my_rows = me * tok_rows
    residual_mine = lax.dynamic_slice_in_dim(residual, my_rows, tok_rows, 0)
    normed_two_grad = sum_swapped(dnormed_two)
    factor_two = lax.rsqrt(jnp.mean(residual_mine * residual_mine, axis=-1, keepdims=True) + EPSILON)
    residual_part, ffn_terms = rms_back(residual_mine, factor_two, ffn_norm, normed_two_grad)
    residual_grad = upstream + residual_part
    attn_out_low = residual_grad.astype(bf16)
    dattn = jnp.dot(attn_out_low, out_full, preferred_element_type=f32).astype(bf16)
    dattn = swap(jnp.transpose(dattn.reshape(tok_rows, count, LANES), (1, 0, 2))).reshape(total, LANES)
    attn_out_all = gather(attn_out_low)

    result = residual_mine + sum_swapped(mixed_part)
    mixed = jnp.where(row_valid, result, 0.0).astype(bf16)[None]

    dnormed, dproj, terms = call(
        attention_backward_kernel,
        (array(bf16, total, width), array(bf16, total, 2 * LANES), array(f32, 2, LANES)),
        scratch_shapes=[pltpu.VMEM((total, LANES), f32)] * 3,
        flops=3_000_000_000,
        moved=10_000_000,
    )(
        lengths, dattn, normed, attn_weight, q_gain, k_gain, *tables, q_proj, kv_proj, q_low, k_pair, v_pair, attn,
        weight_inv, smem=1,
    )
    inputs = tokens[0].astype(f32)
    factor_one = lax.rsqrt(jnp.mean(inputs * inputs, axis=-1, keepdims=True) + EPSILON)
    input_part, attn_terms = rms_back(inputs, factor_one, attn_norm, sum_swapped(dnormed))
    input_grad = (residual_grad + input_part).astype(bf16)[None]

    gate_up_grad = dot_tn(normed_two, dgate_up).astype(bf16)
    down_grad = dot_tn(dout_all, hidden).astype(bf16)[:, :units]
    out_grad_cols = dot_tn(attn_out_all, attn_low).astype(bf16)
    proj_grad = dot_tn(normed, dproj).astype(bf16)

    def to_rows(grad):
        swapped = swap(grad.reshape(count, depth, -1))
        return lax.psum(swapped, "slot").astype(f32)

    def spread(part):
        return jnp.transpose(part, (1, 0, 2)).reshape(depth, -1)

    gate_up_rows = to_rows(gate_up_grad)
    down_rows = to_rows(down_grad)
    attn_rows = to_rows(jnp.concatenate([proj_grad, out_grad_cols], axis=1))
    gate_rows = jnp.concatenate(
        [spread(gate_up_rows[..., :whole]), spread(gate_up_rows[..., 2 * whole : 2 * whole + rest])], axis=1
    )
    up_rows = jnp.concatenate(
        [spread(gate_up_rows[..., whole : 2 * whole]), spread(gate_up_rows[..., 2 * whole + rest :])], axis=1
    )
    down_rows = jnp.concatenate([spread(down_rows[..., :whole]), spread(down_rows[..., whole:])], axis=1)
    half = HEAD_DIM
    query_rows = spread(attn_rows[..., :LANES])
    key_rows = spread(attn_rows[..., LANES : LANES + half])
    value_rows = spread(attn_rows[..., LANES + half : 2 * LANES])
    out_rows = spread(attn_rows[..., 2 * LANES :])

    attn_gain, query_gain, key_gain, ffn_gain = lax.psum(
        (
            jnp.sum(attn_terms, axis=0),
            terms[0, :half] + terms[0, half:],
            terms[1, :half],
            jnp.sum(ffn_terms, axis=0),
        ),
        ("seq", "slot"),
    )
    return (
        mixed, input_grad, query_rows, key_rows, value_rows, out_rows, gate_rows, up_rows, down_rows,
        attn_gain, query_gain, key_gain, ffn_gain,
    )


def solution(mesh):
    in_specs = (
        P("slot", "seq", None),
        P("slot"),
        P("seq", None),
        P("seq", None),
        P("seq", None),
        P("seq", None),
        P("seq", None),
        P("seq", None),
        P("seq", None),
        P(),
        P(),
        P(),
        P(),
        P("slot", "seq", None),
    )
    out_specs = (
        P("slot", "seq", None),
        P("slot", "seq", None),
        P("seq", None),
        P("seq", None),
        P("seq", None),
        P("seq", None),
        P("seq", None),
        P("seq", None),
        P("seq", None),
        P(),
        P(),
        P(),
        P(),
    )
    by_heads = mesh.shape["seq"] == KV_HEADS and mesh.shape["slot"] == SLOTS_BY_HEADS
    body = heads_body if by_heads else general_body
    return jax.shard_map(body, mesh=mesh, in_specs=in_specs, out_specs=out_specs, check_vma=False)
```

```python
import functools

import jax
import jax.numpy as jnp
import numpy as np
from jax import lax
from jax.experimental import pallas as pl
from jax.experimental.pallas import tpu as pltpu
from jax.sharding import PartitionSpec as P

HEADS = 16
KV_HEADS = 8
HEAD_DIM = 64


EPSILON = 1e-05
THETA_BASE = 1000000.0
MASK_FILL = -1e30
HIGHEST = lax.Precision.HIGHEST


def rms_apply(values, gain_vec):
    factor = lax.rsqrt(jnp.mean(values * values, axis=-1, keepdims=True) + EPSILON)
    return (values * factor * gain_vec, factor)


def rms_back(values, factor, gain_vec, upstream):
    normal = values * factor
    weighted = upstream * gain_vec
    shared = jnp.mean(weighted * normal, axis=-1, keepdims=True)
    return (factor * (weighted - normal * shared), upstream * normal)


def rotary_tables(position):
    exponent = jnp.arange(HEAD_DIM // 2, dtype=jnp.float32) * (2.0 / HEAD_DIM)
    inverse = THETA_BASE ** (-exponent)
    angles = position.astype(jnp.float32)[:, None] * inverse[None, :]
    cosine = jnp.concatenate([jnp.cos(angles), jnp.cos(angles)], axis=-1)
    sine_tab = jnp.concatenate([jnp.sin(angles), jnp.sin(angles)], axis=-1)
    return (cosine, sine_tab)


def rotate(values, cosine, sine_tab):
    half_dim = values.shape[-1] // 2
    turned = jnp.concatenate([-values[..., half_dim:], values[..., :half_dim]], axis=-1)
    return values * cosine[:, None, :] + turned * sine_tab[:, None, :]


def rotate_back(upstream, cosine, sine_tab):
    half_dim = upstream.shape[-1] // 2
    scaled = upstream * sine_tab[:, None, :]
    turned = jnp.concatenate([scaled[..., half_dim:], -scaled[..., :half_dim]], axis=-1)
    return upstream * cosine[:, None, :] + turned


def contract_rows(left, right):
    return lax.dot_general(
        left, right, (((0,), (0,)), ((), ())), preferred_element_type=jnp.float32
    )


def contract_cols(left, right):
    return lax.dot_general(
        left, right, (((1,), (1,)), ((), ())), preferred_element_type=jnp.float32
    )


def general_body(
    tokens,
    lengths,
    query_weight,
    key_weight,
    value_weight,
    out_weight,
    gate_weight,
    up_weight,
    down_weight,
    attn_norm,
    query_norm,
    key_norm,
    ffn_norm,
    out_grad,
):
    tok_rows = tokens.shape[1]
    group_size = HEADS // KV_HEADS
    kv_width = KV_HEADS * HEAD_DIM
    score_scale = HEAD_DIM ** (-0.5)
    length = lengths[0]
    my_index = lax.axis_index("seq")
    position = my_index * tok_rows + jnp.arange(tok_rows, dtype=jnp.int32)
    row_valid = (position < length)[:, None]
    cosine, sine_tab = rotary_tables(position)
    inputs = tokens[0].astype(jnp.float32)
    query_full, key_full, value_full, out_full, gate_full, up_full, down_full = (
        lax.all_gather(query_weight, "seq", axis=0, tiled=True),
        lax.all_gather(key_weight, "seq", axis=0, tiled=True),
        lax.all_gather(value_weight, "seq", axis=0, tiled=True),
        lax.all_gather(out_weight, "seq", axis=0, tiled=True),
        lax.all_gather(gate_weight, "seq", axis=0, tiled=True),
        lax.all_gather(up_weight, "seq", axis=0, tiled=True),
        lax.all_gather(down_weight, "seq", axis=0, tiled=True),
    )
    normed_float, factor_one = rms_apply(inputs, attn_norm)
    normed = normed_float.astype(jnp.bfloat16)
    query_proj = jnp.dot(normed, query_full, preferred_element_type=jnp.float32).reshape(
        tok_rows, HEADS, HEAD_DIM
    )
    key_proj = jnp.dot(normed, key_full, preferred_element_type=jnp.float32).reshape(
        tok_rows, KV_HEADS, HEAD_DIM
    )
    value_low = jnp.dot(normed, value_full, preferred_element_type=jnp.float32).astype(jnp.bfloat16)
    query_unit, query_factor = rms_apply(query_proj, query_norm)
    key_unit, key_factor = rms_apply(key_proj, key_norm)
    query_low = (
        rotate(query_unit, cosine, sine_tab)
        .astype(jnp.bfloat16)
        .reshape(tok_rows, KV_HEADS, group_size, HEAD_DIM)
    )
    key_low = rotate(key_unit, cosine, sine_tab).astype(jnp.bfloat16).reshape(tok_rows, kv_width)

    def piece_scores(key_heads):
        key_count = key_heads.shape[0]
        scores = (
            jnp.einsum("tgrd,ngd->grtn", query_low, key_heads, preferred_element_type=jnp.float32)
            * score_scale
        )
        key_place = jnp.arange(key_count, dtype=jnp.int32)
        allowed = (key_place[None, :] <= position[:, None]) & (key_place[None, :] < length)
        return (scores, allowed)

    piece = (
        lax.all_gather(key_low, "seq", axis=0, tiled=True),
        lax.all_gather(value_low, "seq", axis=0, tiled=True),
    )
    forward_top_score = jnp.full((KV_HEADS, group_size, tok_rows), MASK_FILL, jnp.float32)
    key_heads = piece[0].reshape(-1, KV_HEADS, HEAD_DIM)
    value_heads = piece[1].reshape(-1, KV_HEADS, HEAD_DIM)
    scores, allowed = piece_scores(key_heads)
    masked = jnp.where(allowed, scores, MASK_FILL)
    new_top = jnp.maximum(forward_top_score, jnp.max(masked, axis=-1))
    weights = jnp.where(allowed, jnp.exp(masked - new_top[..., None]), 0.0)
    forward_weight_sum = jnp.sum(weights, axis=-1)
    added = jnp.einsum(
        "grtn,ngd->tgrd",
        weights.astype(jnp.bfloat16),
        value_heads,
        preferred_element_type=jnp.float32,
    )
    accum = added
    top_score, weight_sum, accum = (new_top, forward_weight_sum, accum)
    attn_heads = accum / jnp.transpose(weight_sum, (2, 0, 1))[..., None]
    attn_low = attn_heads.reshape(tok_rows, HEADS * HEAD_DIM).astype(jnp.bfloat16)
    residual = inputs + contract_cols(attn_low, out_full)
    normed_two_float, factor_two = rms_apply(residual, ffn_norm)
    normed_two = normed_two_float.astype(jnp.bfloat16)
    gate_val = jnp.dot(normed_two, gate_full, preferred_element_type=jnp.float32)
    up_val = jnp.dot(normed_two, up_full, preferred_element_type=jnp.float32)
    sigmoid_gate = jax.nn.sigmoid(gate_val)
    silu_gate = gate_val * sigmoid_gate
    hidden = (silu_gate * up_val).astype(jnp.bfloat16)
    result = residual + contract_cols(hidden, down_full)
    mixed = jnp.where(row_valid, result, 0.0).astype(jnp.bfloat16)[None]
    query_full, key_full, value_full, out_full, gate_full, up_full, down_full = (
        lax.all_gather(query_weight, "seq", axis=0, tiled=True),
        lax.all_gather(key_weight, "seq", axis=0, tiled=True),
        lax.all_gather(value_weight, "seq", axis=0, tiled=True),
        lax.all_gather(out_weight, "seq", axis=0, tiled=True),
        lax.all_gather(gate_weight, "seq", axis=0, tiled=True),
        lax.all_gather(up_weight, "seq", axis=0, tiled=True),
        lax.all_gather(down_weight, "seq", axis=0, tiled=True),
    )
    upstream = jnp.where(row_valid, out_grad[0].astype(jnp.float32), 0.0)
    branch_grad = upstream.astype(jnp.bfloat16)
    hidden_grad = jnp.dot(branch_grad, down_full, preferred_element_type=jnp.float32)
    down_w_grad = contract_rows(branch_grad, hidden)
    gate_grad_low = (
        hidden_grad * up_val * sigmoid_gate * (1.0 + gate_val * (1.0 - sigmoid_gate))
    ).astype(jnp.bfloat16)
    up_grad_low = (hidden_grad * silu_gate).astype(jnp.bfloat16)
    normed_two_grad = contract_cols(gate_grad_low, gate_full) + contract_cols(up_grad_low, up_full)
    gate_w_grad = contract_rows(normed_two, gate_grad_low)
    up_w_grad = contract_rows(normed_two, up_grad_low)
    residual_part, ffn_terms = rms_back(residual, factor_two, ffn_norm, normed_two_grad)
    residual_grad = upstream + residual_part
    attn_out_low = residual_grad.astype(jnp.bfloat16)
    out_w_grad = contract_rows(attn_out_low, attn_low)
    attn_grad_low = jnp.dot(attn_out_low, out_full, preferred_element_type=jnp.float32).astype(
        jnp.bfloat16
    )
    attn_grad_heads = attn_grad_low.reshape(tok_rows, KV_HEADS, group_size, HEAD_DIM)
    row_inner = jnp.transpose(
        jnp.sum(attn_grad_heads.astype(jnp.float32) * attn_heads, axis=-1), (1, 2, 0)
    )
    scaled_grad = (
        attn_grad_heads.astype(jnp.float32) / jnp.transpose(weight_sum, (2, 0, 1))[..., None]
    )
    piece = (
        lax.all_gather(key_low, "seq", axis=0, tiled=True),
        lax.all_gather(value_low, "seq", axis=0, tiled=True),
    )
    key_heads = piece[0].reshape(-1, KV_HEADS, HEAD_DIM)
    value_heads = piece[1].reshape(-1, KV_HEADS, HEAD_DIM)
    key_count = key_heads.shape[0]
    scores, allowed = piece_scores(key_heads)
    shifted = jnp.where(allowed, scores - top_score[..., None], MASK_FILL)
    exp_vals = jnp.where(allowed, jnp.exp(shifted), 0.0)
    probs = exp_vals / weight_sum[..., None]
    prob_grad = jnp.einsum(
        "tgrd,ngd->grtn", attn_grad_heads, value_heads, preferred_element_type=jnp.float32
    )
    score_grad = (probs * (prob_grad - row_inner[..., None])).astype(jnp.bfloat16)
    backward_query_acc = (
        jnp.einsum("grtn,ngd->tgrd", score_grad, key_heads, preferred_element_type=jnp.float32)
        * score_scale
    )
    key_part = (
        jnp.einsum("grtn,tgrd->ngd", score_grad, query_low, preferred_element_type=jnp.float32)
        * score_scale
    )
    exp_low = exp_vals.astype(jnp.bfloat16).astype(jnp.float32)
    value_part = jnp.einsum(
        "grtn,tgrd->ngd",
        exp_low,
        scaled_grad,
        precision=HIGHEST,
        preferred_element_type=jnp.float32,
    )
    update = jnp.concatenate(
        [key_part.reshape(key_count, kv_width), value_part.reshape(key_count, kv_width)], axis=1
    )
    query_acc, update = (backward_query_acc, update)
    key_buffer = update
    query_acc, key_buffer = (query_acc, key_buffer)
    key_value_grad = lax.psum_scatter(key_buffer, "seq", scatter_dimension=0, tiled=True)
    key_rot_grad = key_value_grad[:, :kv_width].reshape(tok_rows, KV_HEADS, HEAD_DIM)
    value_grad_low = key_value_grad[:, kv_width:].astype(jnp.bfloat16)
    query_rot_grad = query_acc.reshape(tok_rows, HEADS, HEAD_DIM)
    query_proj_grad, query_terms = rms_back(
        query_proj, query_factor, query_norm, rotate_back(query_rot_grad, cosine, sine_tab)
    )
    key_proj_grad, key_terms = rms_back(
        key_proj, key_factor, key_norm, rotate_back(key_rot_grad, cosine, sine_tab)
    )
    query_grad_low = query_proj_grad.reshape(tok_rows, HEADS * HEAD_DIM).astype(jnp.bfloat16)
    key_grad_low = key_proj_grad.reshape(tok_rows, kv_width).astype(jnp.bfloat16)
    normed_grad = (
        contract_cols(query_grad_low, query_full)
        + contract_cols(key_grad_low, key_full)
        + contract_cols(value_grad_low, value_full)
    )
    query_w_grad = contract_rows(normed, query_grad_low)
    key_w_grad = contract_rows(normed, key_grad_low)
    value_w_grad = contract_rows(normed, value_grad_low)
    input_part, attn_terms = rms_back(inputs, factor_one, attn_norm, normed_grad)
    input_grad = (residual_grad + input_part).astype(jnp.bfloat16)[None]
    attn_gain_grad, query_gain_grad, key_gain_grad, ffn_gain_grad = lax.psum(
        (
            jnp.sum(attn_terms, axis=0),
            jnp.sum(query_terms, axis=(0, 1)),
            jnp.sum(key_terms, axis=(0, 1)),
            jnp.sum(ffn_terms, axis=0),
        ),
        ("seq", "slot"),
    )
    query_share, key_share, value_share, out_share, gate_share, up_share, down_share = (
        lax.psum_scatter(query_w_grad, "seq", scatter_dimension=0, tiled=True),
        lax.psum_scatter(key_w_grad, "seq", scatter_dimension=0, tiled=True),
        lax.psum_scatter(value_w_grad, "seq", scatter_dimension=0, tiled=True),
        lax.psum_scatter(out_w_grad, "seq", scatter_dimension=0, tiled=True),
        lax.psum_scatter(gate_w_grad, "seq", scatter_dimension=0, tiled=True),
        lax.psum_scatter(up_w_grad, "seq", scatter_dimension=0, tiled=True),
        lax.psum_scatter(down_w_grad, "seq", scatter_dimension=0, tiled=True),
    )
    query_share, key_share, value_share, out_share, gate_share, up_share, down_share = (
        lax.psum(query_share.astype(jnp.bfloat16), "slot").astype(jnp.float32),
        lax.psum(key_share.astype(jnp.bfloat16), "slot").astype(jnp.float32),
        lax.psum(value_share.astype(jnp.bfloat16), "slot").astype(jnp.float32),
        lax.psum(out_share.astype(jnp.bfloat16), "slot").astype(jnp.float32),
        lax.psum(gate_share.astype(jnp.bfloat16), "slot").astype(jnp.float32),
        lax.psum(up_share.astype(jnp.bfloat16), "slot").astype(jnp.float32),
        lax.psum(down_share.astype(jnp.bfloat16), "slot").astype(jnp.float32),
    )
    return (
        mixed,
        input_grad,
        query_share,
        key_share,
        value_share,
        out_share,
        gate_share,
        up_share,
        down_share,
        attn_gain_grad,
        query_gain_grad,
        key_gain_grad,
        ffn_gain_grad,
    )


SLOTS_BY_HEADS = 4
LANES = 2 * HEAD_DIM
ROW_BLOCK = 256
VMEM_LIMIT = 60 * 1024 * 1024


def dot_nn(left, right):
    return lax.dot_general(left, right, (((1,), (0,)), ((), ())), preferred_element_type=jnp.float32)


def dot_nt(left, right):
    return lax.dot_general(left, right, (((1,), (1,)), ((), ())), preferred_element_type=jnp.float32)


def dot_tn(left, right):
    return lax.dot_general(left, right, (((0,), (0,)), ((), ())), preferred_element_type=jnp.float32)


def lane_is_low(shape):
    return lax.broadcasted_iota(jnp.int32, shape, len(shape) - 1) < HEAD_DIM


def pair_mean(values):
    low = lane_is_low(values.shape)
    first = jnp.sum(jnp.where(low, values, 0.0), axis=-1, keepdims=True)
    second = jnp.sum(jnp.where(low, 0.0, values), axis=-1, keepdims=True)
    return jnp.where(low, first, second) * (1.0 / HEAD_DIM)


def pair_turn(values, cosine, sine_signed):
    lane = lax.broadcasted_iota(jnp.int32, values.shape, 1)
    near = lax.rem(lane, HEAD_DIM) < HEAD_DIM // 2
    half = HEAD_DIM // 2
    turned = jnp.where(near, pltpu.roll(values, LANES - half, 1), pltpu.roll(values, half, 1))
    return values * cosine + turned * sine_signed


def pair_swap(values):
    return pltpu.roll(values.astype(jnp.float32), HEAD_DIM, 1)


def array(kind, *shape):
    return jax.ShapeDtypeStruct(shape, kind)


def call(kernel, out_shape, scratch_shapes=(), token=False):
    vmem, anywhere = pl.BlockSpec(memory_space=pltpu.VMEM), pl.BlockSpec(memory_space=pl.ANY)
    single = not isinstance(out_shape, tuple)
    shapes = ((out_shape,) if single else out_shape) + ((array(jnp.float32, 8, LANES),) if token else ())

    def apply(*operands, smem=0, tokens=()):
        given = len(operands)
        results = given + len(tokens) + len(shapes)

        def whole(*refs):
            if token:
                refs[results - 1][...] = jnp.zeros((8, LANES), jnp.float32)
            kernel(*refs[:given], *refs[given + len(tokens) : results - token], *refs[results:])

        in_specs = [pl.BlockSpec(memory_space=pltpu.SMEM)] * smem + [vmem] * (given - smem) + [anywhere] * len(tokens)
        outputs = pl.pallas_call(
            whole,
            out_shape=shapes,
            in_specs=in_specs,
            out_specs=(vmem,) * len(shapes),
            scratch_shapes=scratch_shapes,
            compiler_params=pltpu.CompilerParams(vmem_limit_bytes=VMEM_LIMIT),
        )(*operands, *tokens)
        return outputs[0] if len(shapes) == 1 else outputs

    return apply


def after(values, *tokens):
    count = len(values)
    anywhere = pl.BlockSpec(memory_space=pl.ANY)
    return pl.pallas_call(
        lambda *refs: None,
        out_shape=tuple(array(value.dtype, *value.shape) for value in values),
        in_specs=[anywhere] * (count + len(tokens)),
        out_specs=(anywhere,) * count,
        input_output_aliases={i: i for i in range(count)},
    )(*values, *tokens)


def block_rows(me_ref, partner, rows):
    return pl.ds(pl.multiple_of(jnp.bitwise_xor(me_ref[0], partner) * rows, rows), rows)


def store_pair(me_ref, chip, values, own_ref, other_ref):
    rows = values.shape[0] // 2
    first = jnp.bitwise_and(me_ref[0], 1) == 0
    own_ref[chip] = jnp.where(first, values[:rows], values[rows:]).astype(jnp.bfloat16)
    other_ref[chip] = jnp.where(first, values[rows:], values[:rows]).astype(jnp.bfloat16)


def pack_attention_kernel(query_ref, key_ref, value_ref, owned_ref):
    for index in range(0, KV_HEADS, 2):
        lanes = pl.ds(index * HEAD_DIM, LANES)
        key, value = key_ref[:, lanes], value_ref[:, lanes]
        low = lane_is_low(key.shape)
        key, value = key.astype(jnp.float32), value.astype(jnp.float32)
        pairs = (jnp.where(low, key, pair_swap(value)), jnp.where(low, pair_swap(key), value))
        for step in range(2):
            owned_ref[index + step, :, :LANES] = query_ref[:, pl.ds((index + step) * LANES, LANES)]
            owned_ref[index + step, :, LANES:] = pairs[step].astype(jnp.bfloat16)


def pack_units_kernel(slot_ref, gate_ref, up_ref, down_ref, first_ref, second_ref):
    rows = first_ref.shape[1]
    block = second_ref.shape[2] // 3
    cut = block * KV_HEADS
    half = pl.ds(pl.multiple_of(jnp.bitwise_and(slot_ref[0], 1) * rows, rows), rows)
    for index in range(KV_HEADS):
        for place, ref in enumerate((gate_ref, up_ref, down_ref)):
            start = place * block + (LANES if place == 2 else 0)
            first_ref[index, :, start : start + block] = ref[half, pl.ds(index * block, block)]
            second_ref[index, :, place * block : (place + 1) * block] = ref[:, pl.ds(cut + index * block, block)]
    for index in range(0, KV_HEADS, 2):
        lanes = pl.ds(2 * cut + index * HEAD_DIM, LANES)
        gate, up, down = (ref[half, lanes].astype(jnp.float32) for ref in (gate_ref, up_ref, down_ref))
        low = lane_is_low(gate.shape)
        rests = (jnp.where(low, gate, pair_swap(up)), jnp.where(low, pair_swap(gate), up))
        downs = (jnp.where(low, down, pair_swap(down)), jnp.where(low, pair_swap(down), down))
        for step in range(2):
            first_ref[index + step, :, 2 * block : 2 * block + LANES] = rests[step].astype(jnp.bfloat16)
            first_ref[index + step, :, 3 * block + LANES :] = downs[step].astype(jnp.bfloat16)


def attention_forward_kernel(length_ref, me_ref, *refs):
    x_refs = refs[:KV_HEADS]
    (
        weight_ref, gain_ref, q_gain_ref, k_gain_ref, cos_ref, sin_ref,
        x_all_ref, normed_ref, q_proj_ref, kv_proj_ref, q_low_ref, k_pair_ref, v_pair_ref, attn_ref, attn_low_ref, weight_inv_ref,
    ) = refs[KV_HEADS:]
    tok_rows = x_refs[0].shape[0]
    total = tok_rows * KV_HEADS
    length = length_ref[0]
    low = lane_is_low((ROW_BLOCK, LANES))
    for partner in range(KV_HEADS):
        x_all_ref[block_rows(me_ref, partner, tok_rows), :] = x_refs[partner][...]
    for start in range(0, total, ROW_BLOCK):
        rows = pl.ds(start, ROW_BLOCK)
        x = x_all_ref[rows, :].astype(jnp.float32)
        factor = lax.rsqrt(jnp.mean(x * x, axis=-1, keepdims=True) + EPSILON)
        normed = (x * factor * gain_ref[...]).astype(jnp.bfloat16)
        normed_ref[rows, :] = normed
        proj = dot_nn(normed, weight_ref[...])
        q_proj = proj[:, :LANES]
        kv_proj = proj[:, LANES:]
        q_proj_ref[rows, :] = q_proj
        kv_proj_ref[rows, :] = kv_proj
        cosine, sine = cos_ref[rows, :], sin_ref[rows, :]
        q_factor = lax.rsqrt(pair_mean(q_proj * q_proj) + EPSILON)
        q_low_ref[rows, :] = pair_turn(q_proj * q_factor * q_gain_ref[...], cosine, sine).astype(jnp.bfloat16)
        k_factor = jnp.where(low, lax.rsqrt(pair_mean(kv_proj * kv_proj) + EPSILON), 1.0)
        kv = pair_turn(
            kv_proj * k_factor * k_gain_ref[...], jnp.where(low, cosine, 1.0), jnp.where(low, sine, 0.0)
        )
        swapped = pltpu.roll(kv, HEAD_DIM, 1)
        k_pair_ref[rows, :] = jnp.where(low, kv, swapped).astype(jnp.bfloat16)
        v_pair_ref[rows, :] = jnp.where(low, swapped, kv).astype(jnp.bfloat16)

    scale = HEAD_DIM ** (-0.5)
    for start in range(0, total, ROW_BLOCK):
        rows = pl.ds(start, ROW_BLOCK)
        q = q_low_ref[rows, :] * scale
        zero = jnp.zeros_like(q)
        heads = (jnp.where(low, q, zero), jnp.where(low, zero, q))
        results = []
        for q_head in heads:
            weight_sum = jnp.zeros((ROW_BLOCK, 1), jnp.float32)
            summed = jnp.zeros((ROW_BLOCK, LANES), jnp.float32)
            if start > 0:
                past = pl.ds(0, start)
                exp_vals = jnp.exp(dot_nt(q_head, k_pair_ref[past, :]))
                weight_sum += jnp.sum(exp_vals, axis=-1, keepdims=True)
                summed += dot_nn(exp_vals.astype(jnp.bfloat16), v_pair_ref[past, :])
            scores = dot_nt(q_head, k_pair_ref[rows, :])
            query = lax.broadcasted_iota(jnp.int32, scores.shape, 0)
            key = lax.broadcasted_iota(jnp.int32, scores.shape, 1)
            allowed = (key <= query) & (key + start < length)
            exp_vals = jnp.where(allowed, jnp.exp(scores), 0.0)
            weight_sum += jnp.sum(exp_vals, axis=-1, keepdims=True)
            summed += dot_nn(exp_vals.astype(jnp.bfloat16), v_pair_ref[rows, :])
            inverse = 1.0 / weight_sum
            results.append((summed * inverse, inverse))
        attn = jnp.where(low, results[0][0], results[1][0])
        attn_ref[rows, :] = attn
        attn_low_ref[rows, :] = attn.astype(jnp.bfloat16)
        weight_inv_ref[rows, :] = jnp.where(low, results[0][1], results[1][1])


def attention_backward_kernel(
    length_ref, me_ref, dattn_ref, weight_ref, q_gain_ref, k_gain_ref, cos_ref, sin_ref,
    q_proj_ref, kv_proj_ref, q_low_ref, k_pair_ref, v_pair_ref, attn_ref, weight_inv_ref,
    dnormed_own_ref, dnormed_other_ref, dproj_ref, terms_ref, dq_acc, dk_acc, dv_acc,
):
    total = dattn_ref.shape[0]
    length = length_ref[0]
    low = lane_is_low((ROW_BLOCK, LANES))
    scale = HEAD_DIM ** (-0.5)
    dk_acc[...] = jnp.zeros_like(dk_acc)
    dv_acc[...] = jnp.zeros_like(dv_acc)
    for start in range(0, total, ROW_BLOCK):
        rows = pl.ds(start, ROW_BLOCK)
        q = q_low_ref[rows, :] * scale
        dattn = dattn_ref[rows, :]
        zero = jnp.zeros_like(q)
        inner = dattn.astype(jnp.float32) * attn_ref[rows, :]
        inverses = weight_inv_ref[rows, :]
        dq_heads = []
        for head in range(2):
            mine = low if head == 0 else jnp.logical_not(low)
            q_head = jnp.where(mine, q, zero)
            dattn_head = jnp.where(mine, dattn, zero)
            delta = jnp.sum(jnp.where(mine, inner, 0.0), axis=-1, keepdims=True)
            inverse = inverses[:, head * HEAD_DIM : head * HEAD_DIM + 1]
            dq = jnp.zeros((ROW_BLOCK, LANES), jnp.float32)
            spans = ([(0, start)] if start > 0 else []) + [(start, ROW_BLOCK)]
            for key_start, key_count in spans:
                keys = pl.ds(key_start, key_count)
                k_pair = k_pair_ref[keys, :]
                probs = jnp.exp(dot_nt(q_head, k_pair)) * inverse
                if key_start == start:
                    query = lax.broadcasted_iota(jnp.int32, probs.shape, 0)
                    key = lax.broadcasted_iota(jnp.int32, probs.shape, 1)
                    allowed = (key <= query) & (key + start < length)
                    probs = jnp.where(allowed, probs, 0.0)
                dprobs = dot_nt(dattn_head, v_pair_ref[keys, :])
                dscores = (probs * (dprobs - delta)).astype(jnp.bfloat16)
                dq += dot_nn(dscores, k_pair)
                dk_acc[keys, :] += dot_tn(dscores, q_head)
                dv_acc[keys, :] += dot_tn(probs.astype(jnp.bfloat16), dattn_head)
            dq_heads.append(dq)
        dq_acc[rows, :] = jnp.where(low, dq_heads[0], dq_heads[1]) * scale

    q_terms = jnp.zeros((1, LANES), jnp.float32)
    k_terms = jnp.zeros((1, LANES), jnp.float32)
    for start in range(0, total, ROW_BLOCK):
        rows = pl.ds(start, ROW_BLOCK)
        cosine, sine = cos_ref[rows, :], sin_ref[rows, :]
        q_proj = q_proj_ref[rows, :]
        upstream = pair_turn(dq_acc[rows, :], cosine, -sine)
        factor = lax.rsqrt(pair_mean(q_proj * q_proj) + EPSILON)
        normal = q_proj * factor
        weighted = upstream * q_gain_ref[...]
        dq_proj = factor * (weighted - normal * pair_mean(weighted * normal))
        q_terms += jnp.sum(upstream * normal, axis=0, keepdims=True)

        dk = dk_acc[rows, :]
        dv = dv_acc[rows, :]
        dk = dk + pltpu.roll(dk, HEAD_DIM, 1)
        dv = dv + pltpu.roll(dv, HEAD_DIM, 1)
        kv_proj = kv_proj_ref[rows, :]
        upstream = pair_turn(jnp.where(low, dk, 0.0), jnp.where(low, cosine, 1.0), jnp.where(low, -sine, 0.0))
        factor = lax.rsqrt(pair_mean(kv_proj * kv_proj) + EPSILON)
        normal = kv_proj * factor
        weighted = upstream * k_gain_ref[...]
        dk_proj = factor * (weighted - normal * pair_mean(weighted * normal))
        k_terms += jnp.sum(upstream * normal, axis=0, keepdims=True)
        dkv_proj = jnp.where(low, dk_proj, dv)
        dproj = jnp.concatenate([dq_proj, dkv_proj], axis=1).astype(jnp.bfloat16)
        dproj_ref[rows, :] = dproj
        store_pair(me_ref, start // ROW_BLOCK, dot_nt(dproj, weight_ref[...]), dnormed_own_ref, dnormed_other_ref)
    terms_ref[0:1, :] = q_terms
    terms_ref[1:2, :] = k_terms


def residual_kernel(me_ref, x_ref, *refs):
    attn_refs = refs[:KV_HEADS]
    out_weight_ref, gain_ref, residual_ref, attn_own_ref, normed_ref, attn_scratch, scratch = refs[KV_HEADS:]
    total, width = x_ref.shape
    tok_rows = total // KV_HEADS
    for partner in range(KV_HEADS):
        attn_scratch[:, block_rows(me_ref, partner, LANES)] = attn_refs[partner][...]
    for start in range(0, total, ROW_BLOCK):
        rows = pl.ds(start, ROW_BLOCK)
        residual = x_ref[rows, :].astype(jnp.float32) + dot_nt(attn_scratch[rows, :], out_weight_ref[...])
        scratch[rows, :] = residual
        factor = lax.rsqrt(jnp.mean(residual * residual, axis=-1, keepdims=True) + EPSILON)
        normed_ref[rows, :] = (residual * factor * gain_ref[...]).astype(jnp.bfloat16)
    residual_ref[...] = scratch[block_rows(me_ref, 0, tok_rows), :]
    attn_own_ref[...] = attn_scratch[block_rows(me_ref, 0, tok_rows), :]


def unit_share(gate, up, upstream):
    sigmoid = jax.nn.sigmoid(gate)
    silu = gate * sigmoid
    dgate = upstream * up * sigmoid * (1.0 + gate * (1.0 - sigmoid))
    return silu * up, dgate, upstream * silu


def first_units_kernel(me_ref, slot_ref, normed_ref, *refs):
    dout_refs = refs[:KV_HEADS]
    own_ref, other_ref, dout_ref, weight_ref, hidden_ref, dgate_up_ref = refs[KV_HEADS:]
    total = normed_ref.shape[0]
    block = hidden_ref.shape[1] - LANES
    units = 2 * block + LANES
    depth, half = 2 * own_ref.shape[1], own_ref.shape[1]
    odd = jnp.bitwise_and(slot_ref[0], 1)
    for index in range(KV_HEADS):
        weight_ref[pl.ds(pl.multiple_of(index * depth + odd * half, half), half), :] = own_ref[index]
        weight_ref[pl.ds(pl.multiple_of(index * depth + (1 - odd) * half, half), half), :] = other_ref[index]
    for partner in range(KV_HEADS):
        dout_ref[block_rows(me_ref, partner, depth), :] = dout_refs[partner][...]
    low = lane_is_low((ROW_BLOCK, LANES))
    for start in range(0, total, ROW_BLOCK):
        rows = pl.ds(start, ROW_BLOCK)
        both = dot_nn(normed_ref[rows, :], weight_ref[:, :units])
        dhidden = dot_nn(dout_ref[rows, :], weight_ref[:, units:])
        hidden, dgate, dup = unit_share(both[:, :block], both[:, block : 2 * block], dhidden[:, :block])
        rest = both[:, 2 * block :]
        swapped = pltpu.roll(rest, HEAD_DIM, 1)
        rest_hidden, rest_dgate, rest_dup = unit_share(
            jnp.where(low, rest, swapped), jnp.where(low, swapped, rest), dhidden[:, block:]
        )
        hidden_ref[rows, :block] = hidden.astype(jnp.bfloat16)
        hidden_ref[rows, block:] = jnp.where(low, rest_hidden, 0.0).astype(jnp.bfloat16)
        dgate_up_ref[rows, :block] = dgate.astype(jnp.bfloat16)
        dgate_up_ref[rows, block : 2 * block] = dup.astype(jnp.bfloat16)
        dgate_up_ref[rows, 2 * block :] = jnp.where(low, rest_dgate, rest_dup).astype(jnp.bfloat16)


def second_units_kernel(
    me_ref, normed_ref, dout_ref, first_ref, second_ref, dgate_up_first_ref, hidden_ref, dgate_up_ref, own_ref, other_ref
):
    total = normed_ref.shape[0]
    block = hidden_ref.shape[1]
    units = dgate_up_first_ref.shape[1]
    for start in range(0, total, ROW_BLOCK):
        rows = pl.ds(start, ROW_BLOCK)
        both = dot_nn(normed_ref[rows, :], second_ref[:, : 2 * block])
        dhidden = dot_nn(dout_ref[rows, :], second_ref[:, 2 * block :])
        hidden, dgate, dup = unit_share(both[:, :block], both[:, block:], dhidden)
        hidden_ref[rows, :] = hidden.astype(jnp.bfloat16)
        dgate_up = jnp.concatenate([dgate, dup], axis=1).astype(jnp.bfloat16)
        dgate_up_ref[rows, :] = dgate_up
        dnormed = dot_nt(dgate_up, second_ref[:, : 2 * block]) + dot_nt(dgate_up_first_ref[rows, :], first_ref[:, :units])
        store_pair(me_ref, start // ROW_BLOCK, dnormed, own_ref, other_ref)


def unit_grads_kernel(normed_ref, dout_ref, hidden_ref, dgate_up_ref, grads_ref):
    slots, _, rows_each, cols = grads_ref.shape
    units = dgate_up_ref.shape[1]
    for start in range(0, normed_ref.shape[1], ROW_BLOCK):
        rows = pl.ds(start, ROW_BLOCK)
        gate_up = dot_tn(normed_ref[:, rows], dgate_up_ref[...]).astype(jnp.bfloat16)
        down = dot_tn(dout_ref[:, rows], hidden_ref[...])[:, : cols - units].astype(jnp.bfloat16)
        for piece in range(0, ROW_BLOCK, rows_each):
            owner, slot = divmod((start + piece) // rows_each, slots)
            grads_ref[slot, owner, :, :units] = gate_up[piece : piece + rows_each]
            grads_ref[slot, owner, :, units:] = down[piece : piece + rows_each]


def mixed_kernel(me_ref, hidden_first_ref, hidden_second_ref, first_ref, second_ref, own_ref, other_ref):
    total = hidden_first_ref.shape[0]
    block = hidden_second_ref.shape[1]
    units = 2 * block + LANES
    for start in range(0, total, ROW_BLOCK):
        rows = pl.ds(start, ROW_BLOCK)
        part = dot_nt(hidden_first_ref[rows, :], first_ref[:, units:]) + dot_nt(
            hidden_second_ref[rows, :], second_ref[:, 2 * block :]
        )
        store_pair(me_ref, start // ROW_BLOCK, part, own_ref, other_ref)


def add_kernel(me_ref, own_ref, other_ref, *part_refs):
    chip = lax.shift_right_logical(me_ref[0], 1)
    for i, part_ref in enumerate(part_refs):
        place = jnp.bitwise_xor(chip, i)
        part_ref[...] = (own_ref[place].astype(jnp.float32) + other_ref[place].astype(jnp.float32)).astype(jnp.bfloat16)


def add_blocks_kernel(own_ref, other_ref, sum_ref):
    sum_ref[...] = (own_ref[...].astype(jnp.float32) + other_ref[...].astype(jnp.float32)).astype(sum_ref.dtype)


def four_sum(parts):
    first, second, third, fourth = (part.astype(jnp.float32) for part in parts)
    return (first + second) + (third + fourth)


def four_sum_kernel(*refs):
    refs[4][...] = four_sum([ref[...] for ref in refs[:4]]).astype(refs[4].dtype)


def residual_back_kernel(
    parts_ref, residual_ref, upstream_ref, gain_ref, out_weight_ref,
    residual_grad_ref, low_ref, dattn_ref, terms_ref,
):
    values = residual_ref[...]
    factor = lax.rsqrt(jnp.mean(values * values, axis=-1, keepdims=True) + EPSILON)
    part, terms = rms_back(values, factor, gain_ref[...], four_sum([parts_ref[i] for i in range(4)]))
    residual_grad = upstream_ref[...].astype(jnp.float32) + part
    residual_grad_ref[...] = residual_grad
    low = residual_grad.astype(jnp.bfloat16)
    low_ref[...] = low
    dattn = dot_nn(low, out_weight_ref[...]).astype(jnp.bfloat16)
    for index in range(KV_HEADS):
        dattn_ref[index] = dattn[:, index * LANES : (index + 1) * LANES]
    terms_ref[...] = jnp.sum(terms, axis=0, keepdims=True)


def input_back_kernel(
    part_a_ref, part_b_ref, part_c_ref, part_d_ref, tokens_ref, residual_grad_ref, gain_ref, input_grad_ref,
):
    values = tokens_ref[...].astype(jnp.float32)
    factor = lax.rsqrt(jnp.mean(values * values, axis=-1, keepdims=True) + EPSILON)
    part, _ = rms_back(values, factor, gain_ref[...], four_sum([ref[...] for ref in (part_a_ref, part_b_ref, part_c_ref, part_d_ref)]))
    input_grad_ref[...] = (residual_grad_ref[...] + part).astype(jnp.bfloat16)


def attention_gain_kernel(me_ref, x_ref, own_ref, other_ref, terms_ref):
    rows = own_ref.shape[1]
    core = jnp.bitwise_and(me_ref[0], 1)
    terms = jnp.zeros(terms_ref.shape, jnp.float32)
    for chip in range(own_ref.shape[0]):
        for place, ref in ((core, own_ref), (1 - core, other_ref)):
            x = x_ref[pl.ds(pl.multiple_of(chip * 2 * rows + place * rows, rows), rows), :].astype(jnp.float32)
            factor = lax.rsqrt(jnp.mean(x * x, axis=-1, keepdims=True) + EPSILON)
            terms += jnp.sum(ref[chip].astype(jnp.float32) * (x * factor), axis=0, keepdims=True)
    terms_ref[...] = terms


def projection_grads_kernel(normed_ref, dproj_ref, grads_ref):
    width = normed_ref.shape[1]
    depth = grads_ref.shape[1]
    for start in range(0, width, ROW_BLOCK):
        blocks = pl.ds(start // depth, ROW_BLOCK // depth)
        grads = dot_tn(normed_ref[:, pl.ds(start, ROW_BLOCK)], dproj_ref[...]).astype(jnp.bfloat16)
        grads_ref[blocks] = grads.reshape(-1, depth, 2 * LANES)


def out_grads_kernel(me_ref, dbranch_ref, attn_ref, own_ref, other_ref):
    width = dbranch_ref.shape[1]
    for start in range(0, width, ROW_BLOCK):
        grads = dot_tn(dbranch_ref[:, pl.ds(start, ROW_BLOCK)], attn_ref[...])
        store_pair(me_ref, start // ROW_BLOCK, grads, own_ref, other_ref)


def rows_kernel(attn_ref, attn_out_ref, first_ref, second_ref, *out_refs):
    query_ref, key_ref, value_ref, out_ref, gate_ref, up_ref, down_ref = out_refs
    f32 = jnp.float32
    block = second_ref.shape[3] // 3
    cut = KV_HEADS * block
    out_ref[...] = attn_out_ref[...].astype(f32)
    for index in range(KV_HEADS):
        query_ref[:, pl.ds(index * LANES, LANES)] = attn_ref[index, :, :LANES].astype(f32)
    low = lane_is_low((attn_ref.shape[1], LANES))
    for index in range(0, KV_HEADS, 2):
        lanes = pl.ds(index * HEAD_DIM, LANES)
        even = attn_ref[index, :, LANES : 2 * LANES].astype(f32)
        odd = attn_ref[index + 1, :, LANES : 2 * LANES].astype(f32)
        key_ref[:, lanes] = jnp.where(low, even, pair_swap(odd))
        value_ref[:, lanes] = jnp.where(low, pair_swap(even), odd)
    low = lane_is_low((first_ref.shape[2], LANES))
    for slot in range(first_ref.shape[0]):
        rows = pl.ds(slot * first_ref.shape[2], first_ref.shape[2])
        for index in range(KV_HEADS):
            for place, ref in enumerate((gate_ref, up_ref, down_ref)):
                start = place * block + (LANES if place == 2 else 0)
                ref[rows, pl.ds(index * block, block)] = first_ref[slot, index, :, start : start + block].astype(f32)
                start = place * block
                ref[rows, pl.ds(cut + index * block, block)] = second_ref[slot, index, :, start : start + block].astype(f32)
        for index in range(0, KV_HEADS, 2):
            lanes = pl.ds(2 * cut + index * HEAD_DIM, LANES)
            even = first_ref[slot, index, :, 2 * block : 2 * block + LANES].astype(f32)
            odd = first_ref[slot, index + 1, :, 2 * block : 2 * block + LANES].astype(f32)
            gate_ref[rows, lanes] = jnp.where(low, even, pair_swap(odd))
            up_ref[rows, lanes] = jnp.where(low, pair_swap(even), odd)
            even = first_ref[slot, index, :, 3 * block + LANES :].astype(f32)
            odd = first_ref[slot, index + 1, :, 3 * block + LANES :].astype(f32)
            down_ref[rows, lanes] = jnp.concatenate([even, odd], axis=1)


def rotary_pair_tables(total):
    half = HEAD_DIM // 2
    exponent = np.arange(half, dtype=np.float32) * np.float32(2.0 / HEAD_DIM)
    inverse = np.float32(THETA_BASE) ** (-exponent)
    angles = np.arange(total, dtype=np.float32)[:, None] * inverse[None, :]
    cosine, sine = np.cos(angles), np.sin(angles)
    return (
        jnp.asarray(np.concatenate([cosine] * 4, axis=1), jnp.float32),
        jnp.asarray(np.concatenate([-sine, sine, -sine, sine], axis=1), jnp.float32),
    )


def to_partner(block, partner):
    return lax.ppermute(block, "seq", [(i, i ^ partner) for i in range(KV_HEADS)])


def gather_chips(block):
    return [block] + [to_partner(block, partner) for partner in (2, 4, 6)]


def gather_cores(parts):
    return [part for pair in zip(parts, [to_partner(part, 1) for part in parts]) for part in pair]


def swap_chips(blocks):
    cores = [list(range(core, KV_HEADS, 2)) for core in range(2)]
    return lax.all_to_all(blocks, "seq", 0, 0, axis_index_groups=cores, tiled=True)


def sum_partners(me, own, other, *tokens):
    parts = call(add_kernel, (array(own.dtype, *own.shape[1:]),) * own.shape[0])(
        me, own, to_partner(other, 1), smem=1, tokens=tokens
    )
    return [parts[0]] + [to_partner(parts[i], 2 * i) for i in (1, 2, 3)]


def add(left, right):
    return (left.astype(jnp.float32) + right.astype(jnp.float32)).astype(left.dtype)


def inward(part):
    return lax.ppermute(part, "slot", [(0, 1), (3, 2)])


def across(part):
    return lax.ppermute(part, "slot", [(1, 2), (2, 1)])


def outward(total):
    slot = lax.axis_index("slot")
    return jnp.where((slot == 1) | (slot == 2), total, lax.ppermute(total, "slot", [(1, 0), (2, 3)]))


def sum_slots(*parts):
    parts = [add(part, inward(part)) for part in parts]
    parts = [add(part, across(part)) for part in parts]
    return [outward(part) for part in parts]


def sum_devices(values):
    for partner in (1, 2, 4):
        values = values + to_partner(values, partner)
    for partner in (1, 2):
        values = values + lax.ppermute(values, "slot", [(i, i ^ partner) for i in range(SLOTS_BY_HEADS)])
    return values


def heads_body(
    tokens, lengths, query_weight, key_weight, value_weight, out_weight, gate_weight, up_weight, down_weight,
    attn_norm, query_norm, key_norm, ffn_norm, out_grad,
):
    f32, bf16 = jnp.float32, jnp.bfloat16
    count = KV_HEADS
    tok_rows, width = tokens.shape[1:]
    depth = query_weight.shape[0]
    total = tok_rows * count
    units = gate_weight.shape[1] // count
    block = (units - HEAD_DIM) // 2
    length = lengths[0]
    index = lax.axis_index("seq")
    me = index[None]
    slot = lax.axis_index("slot")[None]
    position = index * tok_rows + jnp.arange(tok_rows, dtype=jnp.int32)
    row_valid = (position < length)[:, None]

    def swap(blocks):
        return lax.all_to_all(blocks, "seq", 0, 0, tiled=True)

    x_parts = gather_cores(gather_chips(tokens[0]))
    attn_owned, packed = call(pack_attention_kernel, array(bf16, count, depth, 2 * LANES), token=True)(
        query_weight, key_weight, value_weight
    )
    attn_weight = swap(attn_owned).reshape(width, 2 * LANES)
    first_owned, second_owned = call(
        pack_units_kernel,
        (array(bf16, count, depth // 2, 3 * block + 2 * LANES), array(bf16, count, depth, 3 * block)),
    )(slot, gate_weight, up_weight, down_weight, smem=1, tokens=(packed,))
    upstream = jnp.where(row_valid, out_grad[0], jnp.zeros_like(out_grad[0]))
    first_owned, out_weight = after((first_owned, out_weight), *x_parts, attn_weight)
    first_own = swap(first_owned)
    out_full = lax.all_gather(out_weight, "seq", axis=0, tiled=True)

    cosine, sine = rotary_pair_tables(total)
    q_gain = jnp.concatenate([query_norm, query_norm])[None]
    k_gain = jnp.concatenate([key_norm, jnp.ones_like(key_norm)])[None]
    x_all, normed, q_proj, kv_proj, q_low, k_pair, v_pair, attn, attn_low, weight_inv, attended = call(
        attention_forward_kernel,
        (
            array(bf16, total, width), array(bf16, total, width), array(f32, total, LANES), array(f32, total, LANES),
            array(bf16, total, LANES), array(bf16, total, LANES), array(bf16, total, LANES), array(f32, total, LANES),
            array(bf16, total, LANES), array(f32, total, LANES),
        ),
        token=True,
    )(lengths, me, *x_parts, attn_weight, attn_norm[None], q_gain, k_gain, cosine, sine, smem=2)

    attn_parts = gather_cores(gather_chips(attn_low))
    first_own, upstream = after((first_own, upstream), attended)
    first_other = lax.ppermute(first_own, "slot", [(i, i ^ 1) for i in range(SLOTS_BY_HEADS)])
    dout_parts = gather_chips(upstream)
    (second_owned,) = after((second_owned,), *attn_parts, first_own)
    residual, attn_own, normed_two, normed_ready = call(
        residual_kernel,
        (array(f32, tok_rows, width), array(bf16, tok_rows, width), array(bf16, total, width)),
        scratch_shapes=[pltpu.VMEM((total, width), bf16), pltpu.VMEM((total, width), f32)],
        token=True,
    )(me, x_all, *attn_parts, out_full, ffn_norm[None], smem=1, tokens=(second_owned,))
    second_weight = swap(second_owned).reshape(width, -1)

    dout_parts = gather_cores(after(tuple(dout_parts), normed_ready, first_other))
    dout_all, first_weight, hidden_first, dgate_up_first = call(
        first_units_kernel,
        (
            array(bf16, total, width), array(bf16, width, 3 * block + 2 * LANES), array(bf16, total, block + LANES),
            array(bf16, total, 2 * block + LANES),
        ),
    )(me, slot, normed_two, *dout_parts, first_own, first_other, smem=2)
    def unit_grads(hidden, dgate_up, cols, *tokens):
        grads, done = call(unit_grads_kernel, array(bf16, SLOTS_BY_HEADS, count, depth // SLOTS_BY_HEADS, cols), token=True)(
            normed_two, dout_all, hidden, dgate_up, tokens=tokens
        )
        return done, lax.psum_scatter(grads.reshape(width, cols), "slot", scatter_dimension=0, tiled=True)

    def to_owners(sums):
        return swap(sums.reshape(count, -1, sums.shape[1]))

    halves = (array(bf16, count // 2, tok_rows, width),) * 2
    hidden_second, dgate_up_second, *normed_two_grad, summed = call(
        second_units_kernel, (array(bf16, total, block), array(bf16, total, 2 * block), *halves), token=True
    )(me, normed_two, dout_all, first_weight, second_weight, dgate_up_first, smem=1)
    first_grads, first_sums = unit_grads(
        hidden_first, dgate_up_first, 3 * block + LANES + HEAD_DIM, summed
    )
    normed_two_sum = call(add_blocks_kernel, halves[0])(
        normed_two_grad[0], to_partner(normed_two_grad[1], 1), tokens=(first_grads,)
    )
    residual_grad, attn_out_low, dattn, ffn_terms, branched = call(
        residual_back_kernel,
        (
            array(f32, tok_rows, width), array(bf16, tok_rows, width), array(bf16, count, tok_rows, LANES),
            array(f32, 1, width),
        ),
        token=True,
    )(swap_chips(normed_two_sum), residual, upstream, ffn_norm[None], out_full)
    second_grads, second_sums = unit_grads(hidden_second, dgate_up_second, 3 * block, branched)
    dattn = swap(dattn)
    dnormed_own, dnormed_other, dproj, terms = call(
        attention_backward_kernel,
        (*halves, array(bf16, total, 2 * LANES), array(f32, 2, LANES)),
        scratch_shapes=[pltpu.VMEM((total, LANES), f32)] * 3,
    )(
        lengths, me, dattn.reshape(total, LANES), attn_weight, q_gain, k_gain, cosine, sine, q_proj, kv_proj, q_low, k_pair,
        v_pair, attn, weight_inv, smem=2, tokens=(second_grads,),
    )
    proj_grads, projected = call(projection_grads_kernel, array(bf16, count, depth, 2 * LANES), token=True)(normed, dproj)
    proj_part = swap(proj_grads)
    (first_sums,) = after((first_sums,), projected)
    first_rows = to_owners(first_sums)
    first_all = lax.all_gather(first_rows, "slot", axis=0)

    mixed_halves = call(mixed_kernel, halves)(
        me, hidden_first, hidden_second, first_weight, second_weight, smem=1, tokens=(projected,)
    )

    *out_grads, out_ready = call(out_grads_kernel, halves, token=True)(me, attn_out_low, attn_own, smem=1, tokens=(projected,))
    second_sums, proj_part = after((second_sums, proj_part), out_ready, first_rows)
    second_all = lax.all_gather(to_owners(second_sums), "slot", axis=0)
    out_part, out_summed = call(four_sum_kernel, array(bf16, tok_rows, width), token=True)(*sum_partners(me, *out_grads))
    attn_terms = call(attention_gain_kernel, array(f32, 1, width))(
        me, x_all, dnormed_own, dnormed_other, smem=1, tokens=(out_summed,)
    )
    proj_rows, out_rows = sum_slots(proj_part, out_part)
    dnormed_parts = sum_partners(me, dnormed_own, dnormed_other, attn_terms)
    mixed_parts = sum_partners(me, *mixed_halves, attn_terms)
    input_grad = call(input_back_kernel, array(bf16, tok_rows, width))(
        *dnormed_parts, tokens[0], residual_grad, attn_norm[None]
    )
    result = residual + sum(part.astype(f32) for part in mixed_parts)
    mixed = jnp.where(row_valid, result, 0.0).astype(bf16)[None]
    shapes = (query_weight, key_weight, value_weight, out_weight, gate_weight, up_weight, down_weight)
    weight_grads = call(rows_kernel, tuple(array(f32, *weight.shape) for weight in shapes))(
        proj_rows, out_rows, first_all, second_all
    )

    half = HEAD_DIM
    gains = jnp.concatenate([attn_terms[0], ffn_terms[0], terms[0, :half] + terms[0, half:], terms[1, :half]])
    gains = sum_devices(gains.reshape(-1, LANES)).reshape(-1)
    return (
        mixed, input_grad[None], *weight_grads, gains[:width], gains[2 * width : 2 * width + half],
        gains[2 * width + half :], gains[width : 2 * width],
    )


def solution(mesh):
    in_specs = (
        P("slot", "seq", None),
        P("slot"),
        P("seq", None),
        P("seq", None),
        P("seq", None),
        P("seq", None),
        P("seq", None),
        P("seq", None),
        P("seq", None),
        P(),
        P(),
        P(),
        P(),
        P("slot", "seq", None),
    )
    out_specs = (
        P("slot", "seq", None),
        P("slot", "seq", None),
        P("seq", None),
        P("seq", None),
        P("seq", None),
        P("seq", None),
        P("seq", None),
        P("seq", None),
        P("seq", None),
        P(),
        P(),
        P(),
        P(),
    )
    by_heads = mesh.shape["seq"] == KV_HEADS and mesh.shape["slot"] == SLOTS_BY_HEADS
    body = heads_body if by_heads else general_body
    return jax.shard_map(body, mesh=mesh, in_specs=in_specs, out_specs=out_specs, check_vma=False)
```

```python
import functools

import jax
import jax.numpy as jnp
import numpy as np
from jax import lax
from jax.experimental import pallas as pl
from jax.experimental.pallas import tpu as pltpu
from jax.sharding import PartitionSpec as P

HEADS = 16
KV_HEADS = 8
HEAD_DIM = 64


EPSILON = 1e-05
THETA_BASE = 1000000.0
MASK_FILL = -1e30
HIGHEST = lax.Precision.HIGHEST


def rms_apply(values, gain_vec):
    factor = lax.rsqrt(jnp.mean(values * values, axis=-1, keepdims=True) + EPSILON)
    return (values * factor * gain_vec, factor)


def rms_back(values, factor, gain_vec, upstream):
    normal = values * factor
    weighted = upstream * gain_vec
    shared = jnp.mean(weighted * normal, axis=-1, keepdims=True)
    return (factor * (weighted - normal * shared), upstream * normal)


def rotary_tables(position):
    exponent = jnp.arange(HEAD_DIM // 2, dtype=jnp.float32) * (2.0 / HEAD_DIM)
    inverse = THETA_BASE ** (-exponent)
    angles = position.astype(jnp.float32)[:, None] * inverse[None, :]
    cosine = jnp.concatenate([jnp.cos(angles), jnp.cos(angles)], axis=-1)
    sine_tab = jnp.concatenate([jnp.sin(angles), jnp.sin(angles)], axis=-1)
    return (cosine, sine_tab)


def rotate(values, cosine, sine_tab):
    half_dim = values.shape[-1] // 2
    turned = jnp.concatenate([-values[..., half_dim:], values[..., :half_dim]], axis=-1)
    return values * cosine[:, None, :] + turned * sine_tab[:, None, :]


def rotate_back(upstream, cosine, sine_tab):
    half_dim = upstream.shape[-1] // 2
    scaled = upstream * sine_tab[:, None, :]
    turned = jnp.concatenate([scaled[..., half_dim:], -scaled[..., :half_dim]], axis=-1)
    return upstream * cosine[:, None, :] + turned


def contract_rows(left, right):
    return lax.dot_general(
        left, right, (((0,), (0,)), ((), ())), preferred_element_type=jnp.float32
    )


def contract_cols(left, right):
    return lax.dot_general(
        left, right, (((1,), (1,)), ((), ())), preferred_element_type=jnp.float32
    )


def general_body(
    tokens,
    lengths,
    query_weight,
    key_weight,
    value_weight,
    out_weight,
    gate_weight,
    up_weight,
    down_weight,
    attn_norm,
    query_norm,
    key_norm,
    ffn_norm,
    out_grad,
):
    tok_rows = tokens.shape[1]
    group_size = HEADS // KV_HEADS
    kv_width = KV_HEADS * HEAD_DIM
    score_scale = HEAD_DIM ** (-0.5)
    length = lengths[0]
    my_index = lax.axis_index("seq")
    position = my_index * tok_rows + jnp.arange(tok_rows, dtype=jnp.int32)
    row_valid = (position < length)[:, None]
    cosine, sine_tab = rotary_tables(position)
    inputs = tokens[0].astype(jnp.float32)
    query_full, key_full, value_full, out_full, gate_full, up_full, down_full = (
        lax.all_gather(query_weight, "seq", axis=0, tiled=True),
        lax.all_gather(key_weight, "seq", axis=0, tiled=True),
        lax.all_gather(value_weight, "seq", axis=0, tiled=True),
        lax.all_gather(out_weight, "seq", axis=0, tiled=True),
        lax.all_gather(gate_weight, "seq", axis=0, tiled=True),
        lax.all_gather(up_weight, "seq", axis=0, tiled=True),
        lax.all_gather(down_weight, "seq", axis=0, tiled=True),
    )
    normed_float, factor_one = rms_apply(inputs, attn_norm)
    normed = normed_float.astype(jnp.bfloat16)
    query_proj = jnp.dot(normed, query_full, preferred_element_type=jnp.float32).reshape(
        tok_rows, HEADS, HEAD_DIM
    )
    key_proj = jnp.dot(normed, key_full, preferred_element_type=jnp.float32).reshape(
        tok_rows, KV_HEADS, HEAD_DIM
    )
    value_low = jnp.dot(normed, value_full, preferred_element_type=jnp.float32).astype(jnp.bfloat16)
    query_unit, query_factor = rms_apply(query_proj, query_norm)
    key_unit, key_factor = rms_apply(key_proj, key_norm)
    query_low = (
        rotate(query_unit, cosine, sine_tab)
        .astype(jnp.bfloat16)
        .reshape(tok_rows, KV_HEADS, group_size, HEAD_DIM)
    )
    key_low = rotate(key_unit, cosine, sine_tab).astype(jnp.bfloat16).reshape(tok_rows, kv_width)

    def piece_scores(key_heads):
        key_count = key_heads.shape[0]
        scores = (
            jnp.einsum("tgrd,ngd->grtn", query_low, key_heads, preferred_element_type=jnp.float32)
            * score_scale
        )
        key_place = jnp.arange(key_count, dtype=jnp.int32)
        allowed = (key_place[None, :] <= position[:, None]) & (key_place[None, :] < length)
        return (scores, allowed)

    piece = (
        lax.all_gather(key_low, "seq", axis=0, tiled=True),
        lax.all_gather(value_low, "seq", axis=0, tiled=True),
    )
    forward_top_score = jnp.full((KV_HEADS, group_size, tok_rows), MASK_FILL, jnp.float32)
    key_heads = piece[0].reshape(-1, KV_HEADS, HEAD_DIM)
    value_heads = piece[1].reshape(-1, KV_HEADS, HEAD_DIM)
    scores, allowed = piece_scores(key_heads)
    masked = jnp.where(allowed, scores, MASK_FILL)
    new_top = jnp.maximum(forward_top_score, jnp.max(masked, axis=-1))
    weights = jnp.where(allowed, jnp.exp(masked - new_top[..., None]), 0.0)
    forward_weight_sum = jnp.sum(weights, axis=-1)
    added = jnp.einsum(
        "grtn,ngd->tgrd",
        weights.astype(jnp.bfloat16),
        value_heads,
        preferred_element_type=jnp.float32,
    )
    accum = added
    top_score, weight_sum, accum = (new_top, forward_weight_sum, accum)
    attn_heads = accum / jnp.transpose(weight_sum, (2, 0, 1))[..., None]
    attn_low = attn_heads.reshape(tok_rows, HEADS * HEAD_DIM).astype(jnp.bfloat16)
    residual = inputs + contract_cols(attn_low, out_full)
    normed_two_float, factor_two = rms_apply(residual, ffn_norm)
    normed_two = normed_two_float.astype(jnp.bfloat16)
    gate_val = jnp.dot(normed_two, gate_full, preferred_element_type=jnp.float32)
    up_val = jnp.dot(normed_two, up_full, preferred_element_type=jnp.float32)
    sigmoid_gate = jax.nn.sigmoid(gate_val)
    silu_gate = gate_val * sigmoid_gate
    hidden = (silu_gate * up_val).astype(jnp.bfloat16)
    result = residual + contract_cols(hidden, down_full)
    mixed = jnp.where(row_valid, result, 0.0).astype(jnp.bfloat16)[None]
    query_full, key_full, value_full, out_full, gate_full, up_full, down_full = (
        lax.all_gather(query_weight, "seq", axis=0, tiled=True),
        lax.all_gather(key_weight, "seq", axis=0, tiled=True),
        lax.all_gather(value_weight, "seq", axis=0, tiled=True),
        lax.all_gather(out_weight, "seq", axis=0, tiled=True),
        lax.all_gather(gate_weight, "seq", axis=0, tiled=True),
        lax.all_gather(up_weight, "seq", axis=0, tiled=True),
        lax.all_gather(down_weight, "seq", axis=0, tiled=True),
    )
    upstream = jnp.where(row_valid, out_grad[0].astype(jnp.float32), 0.0)
    branch_grad = upstream.astype(jnp.bfloat16)
    hidden_grad = jnp.dot(branch_grad, down_full, preferred_element_type=jnp.float32)
    down_w_grad = contract_rows(branch_grad, hidden)
    gate_grad_low = (
        hidden_grad * up_val * sigmoid_gate * (1.0 + gate_val * (1.0 - sigmoid_gate))
    ).astype(jnp.bfloat16)
    up_grad_low = (hidden_grad * silu_gate).astype(jnp.bfloat16)
    normed_two_grad = contract_cols(gate_grad_low, gate_full) + contract_cols(up_grad_low, up_full)
    gate_w_grad = contract_rows(normed_two, gate_grad_low)
    up_w_grad = contract_rows(normed_two, up_grad_low)
    residual_part, ffn_terms = rms_back(residual, factor_two, ffn_norm, normed_two_grad)
    residual_grad = upstream + residual_part
    attn_out_low = residual_grad.astype(jnp.bfloat16)
    out_w_grad = contract_rows(attn_out_low, attn_low)
    attn_grad_low = jnp.dot(attn_out_low, out_full, preferred_element_type=jnp.float32).astype(
        jnp.bfloat16
    )
    attn_grad_heads = attn_grad_low.reshape(tok_rows, KV_HEADS, group_size, HEAD_DIM)
    row_inner = jnp.transpose(
        jnp.sum(attn_grad_heads.astype(jnp.float32) * attn_heads, axis=-1), (1, 2, 0)
    )
    scaled_grad = (
        attn_grad_heads.astype(jnp.float32) / jnp.transpose(weight_sum, (2, 0, 1))[..., None]
    )
    piece = (
        lax.all_gather(key_low, "seq", axis=0, tiled=True),
        lax.all_gather(value_low, "seq", axis=0, tiled=True),
    )
    key_heads = piece[0].reshape(-1, KV_HEADS, HEAD_DIM)
    value_heads = piece[1].reshape(-1, KV_HEADS, HEAD_DIM)
    key_count = key_heads.shape[0]
    scores, allowed = piece_scores(key_heads)
    shifted = jnp.where(allowed, scores - top_score[..., None], MASK_FILL)
    exp_vals = jnp.where(allowed, jnp.exp(shifted), 0.0)
    probs = exp_vals / weight_sum[..., None]
    prob_grad = jnp.einsum(
        "tgrd,ngd->grtn", attn_grad_heads, value_heads, preferred_element_type=jnp.float32
    )
    score_grad = (probs * (prob_grad - row_inner[..., None])).astype(jnp.bfloat16)
    backward_query_acc = (
        jnp.einsum("grtn,ngd->tgrd", score_grad, key_heads, preferred_element_type=jnp.float32)
        * score_scale
    )
    key_part = (
        jnp.einsum("grtn,tgrd->ngd", score_grad, query_low, preferred_element_type=jnp.float32)
        * score_scale
    )
    exp_low = exp_vals.astype(jnp.bfloat16).astype(jnp.float32)
    value_part = jnp.einsum(
        "grtn,tgrd->ngd",
        exp_low,
        scaled_grad,
        precision=HIGHEST,
        preferred_element_type=jnp.float32,
    )
    update = jnp.concatenate(
        [key_part.reshape(key_count, kv_width), value_part.reshape(key_count, kv_width)], axis=1
    )
    query_acc, update = (backward_query_acc, update)
    key_buffer = update
    query_acc, key_buffer = (query_acc, key_buffer)
    key_value_grad = lax.psum_scatter(key_buffer, "seq", scatter_dimension=0, tiled=True)
    key_rot_grad = key_value_grad[:, :kv_width].reshape(tok_rows, KV_HEADS, HEAD_DIM)
    value_grad_low = key_value_grad[:, kv_width:].astype(jnp.bfloat16)
    query_rot_grad = query_acc.reshape(tok_rows, HEADS, HEAD_DIM)
    query_proj_grad, query_terms = rms_back(
        query_proj, query_factor, query_norm, rotate_back(query_rot_grad, cosine, sine_tab)
    )
    key_proj_grad, key_terms = rms_back(
        key_proj, key_factor, key_norm, rotate_back(key_rot_grad, cosine, sine_tab)
    )
    query_grad_low = query_proj_grad.reshape(tok_rows, HEADS * HEAD_DIM).astype(jnp.bfloat16)
    key_grad_low = key_proj_grad.reshape(tok_rows, kv_width).astype(jnp.bfloat16)
    normed_grad = (
        contract_cols(query_grad_low, query_full)
        + contract_cols(key_grad_low, key_full)
        + contract_cols(value_grad_low, value_full)
    )
    query_w_grad = contract_rows(normed, query_grad_low)
    key_w_grad = contract_rows(normed, key_grad_low)
    value_w_grad = contract_rows(normed, value_grad_low)
    input_part, attn_terms = rms_back(inputs, factor_one, attn_norm, normed_grad)
    input_grad = (residual_grad + input_part).astype(jnp.bfloat16)[None]
    attn_gain_grad, query_gain_grad, key_gain_grad, ffn_gain_grad = lax.psum(
        (
            jnp.sum(attn_terms, axis=0),
            jnp.sum(query_terms, axis=(0, 1)),
            jnp.sum(key_terms, axis=(0, 1)),
            jnp.sum(ffn_terms, axis=0),
        ),
        ("seq", "slot"),
    )
    query_share, key_share, value_share, out_share, gate_share, up_share, down_share = (
        lax.psum_scatter(query_w_grad, "seq", scatter_dimension=0, tiled=True),
        lax.psum_scatter(key_w_grad, "seq", scatter_dimension=0, tiled=True),
        lax.psum_scatter(value_w_grad, "seq", scatter_dimension=0, tiled=True),
        lax.psum_scatter(out_w_grad, "seq", scatter_dimension=0, tiled=True),
        lax.psum_scatter(gate_w_grad, "seq", scatter_dimension=0, tiled=True),
        lax.psum_scatter(up_w_grad, "seq", scatter_dimension=0, tiled=True),
        lax.psum_scatter(down_w_grad, "seq", scatter_dimension=0, tiled=True),
    )
    query_share, key_share, value_share, out_share, gate_share, up_share, down_share = (
        lax.psum(query_share.astype(jnp.bfloat16), "slot").astype(jnp.float32),
        lax.psum(key_share.astype(jnp.bfloat16), "slot").astype(jnp.float32),
        lax.psum(value_share.astype(jnp.bfloat16), "slot").astype(jnp.float32),
        lax.psum(out_share.astype(jnp.bfloat16), "slot").astype(jnp.float32),
        lax.psum(gate_share.astype(jnp.bfloat16), "slot").astype(jnp.float32),
        lax.psum(up_share.astype(jnp.bfloat16), "slot").astype(jnp.float32),
        lax.psum(down_share.astype(jnp.bfloat16), "slot").astype(jnp.float32),
    )
    return (
        mixed,
        input_grad,
        query_share,
        key_share,
        value_share,
        out_share,
        gate_share,
        up_share,
        down_share,
        attn_gain_grad,
        query_gain_grad,
        key_gain_grad,
        ffn_gain_grad,
    )


SLOTS_BY_HEADS = 4
LANES = 2 * HEAD_DIM
ROW_BLOCK = 256
VMEM_LIMIT = 60 * 1024 * 1024


def dot_nn(left, right):
    return lax.dot_general(left, right, (((1,), (0,)), ((), ())), preferred_element_type=jnp.float32)


def dot_nt(left, right):
    return lax.dot_general(left, right, (((1,), (1,)), ((), ())), preferred_element_type=jnp.float32)


def dot_tn(left, right):
    return lax.dot_general(left, right, (((0,), (0,)), ((), ())), preferred_element_type=jnp.float32)


def lane_is_low(shape):
    return lax.broadcasted_iota(jnp.int32, shape, len(shape) - 1) < HEAD_DIM


def pair_mean(values):
    low = lane_is_low(values.shape)
    first = jnp.sum(jnp.where(low, values, 0.0), axis=-1, keepdims=True)
    second = jnp.sum(jnp.where(low, 0.0, values), axis=-1, keepdims=True)
    return jnp.where(low, first, second) * (1.0 / HEAD_DIM)


def pair_turn(values, cosine, sine_signed):
    lane = lax.broadcasted_iota(jnp.int32, values.shape, 1)
    near = lax.rem(lane, HEAD_DIM) < HEAD_DIM // 2
    half = HEAD_DIM // 2
    turned = jnp.where(near, pltpu.roll(values, LANES - half, 1), pltpu.roll(values, half, 1))
    return values * cosine + turned * sine_signed


def pair_swap(values):
    return pltpu.roll(values.astype(jnp.float32), HEAD_DIM, 1)


def array(kind, *shape):
    return jax.ShapeDtypeStruct(shape, kind)


def call(kernel, out_shape, scratch_shapes=(), token=False):
    vmem, anywhere = pl.BlockSpec(memory_space=pltpu.VMEM), pl.BlockSpec(memory_space=pl.ANY)
    single = not isinstance(out_shape, tuple)
    shapes = ((out_shape,) if single else out_shape) + ((array(jnp.float32, 8, LANES),) if token else ())

    def apply(*operands, smem=0, tokens=()):
        given = len(operands)
        results = given + len(tokens) + len(shapes)

        def whole(*refs):
            if token:
                refs[results - 1][...] = jnp.zeros((8, LANES), jnp.float32)
            kernel(*refs[:given], *refs[given + len(tokens) : results - token], *refs[results:])

        in_specs = [pl.BlockSpec(memory_space=pltpu.SMEM)] * smem + [vmem] * (given - smem) + [anywhere] * len(tokens)
        outputs = pl.pallas_call(
            whole,
            out_shape=shapes,
            in_specs=in_specs,
            out_specs=(vmem,) * len(shapes),
            scratch_shapes=scratch_shapes,
            compiler_params=pltpu.CompilerParams(vmem_limit_bytes=VMEM_LIMIT),
        )(*operands, *tokens)
        return outputs[0] if len(shapes) == 1 else outputs

    return apply


def moving(kernel, out_shape, scratch_shapes, copies, token=False):
    anywhere = pl.BlockSpec(memory_space=pl.ANY)
    shapes = tuple(out_shape) + ((array(jnp.float32, 8, LANES),) if token else ())
    specs = (anywhere,) * len(out_shape) + ((pl.BlockSpec(memory_space=pltpu.VMEM),) if token else ())

    def apply(*operands, smem=0, tokens=()):
        given = len(operands)
        results = given + len(tokens) + len(shapes)

        def body(*refs):
            if token:
                refs[results - 1][...] = jnp.zeros((8, LANES), jnp.float32)
            kernel(*refs[:given], *refs[given + len(tokens) : results - token], *refs[results:])

        outputs = pl.pallas_call(
            body,
            out_shape=shapes,
            in_specs=[pl.BlockSpec(memory_space=pltpu.SMEM)] * smem + [anywhere] * (given - smem + len(tokens)),
            out_specs=specs,
            scratch_shapes=[*scratch_shapes, pltpu.SemaphoreType.DMA((copies,))],
            compiler_params=pltpu.CompilerParams(vmem_limit_bytes=VMEM_LIMIT),
        )(*operands, *tokens)
        return outputs[0] if len(shapes) == 1 else outputs

    return apply


class Copies:
    def __init__(self, sems):
        self.sems, self.used, self.open = sems, 0, []

    def start(self, source, target):
        copy = pltpu.make_async_copy(source, target, self.sems.at[self.used])
        self.used += 1
        copy.start()
        return copy

    def store(self, source, target):
        self.open.append(self.start(source, target))

    def finish(self):
        for copy in self.open:
            copy.wait()


def after(values, *tokens):
    count = len(values)
    anywhere = pl.BlockSpec(memory_space=pl.ANY)
    return pl.pallas_call(
        lambda *refs: None,
        out_shape=tuple(array(value.dtype, *value.shape) for value in values),
        in_specs=[anywhere] * (count + len(tokens)),
        out_specs=(anywhere,) * count,
        input_output_aliases={i: i for i in range(count)},
    )(*values, *tokens)


def block_rows(me_ref, partner, rows):
    return pl.ds(pl.multiple_of(jnp.bitwise_xor(me_ref[0], partner) * rows, rows), rows)


def store_pair(me_ref, chip, values, own_ref, other_ref):
    rows = values.shape[0] // 2
    first = jnp.bitwise_and(me_ref[0], 1) == 0
    own_ref[chip] = jnp.where(first, values[:rows], values[rows:]).astype(jnp.bfloat16)
    other_ref[chip] = jnp.where(first, values[rows:], values[:rows]).astype(jnp.bfloat16)


def pack_attention_kernel(query_ref, key_ref, value_ref, owned_ref):
    for index in range(0, KV_HEADS, 2):
        lanes = pl.ds(index * HEAD_DIM, LANES)
        key, value = key_ref[:, lanes], value_ref[:, lanes]
        low = lane_is_low(key.shape)
        key, value = key.astype(jnp.float32), value.astype(jnp.float32)
        pairs = (jnp.where(low, key, pair_swap(value)), jnp.where(low, pair_swap(key), value))
        for step in range(2):
            owned_ref[index + step, :, :LANES] = query_ref[:, pl.ds((index + step) * LANES, LANES)]
            owned_ref[index + step, :, LANES:] = pairs[step].astype(jnp.bfloat16)


def pack_units_kernel(slot_ref, gate_ref, up_ref, down_ref, first_ref, second_ref):
    rows = first_ref.shape[1]
    block = second_ref.shape[2] // 3
    cut = block * KV_HEADS
    half = pl.ds(pl.multiple_of(jnp.bitwise_and(slot_ref[0], 1) * rows, rows), rows)
    for index in range(KV_HEADS):
        for place, ref in enumerate((gate_ref, up_ref, down_ref)):
            start = place * block + (LANES if place == 2 else 0)
            first_ref[index, :, start : start + block] = ref[half, pl.ds(index * block, block)]
            second_ref[index, :, place * block : (place + 1) * block] = ref[:, pl.ds(cut + index * block, block)]
    for index in range(0, KV_HEADS, 2):
        lanes = pl.ds(2 * cut + index * HEAD_DIM, LANES)
        gate, up, down = (ref[half, lanes].astype(jnp.float32) for ref in (gate_ref, up_ref, down_ref))
        low = lane_is_low(gate.shape)
        rests = (jnp.where(low, gate, pair_swap(up)), jnp.where(low, pair_swap(gate), up))
        downs = (jnp.where(low, down, pair_swap(down)), jnp.where(low, pair_swap(down), down))
        for step in range(2):
            first_ref[index + step, :, 2 * block : 2 * block + LANES] = rests[step].astype(jnp.bfloat16)
            first_ref[index + step, :, 3 * block + LANES :] = downs[step].astype(jnp.bfloat16)


def attention_forward_kernel(length_ref, me_ref, *refs):
    x_refs = refs[:KV_HEADS]
    (
        weight_ref, gain_ref, q_gain_ref, k_gain_ref, cos_ref, sin_ref,
        x_all_ref, normed_ref, q_proj_ref, kv_proj_ref, q_low_ref, k_pair_ref, v_pair_ref, attn_ref, attn_low_ref, weight_inv_ref,
    ) = refs[KV_HEADS:]
    tok_rows = x_refs[0].shape[0]
    total = tok_rows * KV_HEADS
    length = length_ref[0]
    low = lane_is_low((ROW_BLOCK, LANES))
    for partner in range(KV_HEADS):
        x_all_ref[block_rows(me_ref, partner, tok_rows), :] = x_refs[partner][...]
    for start in range(0, total, ROW_BLOCK):
        rows = pl.ds(start, ROW_BLOCK)
        x = x_all_ref[rows, :].astype(jnp.float32)
        factor = lax.rsqrt(jnp.mean(x * x, axis=-1, keepdims=True) + EPSILON)
        normed = (x * factor * gain_ref[...]).astype(jnp.bfloat16)
        normed_ref[rows, :] = normed
        proj = dot_nn(normed, weight_ref[...])
        q_proj = proj[:, :LANES]
        kv_proj = proj[:, LANES:]
        q_proj_ref[rows, :] = q_proj
        kv_proj_ref[rows, :] = kv_proj
        cosine, sine = cos_ref[rows, :], sin_ref[rows, :]
        q_factor = lax.rsqrt(pair_mean(q_proj * q_proj) + EPSILON)
        q_low_ref[rows, :] = pair_turn(q_proj * q_factor * q_gain_ref[...], cosine, sine).astype(jnp.bfloat16)
        k_factor = jnp.where(low, lax.rsqrt(pair_mean(kv_proj * kv_proj) + EPSILON), 1.0)
        kv = pair_turn(
            kv_proj * k_factor * k_gain_ref[...], jnp.where(low, cosine, 1.0), jnp.where(low, sine, 0.0)
        )
        swapped = pltpu.roll(kv, HEAD_DIM, 1)
        k_pair_ref[rows, :] = jnp.where(low, kv, swapped).astype(jnp.bfloat16)
        v_pair_ref[rows, :] = jnp.where(low, swapped, kv).astype(jnp.bfloat16)

    scale = HEAD_DIM ** (-0.5)
    for start in range(0, total, ROW_BLOCK):
        rows = pl.ds(start, ROW_BLOCK)
        q = q_low_ref[rows, :] * scale
        zero = jnp.zeros_like(q)
        heads = (jnp.where(low, q, zero), jnp.where(low, zero, q))
        results = []
        for q_head in heads:
            weight_sum = jnp.zeros((ROW_BLOCK, 1), jnp.float32)
            summed = jnp.zeros((ROW_BLOCK, LANES), jnp.float32)
            if start > 0:
                past = pl.ds(0, start)
                exp_vals = jnp.exp(dot_nt(q_head, k_pair_ref[past, :]))
                weight_sum += jnp.sum(exp_vals, axis=-1, keepdims=True)
                summed += dot_nn(exp_vals.astype(jnp.bfloat16), v_pair_ref[past, :])
            scores = dot_nt(q_head, k_pair_ref[rows, :])
            query = lax.broadcasted_iota(jnp.int32, scores.shape, 0)
            key = lax.broadcasted_iota(jnp.int32, scores.shape, 1)
            allowed = (key <= query) & (key + start < length)
            exp_vals = jnp.where(allowed, jnp.exp(scores), 0.0)
            weight_sum += jnp.sum(exp_vals, axis=-1, keepdims=True)
            summed += dot_nn(exp_vals.astype(jnp.bfloat16), v_pair_ref[rows, :])
            inverse = 1.0 / weight_sum
            results.append((summed * inverse, inverse))
        attn = jnp.where(low, results[0][0], results[1][0])
        attn_ref[rows, :] = attn
        attn_low_ref[rows, :] = attn.astype(jnp.bfloat16)
        weight_inv_ref[rows, :] = jnp.where(low, results[0][1], results[1][1])


def attention_backward_kernel(
    length_ref, me_ref, dattn_ref, weight_ref, q_gain_ref, k_gain_ref, cos_ref, sin_ref,
    q_proj_ref, kv_proj_ref, q_low_ref, k_pair_ref, v_pair_ref, attn_ref, weight_inv_ref,
    dnormed_own_ref, dnormed_other_ref, dproj_ref, terms_ref, dq_acc, dk_acc, dv_acc,
):
    total = dattn_ref.shape[0]
    length = length_ref[0]
    low = lane_is_low((ROW_BLOCK, LANES))
    scale = HEAD_DIM ** (-0.5)
    dk_acc[...] = jnp.zeros_like(dk_acc)
    dv_acc[...] = jnp.zeros_like(dv_acc)
    for start in range(0, total, ROW_BLOCK):
        rows = pl.ds(start, ROW_BLOCK)
        q = q_low_ref[rows, :] * scale
        dattn = dattn_ref[rows, :]
        zero = jnp.zeros_like(q)
        inner = dattn.astype(jnp.float32) * attn_ref[rows, :]
        inverses = weight_inv_ref[rows, :]
        dq_heads = []
        for head in range(2):
            mine = low if head == 0 else jnp.logical_not(low)
            q_head = jnp.where(mine, q, zero)
            dattn_head = jnp.where(mine, dattn, zero)
            delta = jnp.sum(jnp.where(mine, inner, 0.0), axis=-1, keepdims=True)
            inverse = inverses[:, head * HEAD_DIM : head * HEAD_DIM + 1]
            dq = jnp.zeros((ROW_BLOCK, LANES), jnp.float32)
            spans = ([(0, start)] if start > 0 else []) + [(start, ROW_BLOCK)]
            for key_start, key_count in spans:
                keys = pl.ds(key_start, key_count)
                k_pair = k_pair_ref[keys, :]
                probs = jnp.exp(dot_nt(q_head, k_pair)) * inverse
                if key_start == start:
                    query = lax.broadcasted_iota(jnp.int32, probs.shape, 0)
                    key = lax.broadcasted_iota(jnp.int32, probs.shape, 1)
                    allowed = (key <= query) & (key + start < length)
                    probs = jnp.where(allowed, probs, 0.0)
                dprobs = dot_nt(dattn_head, v_pair_ref[keys, :])
                dscores = (probs * (dprobs - delta)).astype(jnp.bfloat16)
                dq += dot_nn(dscores, k_pair)
                dk_acc[keys, :] += dot_tn(dscores, q_head)
                dv_acc[keys, :] += dot_tn(probs.astype(jnp.bfloat16), dattn_head)
            dq_heads.append(dq)
        dq_acc[rows, :] = jnp.where(low, dq_heads[0], dq_heads[1]) * scale

    q_terms = jnp.zeros((1, LANES), jnp.float32)
    k_terms = jnp.zeros((1, LANES), jnp.float32)
    for start in range(0, total, ROW_BLOCK):
        rows = pl.ds(start, ROW_BLOCK)
        cosine, sine = cos_ref[rows, :], sin_ref[rows, :]
        q_proj = q_proj_ref[rows, :]
        upstream = pair_turn(dq_acc[rows, :], cosine, -sine)
        factor = lax.rsqrt(pair_mean(q_proj * q_proj) + EPSILON)
        normal = q_proj * factor
        weighted = upstream * q_gain_ref[...]
        dq_proj = factor * (weighted - normal * pair_mean(weighted * normal))
        q_terms += jnp.sum(upstream * normal, axis=0, keepdims=True)

        dk = dk_acc[rows, :]
        dv = dv_acc[rows, :]
        dk = dk + pltpu.roll(dk, HEAD_DIM, 1)
        dv = dv + pltpu.roll(dv, HEAD_DIM, 1)
        kv_proj = kv_proj_ref[rows, :]
        upstream = pair_turn(jnp.where(low, dk, 0.0), jnp.where(low, cosine, 1.0), jnp.where(low, -sine, 0.0))
        factor = lax.rsqrt(pair_mean(kv_proj * kv_proj) + EPSILON)
        normal = kv_proj * factor
        weighted = upstream * k_gain_ref[...]
        dk_proj = factor * (weighted - normal * pair_mean(weighted * normal))
        k_terms += jnp.sum(upstream * normal, axis=0, keepdims=True)
        dkv_proj = jnp.where(low, dk_proj, dv)
        dproj = jnp.concatenate([dq_proj, dkv_proj], axis=1).astype(jnp.bfloat16)
        dproj_ref[rows, :] = dproj
        store_pair(me_ref, start // ROW_BLOCK, dot_nt(dproj, weight_ref[...]), dnormed_own_ref, dnormed_other_ref)
    terms_ref[0:1, :] = q_terms
    terms_ref[1:2, :] = k_terms


def residual_kernel(me_ref, x_ref, *refs):
    attn_refs = refs[:KV_HEADS]
    out_weight_ref, gain_ref, residual_ref, normed_ref, attn_scratch, scratch = refs[KV_HEADS:]
    total, width = x_ref.shape
    tok_rows = total // KV_HEADS
    for partner in range(KV_HEADS):
        attn_scratch[:, block_rows(me_ref, partner, LANES)] = attn_refs[partner][...]
    for start in range(0, total, ROW_BLOCK):
        rows = pl.ds(start, ROW_BLOCK)
        residual = x_ref[rows, :].astype(jnp.float32) + dot_nt(attn_scratch[rows, :], out_weight_ref[...])
        scratch[rows, :] = residual
        factor = lax.rsqrt(jnp.mean(residual * residual, axis=-1, keepdims=True) + EPSILON)
        normed_ref[rows, :] = (residual * factor * gain_ref[...]).astype(jnp.bfloat16)
    residual_ref[...] = scratch[block_rows(me_ref, 0, tok_rows), :]


def unit_share(gate, up, upstream):
    sigmoid = jax.nn.sigmoid(gate)
    silu = gate * sigmoid
    dgate = upstream * up * sigmoid * (1.0 + gate * (1.0 - sigmoid))
    return silu * up, dgate, upstream * silu


def first_units_kernel(me_ref, slot_ref, normed_ref, *refs):
    dout_refs, refs = refs[:KV_HEADS], refs[KV_HEADS:]
    halves, outs, refs = refs[:2], refs[2:7], refs[7:]
    dout_out, weight_out, hidden_out, dgate_out, grads_out = outs
    normed, dout, weight, hidden, dgate, grads, sems = refs
    copies = Copies(sems)
    total, width = normed.shape
    half = halves[0].shape[1]
    slots, _, rows_each, _ = grads.shape
    owners = ROW_BLOCK // (slots * rows_each)
    block = hidden.shape[1] - LANES
    units = dgate.shape[1]
    odd = jnp.bitwise_and(slot_ref[0], 1)
    starts = range(0, total, ROW_BLOCK)
    loads = []
    for index in range(KV_HEADS):
        for place, ref in ((odd, halves[0]), (1 - odd, halves[1])):
            rows = pl.ds(pl.multiple_of((2 * index + place) * half, half), half)
            loads.append(copies.start(ref.at[index], weight.at[rows, :]))
    normed_loads = [copies.start(normed_ref.at[pl.ds(start, ROW_BLOCK), :], normed.at[pl.ds(start, ROW_BLOCK), :]) for start in starts]
    dout_loads = [
        copies.start(dout_refs[partner], dout.at[block_rows(me_ref, partner, 2 * half), :]) for partner in range(KV_HEADS)
    ]
    for load in loads:
        load.wait()
    copies.store(weight, weight_out)
    low = lane_is_low((ROW_BLOCK, LANES))
    for step, start in enumerate(starts):
        rows = pl.ds(start, ROW_BLOCK)
        normed_loads[step].wait()
        both = dot_nn(normed[rows, :], weight[:, :units])
        if step == 0:
            for load in dout_loads:
                load.wait()
            copies.store(dout, dout_out)
        dhidden = dot_nn(dout[rows, :], weight[:, units:])
        share = unit_share(both[:, :block], both[:, block : 2 * block], dhidden[:, :block])
        rest = both[:, 2 * block :]
        swapped = pltpu.roll(rest, HEAD_DIM, 1)
        rest_share = unit_share(jnp.where(low, rest, swapped), jnp.where(low, swapped, rest), dhidden[:, block:])
        hidden[rows, :block] = share[0].astype(jnp.bfloat16)
        hidden[rows, block:] = jnp.where(low, rest_share[0], 0.0).astype(jnp.bfloat16)
        dgate[rows, :block] = share[1].astype(jnp.bfloat16)
        dgate[rows, block : 2 * block] = share[2].astype(jnp.bfloat16)
        dgate[rows, 2 * block :] = jnp.where(low, rest_share[1], rest_share[2]).astype(jnp.bfloat16)
    copies.store(hidden, hidden_out)
    copies.store(dgate, dgate_out)
    for step, start in enumerate(range(0, width, ROW_BLOCK)):
        lanes = pl.ds(start, ROW_BLOCK)
        gate_up = dot_tn(normed[:, lanes], dgate[...]).astype(jnp.bfloat16)
        down = dot_tn(dout[:, lanes], hidden[...])[:, : block + HEAD_DIM].astype(jnp.bfloat16)
        for owner in range(owners):
            for slot in range(slots):
                piece = (owner * slots + slot) * rows_each
                grads[slot, step * owners + owner, :, :units] = gate_up[piece : piece + rows_each]
                grads[slot, step * owners + owner, :, units:] = down[piece : piece + rows_each]
        done = pl.ds(step * owners, owners)
        copies.store(grads.at[:, done], grads_out.at[:, done])
    copies.finish()


def second_units_kernel(
    me_ref, normed_ref, dout_ref, first_ref, second_ref, dgate_up_first_ref, hidden_ref, dgate_up_ref, own_ref, other_ref
):
    total = normed_ref.shape[0]
    block = hidden_ref.shape[1]
    units = dgate_up_first_ref.shape[1]
    for start in range(0, total, ROW_BLOCK):
        rows = pl.ds(start, ROW_BLOCK)
        both = dot_nn(normed_ref[rows, :], second_ref[:, : 2 * block])
        dhidden = dot_nn(dout_ref[rows, :], second_ref[:, 2 * block :])
        hidden, dgate, dup = unit_share(both[:, :block], both[:, block:], dhidden)
        hidden_ref[rows, :] = hidden.astype(jnp.bfloat16)
        dgate_up = jnp.concatenate([dgate, dup], axis=1).astype(jnp.bfloat16)
        dgate_up_ref[rows, :] = dgate_up
        dnormed = dot_nt(dgate_up, second_ref[:, : 2 * block]) + dot_nt(dgate_up_first_ref[rows, :], first_ref[:, :units])
        store_pair(me_ref, start // ROW_BLOCK, dnormed, own_ref, other_ref)


def unit_grads_kernel(normed_ref, dout_ref, hidden_ref, dgate_up_ref, grads_ref):
    slots, _, rows_each, cols = grads_ref.shape
    units = dgate_up_ref.shape[1]
    for start in range(0, normed_ref.shape[1], ROW_BLOCK):
        rows = pl.ds(start, ROW_BLOCK)
        gate_up = dot_tn(normed_ref[:, rows], dgate_up_ref[...]).astype(jnp.bfloat16)
        down = dot_tn(dout_ref[:, rows], hidden_ref[...])[:, : cols - units].astype(jnp.bfloat16)
        for piece in range(0, ROW_BLOCK, rows_each):
            owner, slot = divmod((start + piece) // rows_each, slots)
            grads_ref[slot, owner, :, :units] = gate_up[piece : piece + rows_each]
            grads_ref[slot, owner, :, units:] = down[piece : piece + rows_each]


def mixed_kernel(me_ref, hidden_first_ref, hidden_second_ref, first_ref, second_ref, own_ref, other_ref):
    total = hidden_first_ref.shape[0]
    block = hidden_second_ref.shape[1]
    units = 2 * block + LANES
    for start in range(0, total, ROW_BLOCK):
        rows = pl.ds(start, ROW_BLOCK)
        part = dot_nt(hidden_first_ref[rows, :], first_ref[:, units:]) + dot_nt(
            hidden_second_ref[rows, :], second_ref[:, 2 * block :]
        )
        store_pair(me_ref, start // ROW_BLOCK, part, own_ref, other_ref)


def add_kernel(me_ref, own_ref, other_ref, *part_refs):
    chip = lax.shift_right_logical(me_ref[0], 1)
    for i, part_ref in enumerate(part_refs):
        place = jnp.bitwise_xor(chip, i)
        part_ref[...] = (own_ref[place].astype(jnp.float32) + other_ref[place].astype(jnp.float32)).astype(jnp.bfloat16)


def add_blocks_kernel(own_ref, other_ref, sum_ref):
    sum_ref[...] = (own_ref[...].astype(jnp.float32) + other_ref[...].astype(jnp.float32)).astype(sum_ref.dtype)


def four_sum(parts):
    first, second, third, fourth = (part.astype(jnp.float32) for part in parts)
    return (first + second) + (third + fourth)


def join_kernel(left_ref, *refs):
    joined_ref = refs[4]
    split = left_ref.shape[2]
    joined_ref[:, :, :split] = left_ref[...]
    joined_ref[:, :, split:] = four_sum([ref[...] for ref in refs[:4]]).astype(joined_ref.dtype)


def residual_back_kernel(
    parts_ref, residual_ref, upstream_ref, gain_ref, out_weight_ref,
    residual_grad_ref, low_ref, dattn_ref, terms_ref,
):
    values = residual_ref[...]
    factor = lax.rsqrt(jnp.mean(values * values, axis=-1, keepdims=True) + EPSILON)
    part, terms = rms_back(values, factor, gain_ref[...], four_sum([parts_ref[i] for i in range(4)]))
    residual_grad = upstream_ref[...].astype(jnp.float32) + part
    residual_grad_ref[...] = residual_grad
    low = residual_grad.astype(jnp.bfloat16)
    low_ref[...] = low
    dattn = dot_nn(low, out_weight_ref[...]).astype(jnp.bfloat16)
    for index in range(KV_HEADS):
        dattn_ref[index] = dattn[:, index * LANES : (index + 1) * LANES]
    terms_ref[...] = jnp.sum(terms, axis=0, keepdims=True)


def input_back_kernel(
    part_a_ref, part_b_ref, part_c_ref, part_d_ref, tokens_ref, residual_grad_ref, gain_ref, input_grad_ref,
):
    values = tokens_ref[...].astype(jnp.float32)
    factor = lax.rsqrt(jnp.mean(values * values, axis=-1, keepdims=True) + EPSILON)
    part, _ = rms_back(values, factor, gain_ref[...], four_sum([ref[...] for ref in (part_a_ref, part_b_ref, part_c_ref, part_d_ref)]))
    input_grad_ref[...] = (residual_grad_ref[...] + part).astype(jnp.bfloat16)


def attention_gain_kernel(me_ref, x_ref, own_ref, other_ref, terms_ref):
    rows = own_ref.shape[1]
    core = jnp.bitwise_and(me_ref[0], 1)
    terms = jnp.zeros(terms_ref.shape, jnp.float32)
    for chip in range(own_ref.shape[0]):
        for place, ref in ((core, own_ref), (1 - core, other_ref)):
            x = x_ref[pl.ds(pl.multiple_of(chip * 2 * rows + place * rows, rows), rows), :].astype(jnp.float32)
            factor = lax.rsqrt(jnp.mean(x * x, axis=-1, keepdims=True) + EPSILON)
            terms += jnp.sum(ref[chip].astype(jnp.float32) * (x * factor), axis=0, keepdims=True)
    terms_ref[...] = terms


def attention_weights_kernel(me_ref, slot_ref, normed_ref, dproj_ref, attn_low_ref, *refs):
    dbranch_refs, quarters, grads, dbranch = refs[:KV_HEADS], refs[KV_HEADS:-2], refs[-2], refs[-1]
    slots, _, rows_each, _ = grads.shape
    tok_rows = dbranch_refs[0].shape[0]
    for partner in range(KV_HEADS):
        dbranch[block_rows(me_ref, partner, tok_rows), :] = dbranch_refs[partner][...]
    for start in range(0, normed_ref.shape[1], ROW_BLOCK):
        lanes = pl.ds(start, ROW_BLOCK)
        proj = dot_tn(normed_ref[:, lanes], dproj_ref[...]).astype(jnp.bfloat16)
        out = dot_tn(dbranch[:, lanes], attn_low_ref[...]).astype(jnp.bfloat16)
        for piece in range(0, ROW_BLOCK, rows_each):
            owner, slot = divmod((start + piece) // rows_each, slots)
            grads[slot, owner, :, : 2 * LANES] = proj[piece : piece + rows_each]
            grads[slot, owner, :, 2 * LANES :] = out[piece : piece + rows_each]
    for partner, quarter in enumerate(quarters):
        quarter[...] = grads[jnp.bitwise_xor(slot_ref[0], partner)]


def rows_kernel(first_ref, second_ref, *out_refs):
    query_ref, key_ref, value_ref, out_ref, gate_ref, up_ref, down_ref = out_refs
    f32 = jnp.float32
    block = (first_ref.shape[3] - LANES - HEAD_DIM) // 3
    cut = KV_HEADS * block
    heads = 3 * block
    rows_each = first_ref.shape[2]
    low = lane_is_low((rows_each, LANES))
    for slot in range(first_ref.shape[0]):
        rows = pl.ds(slot * rows_each, rows_each)
        for index in range(KV_HEADS):
            for place, ref in enumerate((gate_ref, up_ref, down_ref)):
                start = place * block + (LANES if place == 2 else 0)
                ref[rows, pl.ds(index * block, block)] = first_ref[slot, index, :, start : start + block].astype(f32)
                start = place * block
                ref[rows, pl.ds(cut + index * block, block)] = second_ref[slot, index, :, start : start + block].astype(f32)
            lanes = pl.ds(index * LANES, LANES)
            query_ref[rows, lanes] = second_ref[slot, index, :, heads : heads + LANES].astype(f32)
            out_ref[rows, lanes] = second_ref[slot, index, :, heads + 2 * LANES :].astype(f32)
        for index in range(0, KV_HEADS, 2):
            lanes = pl.ds(index * HEAD_DIM, LANES)
            even = second_ref[slot, index, :, heads + LANES : heads + 2 * LANES].astype(f32)
            odd = second_ref[slot, index + 1, :, heads + LANES : heads + 2 * LANES].astype(f32)
            key_ref[rows, lanes] = jnp.where(low, even, pair_swap(odd))
            value_ref[rows, lanes] = jnp.where(low, pair_swap(even), odd)
            lanes = pl.ds(2 * cut + index * HEAD_DIM, LANES)
            even = first_ref[slot, index, :, 2 * block : 2 * block + LANES].astype(f32)
            odd = first_ref[slot, index + 1, :, 2 * block : 2 * block + LANES].astype(f32)
            gate_ref[rows, lanes] = jnp.where(low, even, pair_swap(odd))
            up_ref[rows, lanes] = jnp.where(low, pair_swap(even), odd)
            even = first_ref[slot, index, :, 3 * block + LANES :].astype(f32)
            odd = first_ref[slot, index + 1, :, 3 * block + LANES :].astype(f32)
            down_ref[rows, lanes] = jnp.concatenate([even, odd], axis=1)


def rotary_pair_tables(total):
    half = HEAD_DIM // 2
    exponent = np.arange(half, dtype=np.float32) * np.float32(2.0 / HEAD_DIM)
    inverse = np.float32(THETA_BASE) ** (-exponent)
    angles = np.arange(total, dtype=np.float32)[:, None] * inverse[None, :]
    cosine, sine = np.cos(angles), np.sin(angles)
    return (
        jnp.asarray(np.concatenate([cosine] * 4, axis=1), jnp.float32),
        jnp.asarray(np.concatenate([-sine, sine, -sine, sine], axis=1), jnp.float32),
    )


def to_partner(block, partner):
    return lax.ppermute(block, "seq", [(i, i ^ partner) for i in range(KV_HEADS)])


def gather_chips(block):
    return [block] + [to_partner(block, partner) for partner in (2, 4, 6)]


def gather_cores(parts):
    return [part for pair in zip(parts, [to_partner(part, 1) for part in parts]) for part in pair]


def swap_chips(blocks):
    cores = [list(range(core, KV_HEADS, 2)) for core in range(2)]
    return lax.all_to_all(blocks, "seq", 0, 0, axis_index_groups=cores, tiled=True)


def sum_partners(me, own, other, *tokens):
    *parts, added = call(add_kernel, (array(own.dtype, *own.shape[1:]),) * own.shape[0], token=True)(
        me, own, to_partner(other, 1), smem=1, tokens=tokens
    )
    return [parts[0]] + [to_partner(parts[i], 2 * i) for i in (1, 2, 3)], added


def to_slot(block, partner):
    return lax.ppermute(block, "slot", [(i, i ^ partner) for i in range(SLOTS_BY_HEADS)])


def send_quarters(quarters):
    return [quarters[0]] + [to_slot(quarters[partner], partner) for partner in (1, 2, 3)]


def sum_devices(values):
    for partner in (1, 2, 4):
        values = values + to_partner(values, partner)
    return four_sum([values] + [to_slot(values, partner) for partner in (1, 2, 3)])


def heads_body(
    tokens, lengths, query_weight, key_weight, value_weight, out_weight, gate_weight, up_weight, down_weight,
    attn_norm, query_norm, key_norm, ffn_norm, out_grad,
):
    f32, bf16 = jnp.float32, jnp.bfloat16
    count = KV_HEADS
    tok_rows, width = tokens.shape[1:]
    depth = query_weight.shape[0]
    total = tok_rows * count
    units = gate_weight.shape[1] // count
    block = (units - HEAD_DIM) // 2
    length = lengths[0]
    index = lax.axis_index("seq")
    me = index[None]
    slot = lax.axis_index("slot")[None]
    position = index * tok_rows + jnp.arange(tok_rows, dtype=jnp.int32)
    row_valid = (position < length)[:, None]

    def swap(blocks):
        return lax.all_to_all(blocks, "seq", 0, 0, tiled=True)

    x_parts = gather_cores(gather_chips(tokens[0]))
    attn_owned, packed = call(pack_attention_kernel, array(bf16, count, depth, 2 * LANES), token=True)(
        query_weight, key_weight, value_weight
    )
    attn_weight = swap(attn_owned).reshape(width, 2 * LANES)
    first_owned, second_owned = call(
        pack_units_kernel,
        (array(bf16, count, depth // 2, 3 * block + 2 * LANES), array(bf16, count, depth, 3 * block)),
    )(slot, gate_weight, up_weight, down_weight, smem=1, tokens=(packed,))
    upstream = jnp.where(row_valid, out_grad[0], jnp.zeros_like(out_grad[0]))
    (first_owned,) = after((first_owned,), *x_parts, attn_weight)
    first_own = swap(first_owned)
    out_full = lax.all_gather(out_weight, "seq", axis=0, tiled=True)

    cosine, sine = rotary_pair_tables(total)
    q_gain = jnp.concatenate([query_norm, query_norm])[None]
    k_gain = jnp.concatenate([key_norm, jnp.ones_like(key_norm)])[None]
    x_all, normed, q_proj, kv_proj, q_low, k_pair, v_pair, attn, attn_low, weight_inv, attended = call(
        attention_forward_kernel,
        (
            array(bf16, total, width), array(bf16, total, width), array(f32, total, LANES), array(f32, total, LANES),
            array(bf16, total, LANES), array(bf16, total, LANES), array(bf16, total, LANES), array(f32, total, LANES),
            array(bf16, total, LANES), array(f32, total, LANES),
        ),
        token=True,
    )(lengths, me, *x_parts, attn_weight, attn_norm[None], q_gain, k_gain, cosine, sine, smem=2)

    attn_parts = gather_chips(attn_low)
    (second_owned,) = after((second_owned,), attended)
    second_weight = swap(second_owned).reshape(width, -1)
    first_own, upstream = after((first_own, upstream), *attn_parts[1:])
    first_other = to_slot(first_own, 1)
    dout_parts = gather_chips(upstream)
    attn_parts = gather_cores(attn_parts)
    residual, normed_two, normed_ready = call(
        residual_kernel,
        (array(f32, tok_rows, width), array(bf16, total, width)),
        scratch_shapes=[pltpu.VMEM((total, width), bf16), pltpu.VMEM((total, width), f32)],
        token=True,
    )(me, x_all, *attn_parts, out_full, ffn_norm[None], smem=1, tokens=(second_owned,))

    dout_parts = gather_cores(after(tuple(dout_parts), normed_ready, first_other))
    first_cols, second_cols = 3 * block + 2 * LANES, 3 * block
    units_first, units_second = 2 * block + LANES, 2 * block
    halves = (array(bf16, count // 2, tok_rows, width),) * 2
    quarter = depth // SLOTS_BY_HEADS
    first_arrays = (
        array(bf16, total, width), array(bf16, width, first_cols), array(bf16, total, block + LANES),
        array(bf16, total, units_first), array(bf16, SLOTS_BY_HEADS, count, quarter, first_cols - HEAD_DIM),
    )
    dout_all, first_weight, hidden_first, dgate_up_first, first_grads, first_done = moving(
        first_units_kernel,
        first_arrays,
        [pltpu.VMEM((total, width), bf16)] + [pltpu.VMEM(shape.shape, shape.dtype) for shape in first_arrays],
        64,
        token=True,
    )(me, slot, normed_two, *dout_parts, first_own, first_other, smem=2, tokens=(second_weight,))
    first_sums = lax.psum_scatter(
        first_grads.reshape(width, first_cols - HEAD_DIM), "slot", scatter_dimension=0, tiled=True
    )
    hidden_second, dgate_up_second, *normed_two_grad, summed = call(
        second_units_kernel,
        (array(bf16, total, block), array(bf16, total, units_second), *halves),
        token=True,
    )(
        me, normed_two, dout_all, first_weight, second_weight, dgate_up_first, smem=1,
        tokens=(first_done,),
    )

    def unit_grads(hidden, dgate_up, cols, *tokens):
        grads, done = call(unit_grads_kernel, array(bf16, SLOTS_BY_HEADS, count, depth // SLOTS_BY_HEADS, cols), token=True)(
            normed_two, dout_all, hidden, dgate_up, tokens=tokens
        )
        return done, lax.psum_scatter(grads.reshape(width, cols), "slot", scatter_dimension=0, tiled=True)

    def to_owners(sums):
        return swap(sums.reshape(count, -1, sums.shape[1]))

    normed_two_sum = call(add_blocks_kernel, halves[0])(
        normed_two_grad[0], to_partner(normed_two_grad[1], 1)
    )
    residual_grad, attn_out_low, dattn, ffn_terms, branched = call(
        residual_back_kernel,
        (
            array(f32, tok_rows, width), array(bf16, tok_rows, width), array(bf16, count, tok_rows, LANES),
            array(f32, 1, width),
        ),
        token=True,
    )(swap_chips(normed_two_sum), residual, upstream, ffn_norm[None], out_full)
    second_grads, second_sums = unit_grads(hidden_second, dgate_up_second, 3 * block, branched)
    dattn = swap(dattn)
    dbranch_parts = gather_chips(*after((attn_out_low,), dattn))
    dnormed_own, dnormed_other, dproj, terms, passed = call(
        attention_backward_kernel,
        (*halves, array(bf16, total, 2 * LANES), array(f32, 2, LANES)),
        scratch_shapes=[pltpu.VMEM((total, LANES), f32)] * 3,
        token=True,
    )(
        lengths, me, dattn.reshape(total, LANES), attn_weight, q_gain, k_gain, cosine, sine, q_proj, kv_proj, q_low, k_pair,
        v_pair, attn, weight_inv, smem=2, tokens=(second_grads,),
    )
    dbranch_parts = gather_cores(after(tuple(dbranch_parts), passed))
    *quarters, projected = call(
        attention_weights_kernel,
        (array(bf16, count, quarter, 3 * LANES),) * SLOTS_BY_HEADS,
        scratch_shapes=[pltpu.VMEM((SLOTS_BY_HEADS, count, quarter, 3 * LANES), bf16), pltpu.VMEM((total, width), bf16)],
        token=True,
    )(me, slot, normed, dproj, attn_low, *dbranch_parts, smem=2)
    attention_parts = send_quarters(quarters)
    (first_sums,) = after((first_sums,), projected)
    first_rows = to_owners(first_sums)
    first_all = lax.all_gather(first_rows, "slot", axis=0)

    dnormed_parts, added = sum_partners(me, dnormed_own, dnormed_other, first_rows)
    *mixed_halves, mixed_done = call(mixed_kernel, halves, token=True)(
        me, hidden_first, hidden_second, first_weight, second_weight, smem=1, tokens=(added,)
    )
    attn_terms, gained = call(attention_gain_kernel, array(f32, 1, width), token=True)(
        me, x_all, dnormed_own, dnormed_other, smem=1, tokens=(mixed_done,)
    )
    (second_sums,) = after((second_sums,), gained)
    joined = call(join_kernel, array(bf16, count, quarter, second_cols + 3 * LANES))(
        second_sums.reshape(count, quarter, second_cols), *attention_parts
    )
    second_all = lax.all_gather(swap(joined), "slot", axis=0)
    mixed_parts, _ = sum_partners(me, *mixed_halves, gained)
    input_grad = call(input_back_kernel, array(bf16, tok_rows, width))(
        *dnormed_parts, tokens[0], residual_grad, attn_norm[None]
    )
    result = residual + sum(part.astype(f32) for part in mixed_parts)
    mixed = jnp.where(row_valid, result, 0.0).astype(bf16)[None]
    shapes = (query_weight, key_weight, value_weight, out_weight, gate_weight, up_weight, down_weight)
    weight_grads = call(rows_kernel, tuple(array(f32, *weight.shape) for weight in shapes))(
        first_all, second_all
    )

    half = HEAD_DIM
    gains = jnp.concatenate([attn_terms[0], ffn_terms[0], terms[0, :half] + terms[0, half:], terms[1, :half]])
    gains = sum_devices(gains.reshape(-1, LANES)).reshape(-1)
    return (
        mixed, input_grad[None], *weight_grads, gains[:width], gains[2 * width : 2 * width + half],
        gains[2 * width + half :], gains[width : 2 * width],
    )


def solution(mesh):
    in_specs = (
        P("slot", "seq", None),
        P("slot"),
        P("seq", None),
        P("seq", None),
        P("seq", None),
        P("seq", None),
        P("seq", None),
        P("seq", None),
        P("seq", None),
        P(),
        P(),
        P(),
        P(),
        P("slot", "seq", None),
    )
    out_specs = (
        P("slot", "seq", None),
        P("slot", "seq", None),
        P("seq", None),
        P("seq", None),
        P("seq", None),
        P("seq", None),
        P("seq", None),
        P("seq", None),
        P("seq", None),
        P(),
        P(),
        P(),
        P(),
    )
    by_heads = mesh.shape["seq"] == KV_HEADS and mesh.shape["slot"] == SLOTS_BY_HEADS
    body = heads_body if by_heads else general_body
    return jax.shard_map(body, mesh=mesh, in_specs=in_specs, out_specs=out_specs, check_vma=False)
```

```python
import functools

import jax
import jax.numpy as jnp
import numpy as np
from jax import lax
from jax.experimental import pallas as pl
from jax.experimental.pallas import tpu as pltpu
from jax.sharding import PartitionSpec as P

HEADS = 16
KV_HEADS = 8
HEAD_DIM = 64


EPSILON = 1e-05
THETA_BASE = 1000000.0
MASK_FILL = -1e30
HIGHEST = lax.Precision.HIGHEST


def rms_apply(values, gain_vec):
    factor = lax.rsqrt(jnp.mean(values * values, axis=-1, keepdims=True) + EPSILON)
    return (values * factor * gain_vec, factor)


def rms_back(values, factor, gain_vec, upstream):
    normal = values * factor
    weighted = upstream * gain_vec
    shared = jnp.mean(weighted * normal, axis=-1, keepdims=True)
    return (factor * (weighted - normal * shared), upstream * normal)


def rotary_tables(position):
    exponent = jnp.arange(HEAD_DIM // 2, dtype=jnp.float32) * (2.0 / HEAD_DIM)
    inverse = THETA_BASE ** (-exponent)
    angles = position.astype(jnp.float32)[:, None] * inverse[None, :]
    cosine = jnp.concatenate([jnp.cos(angles), jnp.cos(angles)], axis=-1)
    sine_tab = jnp.concatenate([jnp.sin(angles), jnp.sin(angles)], axis=-1)
    return (cosine, sine_tab)


def rotate(values, cosine, sine_tab):
    half_dim = values.shape[-1] // 2
    turned = jnp.concatenate([-values[..., half_dim:], values[..., :half_dim]], axis=-1)
    return values * cosine[:, None, :] + turned * sine_tab[:, None, :]


def rotate_back(upstream, cosine, sine_tab):
    half_dim = upstream.shape[-1] // 2
    scaled = upstream * sine_tab[:, None, :]
    turned = jnp.concatenate([scaled[..., half_dim:], -scaled[..., :half_dim]], axis=-1)
    return upstream * cosine[:, None, :] + turned


def contract_rows(left, right):
    return lax.dot_general(
        left, right, (((0,), (0,)), ((), ())), preferred_element_type=jnp.float32
    )


def contract_cols(left, right):
    return lax.dot_general(
        left, right, (((1,), (1,)), ((), ())), preferred_element_type=jnp.float32
    )


def general_body(
    tokens,
    lengths,
    query_weight,
    key_weight,
    value_weight,
    out_weight,
    gate_weight,
    up_weight,
    down_weight,
    attn_norm,
    query_norm,
    key_norm,
    ffn_norm,
    out_grad,
):
    tok_rows = tokens.shape[1]
    group_size = HEADS // KV_HEADS
    kv_width = KV_HEADS * HEAD_DIM
    score_scale = HEAD_DIM ** (-0.5)
    length = lengths[0]
    my_index = lax.axis_index("seq")
    position = my_index * tok_rows + jnp.arange(tok_rows, dtype=jnp.int32)
    row_valid = (position < length)[:, None]
    cosine, sine_tab = rotary_tables(position)
    inputs = tokens[0].astype(jnp.float32)
    query_full, key_full, value_full, out_full, gate_full, up_full, down_full = (
        lax.all_gather(query_weight, "seq", axis=0, tiled=True),
        lax.all_gather(key_weight, "seq", axis=0, tiled=True),
        lax.all_gather(value_weight, "seq", axis=0, tiled=True),
        lax.all_gather(out_weight, "seq", axis=0, tiled=True),
        lax.all_gather(gate_weight, "seq", axis=0, tiled=True),
        lax.all_gather(up_weight, "seq", axis=0, tiled=True),
        lax.all_gather(down_weight, "seq", axis=0, tiled=True),
    )
    normed_float, factor_one = rms_apply(inputs, attn_norm)
    normed = normed_float.astype(jnp.bfloat16)
    query_proj = jnp.dot(normed, query_full, preferred_element_type=jnp.float32).reshape(
        tok_rows, HEADS, HEAD_DIM
    )
    key_proj = jnp.dot(normed, key_full, preferred_element_type=jnp.float32).reshape(
        tok_rows, KV_HEADS, HEAD_DIM
    )
    value_low = jnp.dot(normed, value_full, preferred_element_type=jnp.float32).astype(jnp.bfloat16)
    query_unit, query_factor = rms_apply(query_proj, query_norm)
    key_unit, key_factor = rms_apply(key_proj, key_norm)
    query_low = (
        rotate(query_unit, cosine, sine_tab)
        .astype(jnp.bfloat16)
        .reshape(tok_rows, KV_HEADS, group_size, HEAD_DIM)
    )
    key_low = rotate(key_unit, cosine, sine_tab).astype(jnp.bfloat16).reshape(tok_rows, kv_width)

    def piece_scores(key_heads):
        key_count = key_heads.shape[0]
        scores = (
            jnp.einsum("tgrd,ngd->grtn", query_low, key_heads, preferred_element_type=jnp.float32)
            * score_scale
        )
        key_place = jnp.arange(key_count, dtype=jnp.int32)
        allowed = (key_place[None, :] <= position[:, None]) & (key_place[None, :] < length)
        return (scores, allowed)

    piece = (
        lax.all_gather(key_low, "seq", axis=0, tiled=True),
        lax.all_gather(value_low, "seq", axis=0, tiled=True),
    )
    forward_top_score = jnp.full((KV_HEADS, group_size, tok_rows), MASK_FILL, jnp.float32)
    key_heads = piece[0].reshape(-1, KV_HEADS, HEAD_DIM)
    value_heads = piece[1].reshape(-1, KV_HEADS, HEAD_DIM)
    scores, allowed = piece_scores(key_heads)
    masked = jnp.where(allowed, scores, MASK_FILL)
    new_top = jnp.maximum(forward_top_score, jnp.max(masked, axis=-1))
    weights = jnp.where(allowed, jnp.exp(masked - new_top[..., None]), 0.0)
    forward_weight_sum = jnp.sum(weights, axis=-1)
    added = jnp.einsum(
        "grtn,ngd->tgrd",
        weights.astype(jnp.bfloat16),
        value_heads,
        preferred_element_type=jnp.float32,
    )
    accum = added
    top_score, weight_sum, accum = (new_top, forward_weight_sum, accum)
    attn_heads = accum / jnp.transpose(weight_sum, (2, 0, 1))[..., None]
    attn_low = attn_heads.reshape(tok_rows, HEADS * HEAD_DIM).astype(jnp.bfloat16)
    residual = inputs + contract_cols(attn_low, out_full)
    normed_two_float, factor_two = rms_apply(residual, ffn_norm)
    normed_two = normed_two_float.astype(jnp.bfloat16)
    gate_val = jnp.dot(normed_two, gate_full, preferred_element_type=jnp.float32)
    up_val = jnp.dot(normed_two, up_full, preferred_element_type=jnp.float32)
    sigmoid_gate = jax.nn.sigmoid(gate_val)
    silu_gate = gate_val * sigmoid_gate
    hidden = (silu_gate * up_val).astype(jnp.bfloat16)
    result = residual + contract_cols(hidden, down_full)
    mixed = jnp.where(row_valid, result, 0.0).astype(jnp.bfloat16)[None]
    query_full, key_full, value_full, out_full, gate_full, up_full, down_full = (
        lax.all_gather(query_weight, "seq", axis=0, tiled=True),
        lax.all_gather(key_weight, "seq", axis=0, tiled=True),
        lax.all_gather(value_weight, "seq", axis=0, tiled=True),
        lax.all_gather(out_weight, "seq", axis=0, tiled=True),
        lax.all_gather(gate_weight, "seq", axis=0, tiled=True),
        lax.all_gather(up_weight, "seq", axis=0, tiled=True),
        lax.all_gather(down_weight, "seq", axis=0, tiled=True),
    )
    upstream = jnp.where(row_valid, out_grad[0].astype(jnp.float32), 0.0)
    branch_grad = upstream.astype(jnp.bfloat16)
    hidden_grad = jnp.dot(branch_grad, down_full, preferred_element_type=jnp.float32)
    down_w_grad = contract_rows(branch_grad, hidden)
    gate_grad_low = (
        hidden_grad * up_val * sigmoid_gate * (1.0 + gate_val * (1.0 - sigmoid_gate))
    ).astype(jnp.bfloat16)
    up_grad_low = (hidden_grad * silu_gate).astype(jnp.bfloat16)
    normed_two_grad = contract_cols(gate_grad_low, gate_full) + contract_cols(up_grad_low, up_full)
    gate_w_grad = contract_rows(normed_two, gate_grad_low)
    up_w_grad = contract_rows(normed_two, up_grad_low)
    residual_part, ffn_terms = rms_back(residual, factor_two, ffn_norm, normed_two_grad)
    residual_grad = upstream + residual_part
    attn_out_low = residual_grad.astype(jnp.bfloat16)
    out_w_grad = contract_rows(attn_out_low, attn_low)
    attn_grad_low = jnp.dot(attn_out_low, out_full, preferred_element_type=jnp.float32).astype(
        jnp.bfloat16
    )
    attn_grad_heads = attn_grad_low.reshape(tok_rows, KV_HEADS, group_size, HEAD_DIM)
    row_inner = jnp.transpose(
        jnp.sum(attn_grad_heads.astype(jnp.float32) * attn_heads, axis=-1), (1, 2, 0)
    )
    scaled_grad = (
        attn_grad_heads.astype(jnp.float32) / jnp.transpose(weight_sum, (2, 0, 1))[..., None]
    )
    piece = (
        lax.all_gather(key_low, "seq", axis=0, tiled=True),
        lax.all_gather(value_low, "seq", axis=0, tiled=True),
    )
    key_heads = piece[0].reshape(-1, KV_HEADS, HEAD_DIM)
    value_heads = piece[1].reshape(-1, KV_HEADS, HEAD_DIM)
    key_count = key_heads.shape[0]
    scores, allowed = piece_scores(key_heads)
    shifted = jnp.where(allowed, scores - top_score[..., None], MASK_FILL)
    exp_vals = jnp.where(allowed, jnp.exp(shifted), 0.0)
    probs = exp_vals / weight_sum[..., None]
    prob_grad = jnp.einsum(
        "tgrd,ngd->grtn", attn_grad_heads, value_heads, preferred_element_type=jnp.float32
    )
    score_grad = (probs * (prob_grad - row_inner[..., None])).astype(jnp.bfloat16)
    backward_query_acc = (
        jnp.einsum("grtn,ngd->tgrd", score_grad, key_heads, preferred_element_type=jnp.float32)
        * score_scale
    )
    key_part = (
        jnp.einsum("grtn,tgrd->ngd", score_grad, query_low, preferred_element_type=jnp.float32)
        * score_scale
    )
    exp_low = exp_vals.astype(jnp.bfloat16).astype(jnp.float32)
    value_part = jnp.einsum(
        "grtn,tgrd->ngd",
        exp_low,
        scaled_grad,
        precision=HIGHEST,
        preferred_element_type=jnp.float32,
    )
    update = jnp.concatenate(
        [key_part.reshape(key_count, kv_width), value_part.reshape(key_count, kv_width)], axis=1
    )
    query_acc, update = (backward_query_acc, update)
    key_buffer = update
    query_acc, key_buffer = (query_acc, key_buffer)
    key_value_grad = lax.psum_scatter(key_buffer, "seq", scatter_dimension=0, tiled=True)
    key_rot_grad = key_value_grad[:, :kv_width].reshape(tok_rows, KV_HEADS, HEAD_DIM)
    value_grad_low = key_value_grad[:, kv_width:].astype(jnp.bfloat16)
    query_rot_grad = query_acc.reshape(tok_rows, HEADS, HEAD_DIM)
    query_proj_grad, query_terms = rms_back(
        query_proj, query_factor, query_norm, rotate_back(query_rot_grad, cosine, sine_tab)
    )
    key_proj_grad, key_terms = rms_back(
        key_proj, key_factor, key_norm, rotate_back(key_rot_grad, cosine, sine_tab)
    )
    query_grad_low = query_proj_grad.reshape(tok_rows, HEADS * HEAD_DIM).astype(jnp.bfloat16)
    key_grad_low = key_proj_grad.reshape(tok_rows, kv_width).astype(jnp.bfloat16)
    normed_grad = (
        contract_cols(query_grad_low, query_full)
        + contract_cols(key_grad_low, key_full)
        + contract_cols(value_grad_low, value_full)
    )
    query_w_grad = contract_rows(normed, query_grad_low)
    key_w_grad = contract_rows(normed, key_grad_low)
    value_w_grad = contract_rows(normed, value_grad_low)
    input_part, attn_terms = rms_back(inputs, factor_one, attn_norm, normed_grad)
    input_grad = (residual_grad + input_part).astype(jnp.bfloat16)[None]
    attn_gain_grad, query_gain_grad, key_gain_grad, ffn_gain_grad = lax.psum(
        (
            jnp.sum(attn_terms, axis=0),
            jnp.sum(query_terms, axis=(0, 1)),
            jnp.sum(key_terms, axis=(0, 1)),
            jnp.sum(ffn_terms, axis=0),
        ),
        ("seq", "slot"),
    )
    query_share, key_share, value_share, out_share, gate_share, up_share, down_share = (
        lax.psum_scatter(query_w_grad, "seq", scatter_dimension=0, tiled=True),
        lax.psum_scatter(key_w_grad, "seq", scatter_dimension=0, tiled=True),
        lax.psum_scatter(value_w_grad, "seq", scatter_dimension=0, tiled=True),
        lax.psum_scatter(out_w_grad, "seq", scatter_dimension=0, tiled=True),
        lax.psum_scatter(gate_w_grad, "seq", scatter_dimension=0, tiled=True),
        lax.psum_scatter(up_w_grad, "seq", scatter_dimension=0, tiled=True),
        lax.psum_scatter(down_w_grad, "seq", scatter_dimension=0, tiled=True),
    )
    query_share, key_share, value_share, out_share, gate_share, up_share, down_share = (
        lax.psum(query_share.astype(jnp.bfloat16), "slot").astype(jnp.float32),
        lax.psum(key_share.astype(jnp.bfloat16), "slot").astype(jnp.float32),
        lax.psum(value_share.astype(jnp.bfloat16), "slot").astype(jnp.float32),
        lax.psum(out_share.astype(jnp.bfloat16), "slot").astype(jnp.float32),
        lax.psum(gate_share.astype(jnp.bfloat16), "slot").astype(jnp.float32),
        lax.psum(up_share.astype(jnp.bfloat16), "slot").astype(jnp.float32),
        lax.psum(down_share.astype(jnp.bfloat16), "slot").astype(jnp.float32),
    )
    return (
        mixed,
        input_grad,
        query_share,
        key_share,
        value_share,
        out_share,
        gate_share,
        up_share,
        down_share,
        attn_gain_grad,
        query_gain_grad,
        key_gain_grad,
        ffn_gain_grad,
    )


SLOTS_BY_HEADS = 4
LANES = 2 * HEAD_DIM
ROW_BLOCK = 256
VMEM_LIMIT = 60 * 1024 * 1024


def dot_nn(left, right):
    return lax.dot_general(left, right, (((1,), (0,)), ((), ())), preferred_element_type=jnp.float32)


def dot_nt(left, right):
    return lax.dot_general(left, right, (((1,), (1,)), ((), ())), preferred_element_type=jnp.float32)


def dot_tn(left, right):
    return lax.dot_general(left, right, (((0,), (0,)), ((), ())), preferred_element_type=jnp.float32)


def lane_is_low(shape):
    return lax.broadcasted_iota(jnp.int32, shape, len(shape) - 1) < HEAD_DIM


def pair_mean(values):
    low = lane_is_low(values.shape)
    first = jnp.sum(jnp.where(low, values, 0.0), axis=-1, keepdims=True)
    second = jnp.sum(jnp.where(low, 0.0, values), axis=-1, keepdims=True)
    return jnp.where(low, first, second) * (1.0 / HEAD_DIM)


def pair_turn(values, cosine, sine_signed):
    lane = lax.broadcasted_iota(jnp.int32, values.shape, 1)
    near = lax.rem(lane, HEAD_DIM) < HEAD_DIM // 2
    half = HEAD_DIM // 2
    turned = jnp.where(near, pltpu.roll(values, LANES - half, 1), pltpu.roll(values, half, 1))
    return values * cosine + turned * sine_signed


def pair_swap(values):
    return pltpu.roll(values.astype(jnp.float32), HEAD_DIM, 1)


def array(kind, *shape):
    return jax.ShapeDtypeStruct(shape, kind)


def call(kernel, out_shape, scratch_shapes=(), token=False, late=0, kept=0):
    vmem, anywhere = pl.BlockSpec(memory_space=pltpu.VMEM), pl.BlockSpec(memory_space=pl.ANY)
    single = not isinstance(out_shape, tuple)
    shapes = ((out_shape,) if single else out_shape) + ((array(jnp.float32, 8, LANES),) if token else ())

    def apply(*operands, smem=0, tokens=()):
        given = len(operands)
        results = given + len(tokens) + len(shapes)

        def whole(*refs):
            if token:
                refs[results - 1][...] = jnp.zeros((8, LANES), jnp.float32)
            kernel(*refs[:given], *refs[given + len(tokens) : results - token], *refs[results:])

        in_specs = [pl.BlockSpec(memory_space=pltpu.SMEM)] * smem + [vmem] * (given - smem - late)
        outputs = pl.pallas_call(
            whole,
            out_shape=shapes,
            in_specs=in_specs + [anywhere] * (late + len(tokens)),
            out_specs=(vmem,) * (len(shapes) - kept - token) + (anywhere,) * kept + (vmem,) * token,
            scratch_shapes=scratch_shapes,
            compiler_params=pltpu.CompilerParams(vmem_limit_bytes=VMEM_LIMIT),
        )(*operands, *tokens)
        return outputs[0] if len(shapes) == 1 else outputs

    return apply


def moving(kernel, out_shape, scratch_shapes, copies, token=False):
    anywhere = pl.BlockSpec(memory_space=pl.ANY)
    shapes = tuple(out_shape) + ((array(jnp.float32, 8, LANES),) if token else ())
    specs = (anywhere,) * len(out_shape) + ((pl.BlockSpec(memory_space=pltpu.VMEM),) if token else ())

    def apply(*operands, smem=0, tokens=()):
        given = len(operands)
        results = given + len(tokens) + len(shapes)

        def body(*refs):
            if token:
                refs[results - 1][...] = jnp.zeros((8, LANES), jnp.float32)
            kernel(*refs[:given], *refs[given + len(tokens) : results - token], *refs[results:])

        outputs = pl.pallas_call(
            body,
            out_shape=shapes,
            in_specs=[pl.BlockSpec(memory_space=pltpu.SMEM)] * smem + [anywhere] * (given - smem + len(tokens)),
            out_specs=specs,
            scratch_shapes=[*scratch_shapes, pltpu.SemaphoreType.DMA((copies,))],
            compiler_params=pltpu.CompilerParams(vmem_limit_bytes=VMEM_LIMIT),
        )(*operands, *tokens)
        return outputs[0] if len(shapes) == 1 else outputs

    return apply


class Copies:
    def __init__(self, sems):
        self.sems, self.used, self.open = sems, 0, []

    def start(self, source, target):
        copy = pltpu.make_async_copy(source, target, self.sems.at[self.used])
        self.used += 1
        copy.start()
        return copy

    def store(self, source, target):
        self.open.append(self.start(source, target))

    def finish(self):
        for copy in self.open:
            copy.wait()


def write_columns(kernel, out_shape, stages, copies):
    vmem, anywhere = pl.BlockSpec(memory_space=pltpu.VMEM), pl.BlockSpec(memory_space=pl.ANY)

    def apply(part, *outputs):
        given = len(outputs)
        return pl.pallas_call(
            kernel,
            out_shape=out_shape,
            in_specs=[vmem] + [anywhere] * given,
            out_specs=(anywhere,) * len(out_shape),
            scratch_shapes=[*stages, pltpu.SemaphoreType.DMA((copies,))],
            input_output_aliases={1 + i: i for i in range(given)},
            compiler_params=pltpu.CompilerParams(vmem_limit_bytes=VMEM_LIMIT),
        )(part, *outputs)

    return apply


def after(values, *tokens):
    count = len(values)
    anywhere = pl.BlockSpec(memory_space=pl.ANY)
    return pl.pallas_call(
        lambda *refs: None,
        out_shape=tuple(array(value.dtype, *value.shape) for value in values),
        in_specs=[anywhere] * (count + len(tokens)),
        out_specs=(anywhere,) * count,
        input_output_aliases={i: i for i in range(count)},
    )(*values, *tokens)


def block_rows(me_ref, partner, rows):
    return pl.ds(pl.multiple_of(jnp.bitwise_xor(me_ref[0], partner) * rows, rows), rows)


def store_pair(me_ref, chip, values, own_ref, other_ref):
    rows = values.shape[0] // 2
    first = jnp.bitwise_and(me_ref[0], 1) == 0
    own_ref[chip] = jnp.where(first, values[:rows], values[rows:]).astype(jnp.bfloat16)
    other_ref[chip] = jnp.where(first, values[rows:], values[:rows]).astype(jnp.bfloat16)


def pack_attention_kernel(query_ref, key_ref, value_ref, owned_ref):
    for index in range(0, KV_HEADS, 2):
        lanes = pl.ds(index * HEAD_DIM, LANES)
        key, value = key_ref[:, lanes], value_ref[:, lanes]
        low = lane_is_low(key.shape)
        key, value = key.astype(jnp.float32), value.astype(jnp.float32)
        pairs = (jnp.where(low, key, pair_swap(value)), jnp.where(low, pair_swap(key), value))
        for step in range(2):
            owned_ref[index + step, :, :LANES] = query_ref[:, pl.ds((index + step) * LANES, LANES)]
            owned_ref[index + step, :, LANES:] = pairs[step].astype(jnp.bfloat16)


def pack_units_kernel(slot_ref, gate_ref, up_ref, down_ref, first_ref, second_ref):
    rows = first_ref.shape[1]
    block = second_ref.shape[2] // 3
    cut = block * KV_HEADS
    half = pl.ds(pl.multiple_of(jnp.bitwise_and(slot_ref[0], 1) * rows, rows), rows)
    for index in range(KV_HEADS):
        for place, ref in enumerate((gate_ref, up_ref, down_ref)):
            start = place * block + (LANES if place == 2 else 0)
            first_ref[index, :, start : start + block] = ref[half, pl.ds(index * block, block)]
            second_ref[index, :, place * block : (place + 1) * block] = ref[:, pl.ds(cut + index * block, block)]
    for index in range(0, KV_HEADS, 2):
        lanes = pl.ds(2 * cut + index * HEAD_DIM, LANES)
        gate, up, down = (ref[half, lanes].astype(jnp.float32) for ref in (gate_ref, up_ref, down_ref))
        low = lane_is_low(gate.shape)
        rests = (jnp.where(low, gate, pair_swap(up)), jnp.where(low, pair_swap(gate), up))
        downs = (jnp.where(low, down, pair_swap(down)), jnp.where(low, pair_swap(down), down))
        for step in range(2):
            first_ref[index + step, :, 2 * block : 2 * block + LANES] = rests[step].astype(jnp.bfloat16)
            first_ref[index + step, :, 3 * block + LANES :] = downs[step].astype(jnp.bfloat16)


def attention_forward_kernel(length_ref, me_ref, *refs):
    x_refs = refs[:KV_HEADS]
    (
        weight_ref, gain_ref, q_gain_ref, k_gain_ref, cos_ref, sin_ref,
        x_all_ref, normed_ref, q_proj_ref, kv_proj_ref, q_low_ref, k_pair_ref, v_pair_ref, attn_ref, attn_low_ref, weight_inv_ref,
    ) = refs[KV_HEADS:]
    tok_rows = x_refs[0].shape[0]
    total = tok_rows * KV_HEADS
    length = length_ref[0]
    low = lane_is_low((ROW_BLOCK, LANES))
    for partner in range(KV_HEADS):
        x_all_ref[block_rows(me_ref, partner, tok_rows), :] = x_refs[partner][...]
    for start in range(0, total, ROW_BLOCK):
        rows = pl.ds(start, ROW_BLOCK)
        x = x_all_ref[rows, :].astype(jnp.float32)
        factor = lax.rsqrt(jnp.mean(x * x, axis=-1, keepdims=True) + EPSILON)
        normed = (x * factor * gain_ref[...]).astype(jnp.bfloat16)
        normed_ref[rows, :] = normed
        proj = dot_nn(normed, weight_ref[...])
        q_proj = proj[:, :LANES]
        kv_proj = proj[:, LANES:]
        q_proj_ref[rows, :] = q_proj
        kv_proj_ref[rows, :] = kv_proj
        cosine, sine = cos_ref[rows, :], sin_ref[rows, :]
        q_factor = lax.rsqrt(pair_mean(q_proj * q_proj) + EPSILON)
        q_low_ref[rows, :] = pair_turn(q_proj * q_factor * q_gain_ref[...], cosine, sine).astype(jnp.bfloat16)
        k_factor = jnp.where(low, lax.rsqrt(pair_mean(kv_proj * kv_proj) + EPSILON), 1.0)
        kv = pair_turn(
            kv_proj * k_factor * k_gain_ref[...], jnp.where(low, cosine, 1.0), jnp.where(low, sine, 0.0)
        )
        swapped = pltpu.roll(kv, HEAD_DIM, 1)
        k_pair_ref[rows, :] = jnp.where(low, kv, swapped).astype(jnp.bfloat16)
        v_pair_ref[rows, :] = jnp.where(low, swapped, kv).astype(jnp.bfloat16)

    scale = HEAD_DIM ** (-0.5)
    for start in range(0, total, ROW_BLOCK):
        rows = pl.ds(start, ROW_BLOCK)
        q = q_low_ref[rows, :] * scale
        zero = jnp.zeros_like(q)
        heads = (jnp.where(low, q, zero), jnp.where(low, zero, q))
        results = []
        for q_head in heads:
            weight_sum = jnp.zeros((ROW_BLOCK, 1), jnp.float32)
            summed = jnp.zeros((ROW_BLOCK, LANES), jnp.float32)
            if start > 0:
                past = pl.ds(0, start)
                exp_vals = jnp.exp(dot_nt(q_head, k_pair_ref[past, :]))
                weight_sum += jnp.sum(exp_vals, axis=-1, keepdims=True)
                summed += dot_nn(exp_vals.astype(jnp.bfloat16), v_pair_ref[past, :])
            scores = dot_nt(q_head, k_pair_ref[rows, :])
            query = lax.broadcasted_iota(jnp.int32, scores.shape, 0)
            key = lax.broadcasted_iota(jnp.int32, scores.shape, 1)
            allowed = (key <= query) & (key + start < length)
            exp_vals = jnp.where(allowed, jnp.exp(scores), 0.0)
            weight_sum += jnp.sum(exp_vals, axis=-1, keepdims=True)
            summed += dot_nn(exp_vals.astype(jnp.bfloat16), v_pair_ref[rows, :])
            inverse = 1.0 / weight_sum
            results.append((summed * inverse, inverse))
        attn = jnp.where(low, results[0][0], results[1][0])
        attn_ref[rows, :] = attn
        attn_low_ref[rows, :] = attn.astype(jnp.bfloat16)
        weight_inv_ref[rows, :] = jnp.where(low, results[0][1], results[1][1])


def quarter_rows(slot_ref, left_ref, right, grads, quarters):
    slots, _, rows_each, _ = grads.shape
    for start in range(0, left_ref.shape[1], ROW_BLOCK):
        product = dot_tn(left_ref[:, pl.ds(start, ROW_BLOCK)], right).astype(jnp.bfloat16)
        for piece in range(0, ROW_BLOCK, rows_each):
            owner, slot = divmod((start + piece) // rows_each, slots)
            grads[slot, owner] = product[piece : piece + rows_each]
    for partner, quarter in enumerate(quarters):
        quarter[...] = grads[jnp.bitwise_xor(slot_ref[0], partner)]


def attention_backward_kernel(
    length_ref, me_ref, slot_ref, dattn_ref, q_gain_ref, k_gain_ref, q_low_ref, k_pair_ref, v_pair_ref, attn_ref, weight_inv_ref,
    *refs,
):
    late_refs, terms_ref, quarters, (dnormed_own_out, dnormed_other_out) = refs[:6], refs[6], refs[7:11], refs[11:13]
    dq_acc, dk_acc, dv_acc, dnormed_own_ref, dnormed_other_ref, dproj_ref, grads = refs[13:20]
    held, sems = refs[20:26], refs[26]
    weight_ref, cos_ref, sin_ref, q_proj_ref, kv_proj_ref, normed_ref = held
    copies = Copies(sems)
    loads = [copies.start(late, target) for late, target in zip(late_refs, held)]
    total = dattn_ref.shape[0]
    length = length_ref[0]
    low = lane_is_low((ROW_BLOCK, LANES))
    scale = HEAD_DIM ** (-0.5)
    dk_acc[...] = jnp.zeros_like(dk_acc)
    dv_acc[...] = jnp.zeros_like(dv_acc)
    for start in range(0, total, ROW_BLOCK):
        rows = pl.ds(start, ROW_BLOCK)
        q = q_low_ref[rows, :] * scale
        dattn = dattn_ref[rows, :]
        zero = jnp.zeros_like(q)
        inner = dattn.astype(jnp.float32) * attn_ref[rows, :]
        inverses = weight_inv_ref[rows, :]
        dq_heads = []
        for head in range(2):
            mine = low if head == 0 else jnp.logical_not(low)
            q_head = jnp.where(mine, q, zero)
            dattn_head = jnp.where(mine, dattn, zero)
            delta = jnp.sum(jnp.where(mine, inner, 0.0), axis=-1, keepdims=True)
            inverse = inverses[:, head * HEAD_DIM : head * HEAD_DIM + 1]
            dq = jnp.zeros((ROW_BLOCK, LANES), jnp.float32)
            spans = ([(0, start)] if start > 0 else []) + [(start, ROW_BLOCK)]
            for key_start, key_count in spans:
                keys = pl.ds(key_start, key_count)
                k_pair = k_pair_ref[keys, :]
                probs = jnp.exp(dot_nt(q_head, k_pair)) * inverse
                if key_start == start:
                    query = lax.broadcasted_iota(jnp.int32, probs.shape, 0)
                    key = lax.broadcasted_iota(jnp.int32, probs.shape, 1)
                    allowed = (key <= query) & (key + start < length)
                    probs = jnp.where(allowed, probs, 0.0)
                dprobs = dot_nt(dattn_head, v_pair_ref[keys, :])
                dscores = (probs * (dprobs - delta)).astype(jnp.bfloat16)
                dq += dot_nn(dscores, k_pair)
                dk_acc[keys, :] += dot_tn(dscores, q_head)
                dv_acc[keys, :] += dot_tn(probs.astype(jnp.bfloat16), dattn_head)
            dq_heads.append(dq)
        dq_acc[rows, :] = jnp.where(low, dq_heads[0], dq_heads[1]) * scale

    for load in loads[:5]:
        load.wait()
    q_terms = jnp.zeros((1, LANES), jnp.float32)
    k_terms = jnp.zeros((1, LANES), jnp.float32)
    for start in range(0, total, ROW_BLOCK):
        rows = pl.ds(start, ROW_BLOCK)
        cosine, sine = cos_ref[rows, :], sin_ref[rows, :]
        q_proj = q_proj_ref[rows, :]
        upstream = pair_turn(dq_acc[rows, :], cosine, -sine)
        factor = lax.rsqrt(pair_mean(q_proj * q_proj) + EPSILON)
        normal = q_proj * factor
        weighted = upstream * q_gain_ref[...]
        dq_proj = factor * (weighted - normal * pair_mean(weighted * normal))
        q_terms += jnp.sum(upstream * normal, axis=0, keepdims=True)

        dk = dk_acc[rows, :]
        dv = dv_acc[rows, :]
        dk = dk + pltpu.roll(dk, HEAD_DIM, 1)
        dv = dv + pltpu.roll(dv, HEAD_DIM, 1)
        kv_proj = kv_proj_ref[rows, :]
        upstream = pair_turn(jnp.where(low, dk, 0.0), jnp.where(low, cosine, 1.0), jnp.where(low, -sine, 0.0))
        factor = lax.rsqrt(pair_mean(kv_proj * kv_proj) + EPSILON)
        normal = kv_proj * factor
        weighted = upstream * k_gain_ref[...]
        dk_proj = factor * (weighted - normal * pair_mean(weighted * normal))
        k_terms += jnp.sum(upstream * normal, axis=0, keepdims=True)
        dkv_proj = jnp.where(low, dk_proj, dv)
        dproj = jnp.concatenate([dq_proj, dkv_proj], axis=1).astype(jnp.bfloat16)
        dproj_ref[rows, :] = dproj
        chip = start // ROW_BLOCK
        store_pair(me_ref, chip, dot_nt(dproj, weight_ref[...]), dnormed_own_ref, dnormed_other_ref)
        copies.store(dnormed_own_ref.at[chip], dnormed_own_out.at[chip])
        copies.store(dnormed_other_ref.at[chip], dnormed_other_out.at[chip])
    terms_ref[0:1, :] = q_terms
    terms_ref[1:2, :] = k_terms
    loads[5].wait()
    quarter_rows(slot_ref, normed_ref, dproj_ref[...], grads, quarters)
    copies.finish()


def residual_kernel(me_ref, x_ref, *refs):
    attn_refs = refs[:KV_HEADS]
    out_weight_ref, gain_ref, residual_ref, normed_ref, attn_scratch, scratch = refs[KV_HEADS:]
    total, width = x_ref.shape
    tok_rows = total // KV_HEADS
    for partner in range(KV_HEADS):
        attn_scratch[:, block_rows(me_ref, partner, LANES)] = attn_refs[partner][...]
    for start in range(0, total, ROW_BLOCK):
        rows = pl.ds(start, ROW_BLOCK)
        residual = x_ref[rows, :].astype(jnp.float32) + dot_nt(attn_scratch[rows, :], out_weight_ref[...])
        scratch[rows, :] = residual
        factor = lax.rsqrt(jnp.mean(residual * residual, axis=-1, keepdims=True) + EPSILON)
        normed_ref[rows, :] = (residual * factor * gain_ref[...]).astype(jnp.bfloat16)
    residual_ref[...] = scratch[block_rows(me_ref, 0, tok_rows), :]


def unit_share(gate, up, upstream):
    sigmoid = jax.nn.sigmoid(gate)
    silu = gate * sigmoid
    dgate = upstream * up * sigmoid * (1.0 + gate * (1.0 - sigmoid))
    return silu * up, dgate, upstream * silu


def first_units_kernel(me_ref, slot_ref, normed_ref, *refs):
    dout_refs, refs = refs[:KV_HEADS], refs[KV_HEADS:]
    halves, outs, refs = refs[:2], refs[2:7], refs[7:]
    dout_out, weight_out, hidden_out, dgate_out, grads_out = outs
    normed, dout, weight, hidden, dgate, grads, sems = refs
    copies = Copies(sems)
    total, width = normed.shape
    half = halves[0].shape[1]
    slots, _, rows_each, _ = grads.shape
    owners = ROW_BLOCK // (slots * rows_each)
    block = hidden.shape[1] - LANES
    units = dgate.shape[1]
    odd = jnp.bitwise_and(slot_ref[0], 1)
    starts = range(0, total, ROW_BLOCK)
    loads = []
    for index in range(KV_HEADS):
        for place, ref in ((odd, halves[0]), (1 - odd, halves[1])):
            rows = pl.ds(pl.multiple_of((2 * index + place) * half, half), half)
            loads.append(copies.start(ref.at[index], weight.at[rows, :]))
    normed_loads = [copies.start(normed_ref.at[pl.ds(start, ROW_BLOCK), :], normed.at[pl.ds(start, ROW_BLOCK), :]) for start in starts]
    dout_loads = [
        copies.start(dout_refs[partner], dout.at[block_rows(me_ref, partner, 2 * half), :]) for partner in range(KV_HEADS)
    ]
    for load in loads:
        load.wait()
    copies.store(weight, weight_out)
    low = lane_is_low((ROW_BLOCK, LANES))
    for step, start in enumerate(starts):
        rows = pl.ds(start, ROW_BLOCK)
        normed_loads[step].wait()
        both = dot_nn(normed[rows, :], weight[:, :units])
        if step == 0:
            for load in dout_loads:
                load.wait()
            copies.store(dout, dout_out)
        dhidden = dot_nn(dout[rows, :], weight[:, units:])
        share = unit_share(both[:, :block], both[:, block : 2 * block], dhidden[:, :block])
        rest = both[:, 2 * block :]
        swapped = pltpu.roll(rest, HEAD_DIM, 1)
        rest_share = unit_share(jnp.where(low, rest, swapped), jnp.where(low, swapped, rest), dhidden[:, block:])
        hidden[rows, :block] = share[0].astype(jnp.bfloat16)
        hidden[rows, block:] = jnp.where(low, rest_share[0], 0.0).astype(jnp.bfloat16)
        dgate[rows, :block] = share[1].astype(jnp.bfloat16)
        dgate[rows, block : 2 * block] = share[2].astype(jnp.bfloat16)
        dgate[rows, 2 * block :] = jnp.where(low, rest_share[1], rest_share[2]).astype(jnp.bfloat16)
    copies.store(hidden, hidden_out)
    copies.store(dgate, dgate_out)
    for step, start in enumerate(range(0, width, ROW_BLOCK)):
        lanes = pl.ds(start, ROW_BLOCK)
        gate_up = dot_tn(normed[:, lanes], dgate[...]).astype(jnp.bfloat16)
        down = dot_tn(dout[:, lanes], hidden[...])[:, : block + HEAD_DIM].astype(jnp.bfloat16)
        for owner in range(owners):
            for slot in range(slots):
                piece = (owner * slots + slot) * rows_each
                grads[slot, step * owners + owner, :, :units] = gate_up[piece : piece + rows_each]
                grads[slot, step * owners + owner, :, units:] = down[piece : piece + rows_each]
        done = pl.ds(step * owners, owners)
        copies.store(grads.at[:, done], grads_out.at[:, done])
    copies.finish()


def second_units_kernel(
    me_ref, normed_ref, dout_ref, first_ref, second_ref, dgate_up_first_ref, hidden_ref, dgate_up_ref, own_ref, other_ref
):
    total = normed_ref.shape[0]
    block = hidden_ref.shape[1]
    units = dgate_up_first_ref.shape[1]
    for start in range(0, total, ROW_BLOCK):
        rows = pl.ds(start, ROW_BLOCK)
        both = dot_nn(normed_ref[rows, :], second_ref[:, : 2 * block])
        dhidden = dot_nn(dout_ref[rows, :], second_ref[:, 2 * block :])
        hidden, dgate, dup = unit_share(both[:, :block], both[:, block:], dhidden)
        hidden_ref[rows, :] = hidden.astype(jnp.bfloat16)
        dgate_up = jnp.concatenate([dgate, dup], axis=1).astype(jnp.bfloat16)
        dgate_up_ref[rows, :] = dgate_up
        dnormed = dot_nt(dgate_up, second_ref[:, : 2 * block]) + dot_nt(dgate_up_first_ref[rows, :], first_ref[:, :units])
        store_pair(me_ref, start // ROW_BLOCK, dnormed, own_ref, other_ref)


def unit_grads_kernel(normed_ref, dout_ref, hidden_ref, dgate_up_ref, grads_ref):
    slots, _, rows_each, cols = grads_ref.shape
    units = dgate_up_ref.shape[1]
    for start in range(0, normed_ref.shape[1], ROW_BLOCK):
        rows = pl.ds(start, ROW_BLOCK)
        gate_up = dot_tn(normed_ref[:, rows], dgate_up_ref[...]).astype(jnp.bfloat16)
        down = dot_tn(dout_ref[:, rows], hidden_ref[...])[:, : cols - units].astype(jnp.bfloat16)
        for piece in range(0, ROW_BLOCK, rows_each):
            owner, slot = divmod((start + piece) // rows_each, slots)
            grads_ref[slot, owner, :, :units] = gate_up[piece : piece + rows_each]
            grads_ref[slot, owner, :, units:] = down[piece : piece + rows_each]


def mixed_kernel(me_ref, hidden_first_ref, hidden_second_ref, first_ref, second_ref, own_ref, other_ref):
    total = hidden_first_ref.shape[0]
    block = hidden_second_ref.shape[1]
    units = 2 * block + LANES
    for start in range(0, total, ROW_BLOCK):
        rows = pl.ds(start, ROW_BLOCK)
        part = dot_nt(hidden_first_ref[rows, :], first_ref[:, units:]) + dot_nt(
            hidden_second_ref[rows, :], second_ref[:, 2 * block :]
        )
        store_pair(me_ref, start // ROW_BLOCK, part, own_ref, other_ref)


def add_kernel(me_ref, own_ref, other_ref, *part_refs):
    chip = lax.shift_right_logical(me_ref[0], 1)
    for i, part_ref in enumerate(part_refs):
        place = jnp.bitwise_xor(chip, i)
        part_ref[...] = (own_ref[place].astype(jnp.float32) + other_ref[place].astype(jnp.float32)).astype(jnp.bfloat16)


def add_blocks_kernel(own_ref, other_ref, sum_ref):
    sum_ref[...] = (own_ref[...].astype(jnp.float32) + other_ref[...].astype(jnp.float32)).astype(sum_ref.dtype)


def four_sum(parts):
    first, second, third, fourth = (part.astype(jnp.float32) for part in parts)
    return (first + second) + (third + fourth)


def tile_rows_kernel(head_ref, sums_ref, joined_ref):
    count, rows, cols = sums_ref.shape
    start = head_ref.shape[1]
    joined_ref[:, :start, :] = head_ref[...]
    for tile in range(0, cols, LANES):
        size = min(LANES, cols - tile)
        joined_ref[:, start : start + rows, :size] = sums_ref[:, :, tile : tile + size]
        if size < LANES:
            joined_ref[:, start : start + rows, size:] = jnp.zeros((count, rows, LANES - size), joined_ref.dtype)
        start += rows


def join_kernel(left_ref, *refs):
    joined_ref = refs[8]
    joined_ref[:, :, : left_ref.shape[2]] = left_ref[...]
    place = left_ref.shape[2]
    for parts in (refs[:4], refs[4:8]):
        cols = parts[0].shape[2]
        joined_ref[:, :, place : place + cols] = four_sum([ref[...] for ref in parts]).astype(joined_ref.dtype)
        place += cols


def residual_back_kernel(
    parts_ref, residual_ref, upstream_ref, gain_ref, out_weight_ref,
    residual_grad_ref, low_ref, dattn_ref, terms_ref,
):
    values = residual_ref[...]
    factor = lax.rsqrt(jnp.mean(values * values, axis=-1, keepdims=True) + EPSILON)
    part, terms = rms_back(values, factor, gain_ref[...], four_sum([parts_ref[i] for i in range(4)]))
    residual_grad = upstream_ref[...].astype(jnp.float32) + part
    residual_grad_ref[...] = residual_grad
    low = residual_grad.astype(jnp.bfloat16)
    low_ref[...] = low
    dattn = dot_nn(low, out_weight_ref[...]).astype(jnp.bfloat16)
    for index in range(KV_HEADS):
        dattn_ref[index] = dattn[:, index * LANES : (index + 1) * LANES]
    terms_ref[...] = jnp.sum(terms, axis=0, keepdims=True)


def input_back_kernel(
    part_a_ref, part_b_ref, part_c_ref, part_d_ref, tokens_ref, residual_grad_ref, gain_ref, input_grad_ref,
):
    values = tokens_ref[...].astype(jnp.float32)
    factor = lax.rsqrt(jnp.mean(values * values, axis=-1, keepdims=True) + EPSILON)
    part, _ = rms_back(values, factor, gain_ref[...], four_sum([ref[...] for ref in (part_a_ref, part_b_ref, part_c_ref, part_d_ref)]))
    input_grad_ref[...] = (residual_grad_ref[...] + part).astype(jnp.bfloat16)


def attention_gain_kernel(me_ref, x_ref, own_ref, other_ref, terms_ref):
    rows = own_ref.shape[1]
    core = jnp.bitwise_and(me_ref[0], 1)
    terms = jnp.zeros(terms_ref.shape, jnp.float32)
    for chip in range(own_ref.shape[0]):
        for place, ref in ((core, own_ref), (1 - core, other_ref)):
            x = x_ref[pl.ds(pl.multiple_of(chip * 2 * rows + place * rows, rows), rows), :].astype(jnp.float32)
            factor = lax.rsqrt(jnp.mean(x * x, axis=-1, keepdims=True) + EPSILON)
            terms += jnp.sum(ref[chip].astype(jnp.float32) * (x * factor), axis=0, keepdims=True)
    terms_ref[...] = terms


def out_grads_kernel(me_ref, slot_ref, attn_low_ref, *refs):
    dbranch_refs, quarters, grads, dbranch = refs[:KV_HEADS], refs[KV_HEADS:-2], refs[-2], refs[-1]
    tok_rows = dbranch_refs[0].shape[0]
    for partner in range(KV_HEADS):
        dbranch[block_rows(me_ref, partner, tok_rows), :] = dbranch_refs[partner][...]
    quarter_rows(slot_ref, dbranch, attn_low_ref[...], grads, quarters)


def first_rows_kernel(first_ref, *refs):
    out_refs, stages, rest_stages, sems = refs[:3], refs[3:6], refs[6:9], refs[9]
    copies = Copies(sems)
    f32 = jnp.float32
    block = stages[0].shape[1] // KV_HEADS
    cut = KV_HEADS * block
    rows_each = out_refs[0].shape[0] // first_ref.shape[0]
    low = lane_is_low((rows_each, LANES))

    def tile(slot, index, place):
        return first_ref[slot, index, place * rows_each : (place + 1) * rows_each, :].astype(f32)

    tiles = block // LANES
    for slot in range(first_ref.shape[0]):
        rows = pl.ds(slot * rows_each, rows_each)
        for index in range(KV_HEADS):
            for place, stage in enumerate(stages):
                for step in range(tiles):
                    source = place * tiles + step + (1 if place == 2 else 0)
                    stage[rows, pl.ds(index * block + step * LANES, LANES)] = tile(slot, index, source)
        for index in range(0, KV_HEADS, 2):
            lanes = pl.ds(index * HEAD_DIM, LANES)
            even, odd = tile(slot, index, 2 * tiles), tile(slot, index + 1, 2 * tiles)
            rest_stages[0][rows, lanes] = jnp.where(low, even, pair_swap(odd))
            rest_stages[1][rows, lanes] = jnp.where(low, pair_swap(even), odd)
            even, odd = tile(slot, index, 3 * tiles + 1), tile(slot, index + 1, 3 * tiles + 1)
            rest_stages[2][rows, lanes] = jnp.where(low, even, pair_swap(odd))
        for out_ref, stage, rest_stage in zip(out_refs, stages, rest_stages):
            copies.store(stage.at[rows, :], out_ref.at[rows, pl.ds(0, cut)])
            copies.store(rest_stage.at[rows, :], out_ref.at[rows, pl.ds(2 * cut, rest_stage.shape[1])])
    copies.finish()


def second_rows_kernel(second_ref, *refs):
    out_refs, stages, sems = refs[3:10], refs[10:17], refs[17]
    copies = Copies(sems)
    f32 = jnp.float32
    block = out_refs[0].shape[1] // 2 // KV_HEADS // LANES * LANES
    cut = KV_HEADS * block
    heads = 3 * block
    rows_each = second_ref.shape[2]
    low = lane_is_low((rows_each, LANES))
    query, key, value, out = stages[3:]
    for slot in range(second_ref.shape[0]):
        rows = pl.ds(slot * rows_each, rows_each)
        for index in range(KV_HEADS):
            for place, stage in enumerate(stages[:3]):
                columns = second_ref[slot, index, :, place * block : (place + 1) * block]
                stage[rows, pl.ds(index * block, block)] = columns.astype(f32)
            lanes = pl.ds(index * LANES, LANES)
            query[rows, lanes] = second_ref[slot, index, :, heads : heads + LANES].astype(f32)
            out[rows, lanes] = second_ref[slot, index, :, heads + 2 * LANES :].astype(f32)
        for index in range(0, KV_HEADS, 2):
            lanes = pl.ds(index * HEAD_DIM, LANES)
            even = second_ref[slot, index, :, heads + LANES : heads + 2 * LANES].astype(f32)
            odd = second_ref[slot, index + 1, :, heads + LANES : heads + 2 * LANES].astype(f32)
            key[rows, lanes] = jnp.where(low, even, pair_swap(odd))
            value[rows, lanes] = jnp.where(low, pair_swap(even), odd)
        for place, (out_ref, stage) in enumerate(zip(out_refs, stages)):
            target = out_ref.at[rows, pl.ds(cut, cut)] if place < 3 else out_ref.at[rows, :]
            copies.store(stage.at[rows, :], target)
    copies.finish()


def rotary_pair_tables(total):
    half = HEAD_DIM // 2
    exponent = np.arange(half, dtype=np.float32) * np.float32(2.0 / HEAD_DIM)
    inverse = np.float32(THETA_BASE) ** (-exponent)
    angles = np.arange(total, dtype=np.float32)[:, None] * inverse[None, :]
    cosine, sine = np.cos(angles), np.sin(angles)
    return (
        jnp.asarray(np.concatenate([cosine] * 4, axis=1), jnp.float32),
        jnp.asarray(np.concatenate([-sine, sine, -sine, sine], axis=1), jnp.float32),
    )


def to_partner(block, partner):
    return lax.ppermute(block, "seq", [(i, i ^ partner) for i in range(KV_HEADS)])


def gather_chips(block):
    return [block] + [to_partner(block, partner) for partner in (2, 4, 6)]


def gather_cores(parts):
    return [part for pair in zip(parts, [to_partner(part, 1) for part in parts]) for part in pair]


def swap_chips(blocks):
    cores = [list(range(core, KV_HEADS, 2)) for core in range(2)]
    return lax.all_to_all(blocks, "seq", 0, 0, axis_index_groups=cores, tiled=True)


def sum_partners(me, own, other, *tokens):
    *parts, added = call(add_kernel, (array(own.dtype, *own.shape[1:]),) * own.shape[0], token=True)(
        me, own, to_partner(other, 1), smem=1, tokens=tokens
    )
    return [parts[0]] + [to_partner(parts[i], 2 * i) for i in (1, 2, 3)], added


def to_slot(block, partner):
    return lax.ppermute(block, "slot", [(i, i ^ partner) for i in range(SLOTS_BY_HEADS)])


def send_quarters(quarters):
    return [quarters[0]] + [to_slot(quarters[partner], partner) for partner in (1, 2, 3)]


def sum_devices(values):
    for partner in (1, 2, 4):
        values = values + to_partner(values, partner)
    return four_sum([values] + [to_slot(values, partner) for partner in (1, 2, 3)])


def heads_body(
    tokens, lengths, query_weight, key_weight, value_weight, out_weight, gate_weight, up_weight, down_weight,
    attn_norm, query_norm, key_norm, ffn_norm, out_grad,
):
    f32, bf16 = jnp.float32, jnp.bfloat16
    count = KV_HEADS
    tok_rows, width = tokens.shape[1:]
    depth = query_weight.shape[0]
    total = tok_rows * count
    units = gate_weight.shape[1] // count
    block = (units - HEAD_DIM) // 2
    length = lengths[0]
    index = lax.axis_index("seq")
    me = index[None]
    slot = lax.axis_index("slot")[None]
    position = index * tok_rows + jnp.arange(tok_rows, dtype=jnp.int32)
    row_valid = (position < length)[:, None]

    def swap(blocks):
        return lax.all_to_all(blocks, "seq", 0, 0, tiled=True)

    x_parts = gather_cores(gather_chips(tokens[0]))
    attn_owned, packed = call(pack_attention_kernel, array(bf16, count, depth, 2 * LANES), token=True)(
        query_weight, key_weight, value_weight
    )
    attn_weight = swap(attn_owned).reshape(width, 2 * LANES)
    first_owned, second_owned = call(
        pack_units_kernel,
        (array(bf16, count, depth // 2, 3 * block + 2 * LANES), array(bf16, count, depth, 3 * block)),
    )(slot, gate_weight, up_weight, down_weight, smem=1, tokens=(packed,))
    upstream = jnp.where(row_valid, out_grad[0], jnp.zeros_like(out_grad[0]))
    (first_owned,) = after((first_owned,), *x_parts, attn_weight)
    first_own = swap(first_owned)
    out_full = lax.all_gather(out_weight, "seq", axis=0, tiled=True)

    cosine, sine = rotary_pair_tables(total)
    q_gain = jnp.concatenate([query_norm, query_norm])[None]
    k_gain = jnp.concatenate([key_norm, jnp.ones_like(key_norm)])[None]
    x_all, normed, q_proj, kv_proj, q_low, k_pair, v_pair, attn, attn_low, weight_inv, attended = call(
        attention_forward_kernel,
        (
            array(bf16, total, width), array(bf16, total, width), array(f32, total, LANES), array(f32, total, LANES),
            array(bf16, total, LANES), array(bf16, total, LANES), array(bf16, total, LANES), array(f32, total, LANES),
            array(bf16, total, LANES), array(f32, total, LANES),
        ),
        token=True,
    )(lengths, me, *x_parts, attn_weight, attn_norm[None], q_gain, k_gain, cosine, sine, smem=2)

    attn_parts = gather_chips(attn_low)
    (second_owned,) = after((second_owned,), attended)
    second_weight = swap(second_owned).reshape(width, -1)
    first_own, upstream = after((first_own, upstream), *attn_parts[1:])
    first_other = to_slot(first_own, 1)
    dout_parts = gather_chips(upstream)
    attn_parts = gather_cores(attn_parts)
    residual, normed_two, normed_ready = call(
        residual_kernel,
        (array(f32, tok_rows, width), array(bf16, total, width)),
        scratch_shapes=[pltpu.VMEM((total, width), bf16), pltpu.VMEM((total, width), f32)],
        token=True,
    )(me, x_all, *attn_parts, out_full, ffn_norm[None], smem=1, tokens=(second_owned,))

    dout_parts = gather_cores(after(tuple(dout_parts), normed_ready, first_other))
    first_cols, second_cols = 3 * block + 2 * LANES, 3 * block
    units_first, units_second = 2 * block + LANES, 2 * block
    halves = (array(bf16, count // 2, tok_rows, width),) * 2
    quarter = depth // SLOTS_BY_HEADS
    first_arrays = (
        array(bf16, total, width), array(bf16, width, first_cols), array(bf16, total, block + LANES),
        array(bf16, total, units_first), array(bf16, SLOTS_BY_HEADS, count, quarter, first_cols - HEAD_DIM),
    )
    dout_all, first_weight, hidden_first, dgate_up_first, first_grads, first_done = moving(
        first_units_kernel,
        first_arrays,
        [pltpu.VMEM((total, width), bf16)] + [pltpu.VMEM(shape.shape, shape.dtype) for shape in first_arrays],
        64,
        token=True,
    )(me, slot, normed_two, *dout_parts, first_own, first_other, smem=2, tokens=(second_weight,))
    first_sums = lax.psum_scatter(
        first_grads.reshape(width, first_cols - HEAD_DIM), "slot", scatter_dimension=0, tiled=True
    )
    hidden_second, dgate_up_second, *normed_two_grad, summed = call(
        second_units_kernel,
        (array(bf16, total, block), array(bf16, total, units_second), *halves),
        token=True,
    )(
        me, normed_two, dout_all, first_weight, second_weight, dgate_up_first, smem=1,
        tokens=(first_done,),
    )

    def unit_grads(hidden, dgate_up, cols, *tokens):
        grads, done = call(unit_grads_kernel, array(bf16, SLOTS_BY_HEADS, count, depth // SLOTS_BY_HEADS, cols), token=True)(
            normed_two, dout_all, hidden, dgate_up, tokens=tokens
        )
        return done, lax.psum_scatter(grads.reshape(width, cols), "slot", scatter_dimension=0, tiled=True)

    def to_owners(sums):
        return swap(sums.reshape(count, -1, sums.shape[1]))

    normed_two_sum = call(add_blocks_kernel, halves[0])(
        normed_two_grad[0], to_partner(normed_two_grad[1], 1)
    )
    residual_grad, attn_out_low, dattn, ffn_terms, branched = call(
        residual_back_kernel,
        (
            array(f32, tok_rows, width), array(bf16, tok_rows, width), array(bf16, count, tok_rows, LANES),
            array(f32, 1, width),
        ),
        token=True,
    )(swap_chips(normed_two_sum), residual, upstream, ffn_norm[None], out_full)
    second_grads, second_sums = unit_grads(hidden_second, dgate_up_second, 3 * block, branched)
    quarter_tiles = quarter * (-(-(first_cols - HEAD_DIM) // LANES))
    swapped = swap(
        call(tile_rows_kernel, array(bf16, count, tok_rows + quarter_tiles, LANES))(
            dattn, first_sums.reshape(count, quarter, -1), tokens=(second_grads,)
        )
    )
    dattn, first_rows = swapped[:, :tok_rows], swapped[:, tok_rows:]
    first_all = lax.all_gather(first_rows, "slot", axis=0)
    dbranch_parts = gather_chips(*after((attn_out_low,), dattn))
    late = (
        (bf16, width, 2 * LANES), (f32, total, LANES), (f32, total, LANES), (f32, total, LANES), (f32, total, LANES),
        (bf16, total, width),
    )
    slots = SLOTS_BY_HEADS
    terms, *quarters, dnormed_own, dnormed_other, passed = call(
        attention_backward_kernel,
        (array(f32, 2, LANES), *(array(bf16, count, quarter, 2 * LANES),) * slots, *halves),
        scratch_shapes=[pltpu.VMEM((total, LANES), f32)] * 3
        + [pltpu.VMEM(shape.shape, bf16) for shape in halves]
        + [pltpu.VMEM((total, 2 * LANES), bf16), pltpu.VMEM((slots, count, quarter, 2 * LANES), bf16)]
        + [pltpu.VMEM(shape, kind) for kind, *shape in late]
        + [pltpu.SemaphoreType.DMA((len(late) + count,))],
        token=True,
        late=len(late),
        kept=2,
    )(
        lengths, me, slot, dattn.reshape(total, LANES), q_gain, k_gain, q_low, k_pair, v_pair, attn, weight_inv,
        attn_weight, cosine, sine, q_proj, kv_proj, normed, smem=3, tokens=(second_grads,),
    )
    proj_parts = send_quarters(quarters)
    dbranch_parts = gather_cores(after(tuple(dbranch_parts), passed))
    *quarters, projected = call(
        out_grads_kernel,
        (array(bf16, count, quarter, LANES),) * slots,
        scratch_shapes=[pltpu.VMEM((slots, count, quarter, LANES), bf16), pltpu.VMEM((total, width), bf16)],
        token=True,
    )(me, slot, attn_low, *dbranch_parts, smem=2, tokens=tuple(proj_parts[1:]))
    out_parts = send_quarters(quarters)

    dnormed_own, dnormed_other = after((dnormed_own, dnormed_other), projected)
    dnormed_parts, added = sum_partners(me, dnormed_own, dnormed_other)
    attn_terms, gained = call(attention_gain_kernel, array(f32, 1, width), token=True)(
        me, x_all, dnormed_own, dnormed_other, smem=1, tokens=(added,)
    )
    (second_sums,) = after((second_sums,), gained)
    joined, join_done = call(join_kernel, array(bf16, count, quarter, second_cols + 3 * LANES), token=True)(
        second_sums.reshape(count, quarter, second_cols), *proj_parts, *out_parts
    )
    second_all = lax.all_gather(swap(joined), "slot", axis=0)
    *mixed_halves, mixed_done = call(mixed_kernel, halves, token=True)(
        me, hidden_first, hidden_second, first_weight, second_weight, smem=1, tokens=(join_done,)
    )
    mixed_parts, _ = sum_partners(me, *mixed_halves, mixed_done)
    input_grad = call(input_back_kernel, array(bf16, tok_rows, width))(
        *dnormed_parts, tokens[0], residual_grad, attn_norm[None]
    )
    result = residual + sum(part.astype(f32) for part in mixed_parts)
    mixed = jnp.where(row_valid, result, 0.0).astype(bf16)[None]
    stages = [pltpu.VMEM((depth, count * block), f32)] * 3
    unit_shapes = (array(f32, *gate_weight.shape),) * 3
    attention_shapes = tuple(array(f32, *weight.shape) for weight in (query_weight, key_weight, value_weight, out_weight))
    unit_rows = write_columns(
        first_rows_kernel, unit_shapes, stages + [pltpu.VMEM((depth, count * HEAD_DIM), f32)] * 3, 24
    )(first_all)
    *unit_rows, query_rows, key_rows, value_rows, out_rows = write_columns(
        second_rows_kernel,
        unit_shapes + attention_shapes,
        stages + [pltpu.VMEM(shape.shape, f32) for shape in attention_shapes],
        28,
    )(second_all, *unit_rows)

    half = HEAD_DIM
    gains = jnp.concatenate([attn_terms[0], ffn_terms[0], terms[0, :half] + terms[0, half:], terms[1, :half]])
    gains = sum_devices(gains.reshape(-1, LANES)).reshape(-1)
    return (
        mixed, input_grad[None], query_rows, key_rows, value_rows, out_rows, *unit_rows, gains[:width], gains[2 * width : 2 * width + half],
        gains[2 * width + half :], gains[width : 2 * width],
    )


def solution(mesh):
    in_specs = (
        P("slot", "seq", None),
        P("slot"),
        P("seq", None),
        P("seq", None),
        P("seq", None),
        P("seq", None),
        P("seq", None),
        P("seq", None),
        P("seq", None),
        P(),
        P(),
        P(),
        P(),
        P("slot", "seq", None),
    )
    out_specs = (
        P("slot", "seq", None),
        P("slot", "seq", None),
        P("seq", None),
        P("seq", None),
        P("seq", None),
        P("seq", None),
        P("seq", None),
        P("seq", None),
        P("seq", None),
        P(),
        P(),
        P(),
        P(),
    )
    by_heads = mesh.shape["seq"] == KV_HEADS and mesh.shape["slot"] == SLOTS_BY_HEADS
    body = heads_body if by_heads else general_body
    return jax.shard_map(body, mesh=mesh, in_specs=in_specs, out_specs=out_specs, check_vma=False)
```

```python
import functools

import jax
import jax.numpy as jnp
import numpy as np
from jax import lax
from jax.experimental import pallas as pl
from jax.experimental.pallas import tpu as pltpu
from jax.sharding import PartitionSpec as P

HEADS = 16
KV_HEADS = 8
HEAD_DIM = 64


EPSILON = 1e-05
THETA_BASE = 1000000.0
MASK_FILL = -1e30
HIGHEST = lax.Precision.HIGHEST


def rms_apply(values, gain_vec):
    factor = lax.rsqrt(jnp.mean(values * values, axis=-1, keepdims=True) + EPSILON)
    return (values * factor * gain_vec, factor)


def rms_back(values, factor, gain_vec, upstream):
    normal = values * factor
    weighted = upstream * gain_vec
    shared = jnp.mean(weighted * normal, axis=-1, keepdims=True)
    return (factor * (weighted - normal * shared), upstream * normal)


def rotary_tables(position):
    exponent = jnp.arange(HEAD_DIM // 2, dtype=jnp.float32) * (2.0 / HEAD_DIM)
    inverse = THETA_BASE ** (-exponent)
    angles = position.astype(jnp.float32)[:, None] * inverse[None, :]
    cosine = jnp.concatenate([jnp.cos(angles), jnp.cos(angles)], axis=-1)
    sine_tab = jnp.concatenate([jnp.sin(angles), jnp.sin(angles)], axis=-1)
    return (cosine, sine_tab)


def rotate(values, cosine, sine_tab):
    half_dim = values.shape[-1] // 2
    turned = jnp.concatenate([-values[..., half_dim:], values[..., :half_dim]], axis=-1)
    return values * cosine[:, None, :] + turned * sine_tab[:, None, :]


def rotate_back(upstream, cosine, sine_tab):
    half_dim = upstream.shape[-1] // 2
    scaled = upstream * sine_tab[:, None, :]
    turned = jnp.concatenate([scaled[..., half_dim:], -scaled[..., :half_dim]], axis=-1)
    return upstream * cosine[:, None, :] + turned


def contract_rows(left, right):
    return lax.dot_general(
        left, right, (((0,), (0,)), ((), ())), preferred_element_type=jnp.float32
    )


def contract_cols(left, right):
    return lax.dot_general(
        left, right, (((1,), (1,)), ((), ())), preferred_element_type=jnp.float32
    )


def general_body(
    tokens,
    lengths,
    query_weight,
    key_weight,
    value_weight,
    out_weight,
    gate_weight,
    up_weight,
    down_weight,
    attn_norm,
    query_norm,
    key_norm,
    ffn_norm,
    out_grad,
):
    tok_rows = tokens.shape[1]
    group_size = HEADS // KV_HEADS
    kv_width = KV_HEADS * HEAD_DIM
    score_scale = HEAD_DIM ** (-0.5)
    length = lengths[0]
    my_index = lax.axis_index("seq")
    position = my_index * tok_rows + jnp.arange(tok_rows, dtype=jnp.int32)
    row_valid = (position < length)[:, None]
    cosine, sine_tab = rotary_tables(position)
    inputs = tokens[0].astype(jnp.float32)
    query_full, key_full, value_full, out_full, gate_full, up_full, down_full = (
        lax.all_gather(query_weight, "seq", axis=0, tiled=True),
        lax.all_gather(key_weight, "seq", axis=0, tiled=True),
        lax.all_gather(value_weight, "seq", axis=0, tiled=True),
        lax.all_gather(out_weight, "seq", axis=0, tiled=True),
        lax.all_gather(gate_weight, "seq", axis=0, tiled=True),
        lax.all_gather(up_weight, "seq", axis=0, tiled=True),
        lax.all_gather(down_weight, "seq", axis=0, tiled=True),
    )
    normed_float, factor_one = rms_apply(inputs, attn_norm)
    normed = normed_float.astype(jnp.bfloat16)
    query_proj = jnp.dot(normed, query_full, preferred_element_type=jnp.float32).reshape(
        tok_rows, HEADS, HEAD_DIM
    )
    key_proj = jnp.dot(normed, key_full, preferred_element_type=jnp.float32).reshape(
        tok_rows, KV_HEADS, HEAD_DIM
    )
    value_low = jnp.dot(normed, value_full, preferred_element_type=jnp.float32).astype(jnp.bfloat16)
    query_unit, query_factor = rms_apply(query_proj, query_norm)
    key_unit, key_factor = rms_apply(key_proj, key_norm)
    query_low = (
        rotate(query_unit, cosine, sine_tab)
        .astype(jnp.bfloat16)
        .reshape(tok_rows, KV_HEADS, group_size, HEAD_DIM)
    )
    key_low = rotate(key_unit, cosine, sine_tab).astype(jnp.bfloat16).reshape(tok_rows, kv_width)

    def piece_scores(key_heads):
        key_count = key_heads.shape[0]
        scores = (
            jnp.einsum("tgrd,ngd->grtn", query_low, key_heads, preferred_element_type=jnp.float32)
            * score_scale
        )
        key_place = jnp.arange(key_count, dtype=jnp.int32)
        allowed = (key_place[None, :] <= position[:, None]) & (key_place[None, :] < length)
        return (scores, allowed)

    piece = (
        lax.all_gather(key_low, "seq", axis=0, tiled=True),
        lax.all_gather(value_low, "seq", axis=0, tiled=True),
    )
    forward_top_score = jnp.full((KV_HEADS, group_size, tok_rows), MASK_FILL, jnp.float32)
    key_heads = piece[0].reshape(-1, KV_HEADS, HEAD_DIM)
    value_heads = piece[1].reshape(-1, KV_HEADS, HEAD_DIM)
    scores, allowed = piece_scores(key_heads)
    masked = jnp.where(allowed, scores, MASK_FILL)
    new_top = jnp.maximum(forward_top_score, jnp.max(masked, axis=-1))
    weights = jnp.where(allowed, jnp.exp(masked - new_top[..., None]), 0.0)
    forward_weight_sum = jnp.sum(weights, axis=-1)
    added = jnp.einsum(
        "grtn,ngd->tgrd",
        weights.astype(jnp.bfloat16),
        value_heads,
        preferred_element_type=jnp.float32,
    )
    accum = added
    top_score, weight_sum, accum = (new_top, forward_weight_sum, accum)
    attn_heads = accum / jnp.transpose(weight_sum, (2, 0, 1))[..., None]
    attn_low = attn_heads.reshape(tok_rows, HEADS * HEAD_DIM).astype(jnp.bfloat16)
    residual = inputs + contract_cols(attn_low, out_full)
    normed_two_float, factor_two = rms_apply(residual, ffn_norm)
    normed_two = normed_two_float.astype(jnp.bfloat16)
    gate_val = jnp.dot(normed_two, gate_full, preferred_element_type=jnp.float32)
    up_val = jnp.dot(normed_two, up_full, preferred_element_type=jnp.float32)
    sigmoid_gate = jax.nn.sigmoid(gate_val)
    silu_gate = gate_val * sigmoid_gate
    hidden = (silu_gate * up_val).astype(jnp.bfloat16)
    result = residual + contract_cols(hidden, down_full)
    mixed = jnp.where(row_valid, result, 0.0).astype(jnp.bfloat16)[None]
    query_full, key_full, value_full, out_full, gate_full, up_full, down_full = (
        lax.all_gather(query_weight, "seq", axis=0, tiled=True),
        lax.all_gather(key_weight, "seq", axis=0, tiled=True),
        lax.all_gather(value_weight, "seq", axis=0, tiled=True),
        lax.all_gather(out_weight, "seq", axis=0, tiled=True),
        lax.all_gather(gate_weight, "seq", axis=0, tiled=True),
        lax.all_gather(up_weight, "seq", axis=0, tiled=True),
        lax.all_gather(down_weight, "seq", axis=0, tiled=True),
    )
    upstream = jnp.where(row_valid, out_grad[0].astype(jnp.float32), 0.0)
    branch_grad = upstream.astype(jnp.bfloat16)
    hidden_grad = jnp.dot(branch_grad, down_full, preferred_element_type=jnp.float32)
    down_w_grad = contract_rows(branch_grad, hidden)
    gate_grad_low = (
        hidden_grad * up_val * sigmoid_gate * (1.0 + gate_val * (1.0 - sigmoid_gate))
    ).astype(jnp.bfloat16)
    up_grad_low = (hidden_grad * silu_gate).astype(jnp.bfloat16)
    normed_two_grad = contract_cols(gate_grad_low, gate_full) + contract_cols(up_grad_low, up_full)
    gate_w_grad = contract_rows(normed_two, gate_grad_low)
    up_w_grad = contract_rows(normed_two, up_grad_low)
    residual_part, ffn_terms = rms_back(residual, factor_two, ffn_norm, normed_two_grad)
    residual_grad = upstream + residual_part
    attn_out_low = residual_grad.astype(jnp.bfloat16)
    out_w_grad = contract_rows(attn_out_low, attn_low)
    attn_grad_low = jnp.dot(attn_out_low, out_full, preferred_element_type=jnp.float32).astype(
        jnp.bfloat16
    )
    attn_grad_heads = attn_grad_low.reshape(tok_rows, KV_HEADS, group_size, HEAD_DIM)
    row_inner = jnp.transpose(
        jnp.sum(attn_grad_heads.astype(jnp.float32) * attn_heads, axis=-1), (1, 2, 0)
    )
    scaled_grad = (
        attn_grad_heads.astype(jnp.float32) / jnp.transpose(weight_sum, (2, 0, 1))[..., None]
    )
    piece = (
        lax.all_gather(key_low, "seq", axis=0, tiled=True),
        lax.all_gather(value_low, "seq", axis=0, tiled=True),
    )
    key_heads = piece[0].reshape(-1, KV_HEADS, HEAD_DIM)
    value_heads = piece[1].reshape(-1, KV_HEADS, HEAD_DIM)
    key_count = key_heads.shape[0]
    scores, allowed = piece_scores(key_heads)
    shifted = jnp.where(allowed, scores - top_score[..., None], MASK_FILL)
    exp_vals = jnp.where(allowed, jnp.exp(shifted), 0.0)
    probs = exp_vals / weight_sum[..., None]
    prob_grad = jnp.einsum(
        "tgrd,ngd->grtn", attn_grad_heads, value_heads, preferred_element_type=jnp.float32
    )
    score_grad = (probs * (prob_grad - row_inner[..., None])).astype(jnp.bfloat16)
    backward_query_acc = (
        jnp.einsum("grtn,ngd->tgrd", score_grad, key_heads, preferred_element_type=jnp.float32)
        * score_scale
    )
    key_part = (
        jnp.einsum("grtn,tgrd->ngd", score_grad, query_low, preferred_element_type=jnp.float32)
        * score_scale
    )
    exp_low = exp_vals.astype(jnp.bfloat16).astype(jnp.float32)
    value_part = jnp.einsum(
        "grtn,tgrd->ngd",
        exp_low,
        scaled_grad,
        precision=HIGHEST,
        preferred_element_type=jnp.float32,
    )
    update = jnp.concatenate(
        [key_part.reshape(key_count, kv_width), value_part.reshape(key_count, kv_width)], axis=1
    )
    query_acc, update = (backward_query_acc, update)
    key_buffer = update
    query_acc, key_buffer = (query_acc, key_buffer)
    key_value_grad = lax.psum_scatter(key_buffer, "seq", scatter_dimension=0, tiled=True)
    key_rot_grad = key_value_grad[:, :kv_width].reshape(tok_rows, KV_HEADS, HEAD_DIM)
    value_grad_low = key_value_grad[:, kv_width:].astype(jnp.bfloat16)
    query_rot_grad = query_acc.reshape(tok_rows, HEADS, HEAD_DIM)
    query_proj_grad, query_terms = rms_back(
        query_proj, query_factor, query_norm, rotate_back(query_rot_grad, cosine, sine_tab)
    )
    key_proj_grad, key_terms = rms_back(
        key_proj, key_factor, key_norm, rotate_back(key_rot_grad, cosine, sine_tab)
    )
    query_grad_low = query_proj_grad.reshape(tok_rows, HEADS * HEAD_DIM).astype(jnp.bfloat16)
    key_grad_low = key_proj_grad.reshape(tok_rows, kv_width).astype(jnp.bfloat16)
    normed_grad = (
        contract_cols(query_grad_low, query_full)
        + contract_cols(key_grad_low, key_full)
        + contract_cols(value_grad_low, value_full)
    )
    query_w_grad = contract_rows(normed, query_grad_low)
    key_w_grad = contract_rows(normed, key_grad_low)
    value_w_grad = contract_rows(normed, value_grad_low)
    input_part, attn_terms = rms_back(inputs, factor_one, attn_norm, normed_grad)
    input_grad = (residual_grad + input_part).astype(jnp.bfloat16)[None]
    attn_gain_grad, query_gain_grad, key_gain_grad, ffn_gain_grad = lax.psum(
        (
            jnp.sum(attn_terms, axis=0),
            jnp.sum(query_terms, axis=(0, 1)),
            jnp.sum(key_terms, axis=(0, 1)),
            jnp.sum(ffn_terms, axis=0),
        ),
        ("seq", "slot"),
    )
    query_share, key_share, value_share, out_share, gate_share, up_share, down_share = (
        lax.psum_scatter(query_w_grad, "seq", scatter_dimension=0, tiled=True),
        lax.psum_scatter(key_w_grad, "seq", scatter_dimension=0, tiled=True),
        lax.psum_scatter(value_w_grad, "seq", scatter_dimension=0, tiled=True),
        lax.psum_scatter(out_w_grad, "seq", scatter_dimension=0, tiled=True),
        lax.psum_scatter(gate_w_grad, "seq", scatter_dimension=0, tiled=True),
        lax.psum_scatter(up_w_grad, "seq", scatter_dimension=0, tiled=True),
        lax.psum_scatter(down_w_grad, "seq", scatter_dimension=0, tiled=True),
    )
    query_share, key_share, value_share, out_share, gate_share, up_share, down_share = (
        lax.psum(query_share.astype(jnp.bfloat16), "slot").astype(jnp.float32),
        lax.psum(key_share.astype(jnp.bfloat16), "slot").astype(jnp.float32),
        lax.psum(value_share.astype(jnp.bfloat16), "slot").astype(jnp.float32),
        lax.psum(out_share.astype(jnp.bfloat16), "slot").astype(jnp.float32),
        lax.psum(gate_share.astype(jnp.bfloat16), "slot").astype(jnp.float32),
        lax.psum(up_share.astype(jnp.bfloat16), "slot").astype(jnp.float32),
        lax.psum(down_share.astype(jnp.bfloat16), "slot").astype(jnp.float32),
    )
    return (
        mixed,
        input_grad,
        query_share,
        key_share,
        value_share,
        out_share,
        gate_share,
        up_share,
        down_share,
        attn_gain_grad,
        query_gain_grad,
        key_gain_grad,
        ffn_gain_grad,
    )


SLOTS_BY_HEADS = 4
LANES = 2 * HEAD_DIM
ROW_BLOCK = 256
VMEM_LIMIT = 60 * 1024 * 1024


def dot_nn(left, right):
    return lax.dot_general(left, right, (((1,), (0,)), ((), ())), preferred_element_type=jnp.float32)


def dot_nt(left, right):
    return lax.dot_general(left, right, (((1,), (1,)), ((), ())), preferred_element_type=jnp.float32)


def dot_tn(left, right):
    return lax.dot_general(left, right, (((0,), (0,)), ((), ())), preferred_element_type=jnp.float32)


def lane_is_low(shape):
    return lax.broadcasted_iota(jnp.int32, shape, len(shape) - 1) < HEAD_DIM


def pair_mean(values):
    low = lane_is_low(values.shape)
    first = jnp.sum(jnp.where(low, values, 0.0), axis=-1, keepdims=True)
    second = jnp.sum(jnp.where(low, 0.0, values), axis=-1, keepdims=True)
    return jnp.where(low, first, second) * (1.0 / HEAD_DIM)


def pair_turn(values, cosine, sine_signed):
    lane = lax.broadcasted_iota(jnp.int32, values.shape, 1)
    near = lax.rem(lane, HEAD_DIM) < HEAD_DIM // 2
    half = HEAD_DIM // 2
    turned = jnp.where(near, pltpu.roll(values, LANES - half, 1), pltpu.roll(values, half, 1))
    return values * cosine + turned * sine_signed


def pair_swap(values):
    return pltpu.roll(values.astype(jnp.float32), HEAD_DIM, 1)


def array(kind, *shape):
    return jax.ShapeDtypeStruct(shape, kind)


def call(kernel, out_shape, scratch_shapes=(), token=False, late=0, kept=0):
    vmem, anywhere = pl.BlockSpec(memory_space=pltpu.VMEM), pl.BlockSpec(memory_space=pl.ANY)
    single = not isinstance(out_shape, tuple)
    shapes = ((out_shape,) if single else out_shape) + ((array(jnp.float32, 8, LANES),) if token else ())

    def apply(*operands, smem=0, tokens=()):
        given = len(operands)
        results = given + len(tokens) + len(shapes)

        def whole(*refs):
            if token:
                refs[results - 1][...] = jnp.zeros((8, LANES), jnp.float32)
            kernel(*refs[:given], *refs[given + len(tokens) : results - token], *refs[results:])

        in_specs = [pl.BlockSpec(memory_space=pltpu.SMEM)] * smem + [vmem] * (given - smem - late)
        outputs = pl.pallas_call(
            whole,
            out_shape=shapes,
            in_specs=in_specs + [anywhere] * (late + len(tokens)),
            out_specs=(vmem,) * (len(shapes) - kept - token) + (anywhere,) * kept + (vmem,) * token,
            scratch_shapes=scratch_shapes,
            compiler_params=pltpu.CompilerParams(vmem_limit_bytes=VMEM_LIMIT),
        )(*operands, *tokens)
        return outputs[0] if len(shapes) == 1 else outputs

    return apply


def moving(kernel, out_shape, scratch_shapes, copies, token=False):
    anywhere = pl.BlockSpec(memory_space=pl.ANY)
    shapes = tuple(out_shape) + ((array(jnp.float32, 8, LANES),) if token else ())
    specs = (anywhere,) * len(out_shape) + ((pl.BlockSpec(memory_space=pltpu.VMEM),) if token else ())

    def apply(*operands, smem=0, tokens=()):
        given = len(operands)
        results = given + len(tokens) + len(shapes)

        def body(*refs):
            if token:
                refs[results - 1][...] = jnp.zeros((8, LANES), jnp.float32)
            kernel(*refs[:given], *refs[given + len(tokens) : results - token], *refs[results:])

        outputs = pl.pallas_call(
            body,
            out_shape=shapes,
            in_specs=[pl.BlockSpec(memory_space=pltpu.SMEM)] * smem + [anywhere] * (given - smem + len(tokens)),
            out_specs=specs,
            scratch_shapes=[*scratch_shapes, pltpu.SemaphoreType.DMA((copies,))],
            compiler_params=pltpu.CompilerParams(vmem_limit_bytes=VMEM_LIMIT),
        )(*operands, *tokens)
        return outputs[0] if len(shapes) == 1 else outputs

    return apply


class Copies:
    def __init__(self, sems):
        self.sems, self.used, self.open = sems, 0, []

    def start(self, source, target):
        copy = pltpu.make_async_copy(source, target, self.sems.at[self.used])
        self.used += 1
        copy.start()
        return copy

    def store(self, source, target):
        self.open.append(self.start(source, target))

    def finish(self):
        for copy in self.open:
            copy.wait()


def write_columns(kernel, out_shape, stages, copies):
    vmem, anywhere = pl.BlockSpec(memory_space=pltpu.VMEM), pl.BlockSpec(memory_space=pl.ANY)

    def apply(part, *outputs):
        given = len(outputs)
        return pl.pallas_call(
            kernel,
            out_shape=out_shape,
            in_specs=[vmem] + [anywhere] * given,
            out_specs=(anywhere,) * len(out_shape),
            scratch_shapes=[*stages, pltpu.SemaphoreType.DMA((copies,))],
            input_output_aliases={1 + i: i for i in range(given)},
            compiler_params=pltpu.CompilerParams(vmem_limit_bytes=VMEM_LIMIT),
        )(part, *outputs)

    return apply


def after(values, *tokens):
    count = len(values)
    anywhere = pl.BlockSpec(memory_space=pl.ANY)
    return pl.pallas_call(
        lambda *refs: None,
        out_shape=tuple(array(value.dtype, *value.shape) for value in values),
        in_specs=[anywhere] * (count + len(tokens)),
        out_specs=(anywhere,) * count,
        input_output_aliases={i: i for i in range(count)},
    )(*values, *tokens)


def block_rows(me_ref, partner, rows):
    return pl.ds(pl.multiple_of(jnp.bitwise_xor(me_ref[0], partner) * rows, rows), rows)


def store_pair(me_ref, chip, values, own_ref, other_ref):
    rows = values.shape[0] // 2
    first = jnp.bitwise_and(me_ref[0], 1) == 0
    own_ref[chip] = jnp.where(first, values[:rows], values[rows:]).astype(jnp.bfloat16)
    other_ref[chip] = jnp.where(first, values[rows:], values[:rows]).astype(jnp.bfloat16)


def pack_attention_kernel(query_ref, key_ref, value_ref, owned_ref):
    for index in range(0, KV_HEADS, 2):
        lanes = pl.ds(index * HEAD_DIM, LANES)
        key, value = key_ref[:, lanes], value_ref[:, lanes]
        low = lane_is_low(key.shape)
        key, value = key.astype(jnp.float32), value.astype(jnp.float32)
        pairs = (jnp.where(low, key, pair_swap(value)), jnp.where(low, pair_swap(key), value))
        for step in range(2):
            owned_ref[index + step, :, :LANES] = query_ref[:, pl.ds((index + step) * LANES, LANES)]
            owned_ref[index + step, :, LANES:] = pairs[step].astype(jnp.bfloat16)


def pack_units_kernel(slot_ref, gate_ref, up_ref, down_ref, first_ref, second_ref):
    rows = first_ref.shape[1]
    block = second_ref.shape[2] // 3
    cut = block * KV_HEADS
    half = pl.ds(pl.multiple_of(jnp.bitwise_and(slot_ref[0], 1) * rows, rows), rows)
    for index in range(KV_HEADS):
        for place, ref in enumerate((gate_ref, up_ref, down_ref)):
            start = place * block + (LANES if place == 2 else 0)
            first_ref[index, :, start : start + block] = ref[half, pl.ds(index * block, block)]
            second_ref[index, :, place * block : (place + 1) * block] = ref[:, pl.ds(cut + index * block, block)]
    for index in range(0, KV_HEADS, 2):
        lanes = pl.ds(2 * cut + index * HEAD_DIM, LANES)
        gate, up, down = (ref[half, lanes].astype(jnp.float32) for ref in (gate_ref, up_ref, down_ref))
        low = lane_is_low(gate.shape)
        rests = (jnp.where(low, gate, pair_swap(up)), jnp.where(low, pair_swap(gate), up))
        downs = (jnp.where(low, down, pair_swap(down)), jnp.where(low, pair_swap(down), down))
        for step in range(2):
            first_ref[index + step, :, 2 * block : 2 * block + LANES] = rests[step].astype(jnp.bfloat16)
            first_ref[index + step, :, 3 * block + LANES :] = downs[step].astype(jnp.bfloat16)


def attention_forward_kernel(length_ref, me_ref, *refs):
    x_refs = refs[:KV_HEADS]
    (
        weight_ref, gain_ref, q_gain_ref, k_gain_ref, cos_ref, sin_ref,
        x_all_ref, normed_ref, q_proj_ref, kv_proj_ref, q_low_ref, k_pair_ref, v_pair_ref, attn_ref, attn_low_ref, weight_inv_ref,
    ) = refs[KV_HEADS:]
    tok_rows = x_refs[0].shape[0]
    total = tok_rows * KV_HEADS
    length = length_ref[0]
    low = lane_is_low((ROW_BLOCK, LANES))
    for partner in range(KV_HEADS):
        x_all_ref[block_rows(me_ref, partner, tok_rows), :] = x_refs[partner][...]
    for start in range(0, total, ROW_BLOCK):
        rows = pl.ds(start, ROW_BLOCK)
        x = x_all_ref[rows, :].astype(jnp.float32)
        factor = lax.rsqrt(jnp.mean(x * x, axis=-1, keepdims=True) + EPSILON)
        normed = (x * factor * gain_ref[...]).astype(jnp.bfloat16)
        normed_ref[rows, :] = normed
        proj = dot_nn(normed, weight_ref[...])
        q_proj = proj[:, :LANES]
        kv_proj = proj[:, LANES:]
        q_proj_ref[rows, :] = q_proj
        kv_proj_ref[rows, :] = kv_proj
        cosine, sine = cos_ref[rows, :], sin_ref[rows, :]
        q_factor = lax.rsqrt(pair_mean(q_proj * q_proj) + EPSILON)
        q_low_ref[rows, :] = pair_turn(q_proj * q_factor * q_gain_ref[...], cosine, sine).astype(jnp.bfloat16)
        k_factor = jnp.where(low, lax.rsqrt(pair_mean(kv_proj * kv_proj) + EPSILON), 1.0)
        kv = pair_turn(
            kv_proj * k_factor * k_gain_ref[...], jnp.where(low, cosine, 1.0), jnp.where(low, sine, 0.0)
        )
        swapped = pltpu.roll(kv, HEAD_DIM, 1)
        k_pair_ref[rows, :] = jnp.where(low, kv, swapped).astype(jnp.bfloat16)
        v_pair_ref[rows, :] = jnp.where(low, swapped, kv).astype(jnp.bfloat16)

    scale = HEAD_DIM ** (-0.5)
    for start in range(0, total, ROW_BLOCK):
        rows = pl.ds(start, ROW_BLOCK)
        q = q_low_ref[rows, :] * scale
        zero = jnp.zeros_like(q)
        heads = (jnp.where(low, q, zero), jnp.where(low, zero, q))
        results = []
        for q_head in heads:
            weight_sum = jnp.zeros((ROW_BLOCK, 1), jnp.float32)
            summed = jnp.zeros((ROW_BLOCK, LANES), jnp.float32)
            if start > 0:
                past = pl.ds(0, start)
                exp_vals = jnp.exp(dot_nt(q_head, k_pair_ref[past, :]))
                weight_sum += jnp.sum(exp_vals, axis=-1, keepdims=True)
                summed += dot_nn(exp_vals.astype(jnp.bfloat16), v_pair_ref[past, :])
            scores = dot_nt(q_head, k_pair_ref[rows, :])
            query = lax.broadcasted_iota(jnp.int32, scores.shape, 0)
            key = lax.broadcasted_iota(jnp.int32, scores.shape, 1)
            allowed = (key <= query) & (key + start < length)
            exp_vals = jnp.where(allowed, jnp.exp(scores), 0.0)
            weight_sum += jnp.sum(exp_vals, axis=-1, keepdims=True)
            summed += dot_nn(exp_vals.astype(jnp.bfloat16), v_pair_ref[rows, :])
            inverse = 1.0 / weight_sum
            results.append((summed * inverse, inverse))
        attn = jnp.where(low, results[0][0], results[1][0])
        attn_ref[rows, :] = attn
        attn_low_ref[rows, :] = attn.astype(jnp.bfloat16)
        weight_inv_ref[rows, :] = jnp.where(low, results[0][1], results[1][1])


def quarter_rows(slot_ref, left_ref, right, grads, quarters):
    slots, _, rows_each, _ = grads.shape
    for start in range(0, left_ref.shape[1], ROW_BLOCK):
        product = dot_tn(left_ref[:, pl.ds(start, ROW_BLOCK)], right).astype(jnp.bfloat16)
        for piece in range(0, ROW_BLOCK, rows_each):
            owner, slot = divmod((start + piece) // rows_each, slots)
            grads[slot, owner] = product[piece : piece + rows_each]
    for partner, quarter in enumerate(quarters):
        quarter[...] = grads[jnp.bitwise_xor(slot_ref[0], partner)]


def attention_backward_kernel(
    length_ref, me_ref, slot_ref, dattn_ref, q_gain_ref, k_gain_ref, q_low_ref, k_pair_ref, v_pair_ref, attn_ref, weight_inv_ref,
    *refs,
):
    late_refs, terms_ref, quarters, (dnormed_own_out, dnormed_other_out) = refs[:6], refs[6], refs[7:11], refs[11:13]
    dq_acc, dk_acc, dv_acc, dnormed_own_ref, dnormed_other_ref, dproj_ref, grads = refs[13:20]
    held, sems = refs[20:26], refs[26]
    weight_ref, cos_ref, sin_ref, q_proj_ref, kv_proj_ref, normed_ref = held
    copies = Copies(sems)
    loads = [copies.start(late, target) for late, target in zip(late_refs, held)]
    total = dattn_ref.shape[0]
    length = length_ref[0]
    low = lane_is_low((ROW_BLOCK, LANES))
    scale = HEAD_DIM ** (-0.5)
    dk_acc[...] = jnp.zeros_like(dk_acc)
    dv_acc[...] = jnp.zeros_like(dv_acc)
    for start in range(0, total, ROW_BLOCK):
        rows = pl.ds(start, ROW_BLOCK)
        q = q_low_ref[rows, :] * scale
        dattn = dattn_ref[rows, :]
        zero = jnp.zeros_like(q)
        inner = dattn.astype(jnp.float32) * attn_ref[rows, :]
        inverses = weight_inv_ref[rows, :]
        dq_heads = []
        for head in range(2):
            mine = low if head == 0 else jnp.logical_not(low)
            q_head = jnp.where(mine, q, zero)
            dattn_head = jnp.where(mine, dattn, zero)
            delta = jnp.sum(jnp.where(mine, inner, 0.0), axis=-1, keepdims=True)
            inverse = inverses[:, head * HEAD_DIM : head * HEAD_DIM + 1]
            dq = jnp.zeros((ROW_BLOCK, LANES), jnp.float32)
            spans = ([(0, start)] if start > 0 else []) + [(start, ROW_BLOCK)]
            for key_start, key_count in spans:
                keys = pl.ds(key_start, key_count)
                k_pair = k_pair_ref[keys, :]
                probs = jnp.exp(dot_nt(q_head, k_pair)) * inverse
                if key_start == start:
                    query = lax.broadcasted_iota(jnp.int32, probs.shape, 0)
                    key = lax.broadcasted_iota(jnp.int32, probs.shape, 1)
                    allowed = (key <= query) & (key + start < length)
                    probs = jnp.where(allowed, probs, 0.0)
                dprobs = dot_nt(dattn_head, v_pair_ref[keys, :])
                dscores = (probs * (dprobs - delta)).astype(jnp.bfloat16)
                dq += dot_nn(dscores, k_pair)
                dk_acc[keys, :] += dot_tn(dscores, q_head)
                dv_acc[keys, :] += dot_tn(probs.astype(jnp.bfloat16), dattn_head)
            dq_heads.append(dq)
        dq_acc[rows, :] = jnp.where(low, dq_heads[0], dq_heads[1]) * scale

    for load in loads[:5]:
        load.wait()
    q_terms = jnp.zeros((1, LANES), jnp.float32)
    k_terms = jnp.zeros((1, LANES), jnp.float32)
    for start in range(0, total, ROW_BLOCK):
        rows = pl.ds(start, ROW_BLOCK)
        cosine, sine = cos_ref[rows, :], sin_ref[rows, :]
        q_proj = q_proj_ref[rows, :]
        upstream = pair_turn(dq_acc[rows, :], cosine, -sine)
        factor = lax.rsqrt(pair_mean(q_proj * q_proj) + EPSILON)
        normal = q_proj * factor
        weighted = upstream * q_gain_ref[...]
        dq_proj = factor * (weighted - normal * pair_mean(weighted * normal))
        q_terms += jnp.sum(upstream * normal, axis=0, keepdims=True)

        dk = dk_acc[rows, :]
        dv = dv_acc[rows, :]
        dk = dk + pltpu.roll(dk, HEAD_DIM, 1)
        dv = dv + pltpu.roll(dv, HEAD_DIM, 1)
        kv_proj = kv_proj_ref[rows, :]
        upstream = pair_turn(jnp.where(low, dk, 0.0), jnp.where(low, cosine, 1.0), jnp.where(low, -sine, 0.0))
        factor = lax.rsqrt(pair_mean(kv_proj * kv_proj) + EPSILON)
        normal = kv_proj * factor
        weighted = upstream * k_gain_ref[...]
        dk_proj = factor * (weighted - normal * pair_mean(weighted * normal))
        k_terms += jnp.sum(upstream * normal, axis=0, keepdims=True)
        dkv_proj = jnp.where(low, dk_proj, dv)
        dproj = jnp.concatenate([dq_proj, dkv_proj], axis=1).astype(jnp.bfloat16)
        dproj_ref[rows, :] = dproj
        chip = start // ROW_BLOCK
        store_pair(me_ref, chip, dot_nt(dproj, weight_ref[...]), dnormed_own_ref, dnormed_other_ref)
        copies.store(dnormed_own_ref.at[chip], dnormed_own_out.at[chip])
        copies.store(dnormed_other_ref.at[chip], dnormed_other_out.at[chip])
    terms_ref[0:1, :] = q_terms
    terms_ref[1:2, :] = k_terms
    loads[5].wait()
    quarter_rows(slot_ref, normed_ref, dproj_ref[...], grads, quarters)
    copies.finish()


def residual_kernel(me_ref, x_ref, *refs):
    attn_refs = refs[:KV_HEADS]
    out_weight_ref, gain_ref, residual_ref, normed_ref, attn_scratch, scratch = refs[KV_HEADS:]
    total, width = x_ref.shape
    tok_rows = total // KV_HEADS
    for partner in range(KV_HEADS):
        attn_scratch[:, block_rows(me_ref, partner, LANES)] = attn_refs[partner][...]
    for start in range(0, total, ROW_BLOCK):
        rows = pl.ds(start, ROW_BLOCK)
        residual = x_ref[rows, :].astype(jnp.float32) + dot_nt(attn_scratch[rows, :], out_weight_ref[...])
        scratch[rows, :] = residual
        factor = lax.rsqrt(jnp.mean(residual * residual, axis=-1, keepdims=True) + EPSILON)
        normed_ref[rows, :] = (residual * factor * gain_ref[...]).astype(jnp.bfloat16)
    residual_ref[...] = scratch[block_rows(me_ref, 0, tok_rows), :]


def unit_share(gate, up, upstream):
    sigmoid = jax.nn.sigmoid(gate)
    silu = gate * sigmoid
    dgate = upstream * up * sigmoid * (1.0 + gate * (1.0 - sigmoid))
    return silu * up, dgate, upstream * silu


def first_units_kernel(me_ref, slot_ref, normed_ref, *refs):
    dout_refs, refs = refs[:KV_HEADS], refs[KV_HEADS:]
    halves, outs, refs = refs[:2], refs[2:7], refs[7:]
    dout_out, weight_out, hidden_out, dgate_out, grads_out = outs
    normed, dout, weight, hidden, dgate, grads, sems = refs
    copies = Copies(sems)
    total, width = normed.shape
    half = halves[0].shape[1]
    slots, _, rows_each, _ = grads.shape
    owners = ROW_BLOCK // (slots * rows_each)
    block = hidden.shape[1] - LANES
    units = dgate.shape[1]
    odd = jnp.bitwise_and(slot_ref[0], 1)
    starts = range(0, total, ROW_BLOCK)
    loads = []
    for index in range(KV_HEADS):
        for place, ref in ((odd, halves[0]), (1 - odd, halves[1])):
            rows = pl.ds(pl.multiple_of((2 * index + place) * half, half), half)
            loads.append(copies.start(ref.at[index], weight.at[rows, :]))
    normed_loads = [copies.start(normed_ref.at[pl.ds(start, ROW_BLOCK), :], normed.at[pl.ds(start, ROW_BLOCK), :]) for start in starts]
    dout_loads = [
        copies.start(dout_refs[partner], dout.at[block_rows(me_ref, partner, 2 * half), :]) for partner in range(KV_HEADS)
    ]
    for load in loads:
        load.wait()
    copies.store(weight, weight_out)
    low = lane_is_low((ROW_BLOCK, LANES))
    for step, start in enumerate(starts):
        rows = pl.ds(start, ROW_BLOCK)
        normed_loads[step].wait()
        both = dot_nn(normed[rows, :], weight[:, :units])
        if step == 0:
            for load in dout_loads:
                load.wait()
            copies.store(dout, dout_out)
        dhidden = dot_nn(dout[rows, :], weight[:, units:])
        share = unit_share(both[:, :block], both[:, block : 2 * block], dhidden[:, :block])
        rest = both[:, 2 * block :]
        swapped = pltpu.roll(rest, HEAD_DIM, 1)
        rest_share = unit_share(jnp.where(low, rest, swapped), jnp.where(low, swapped, rest), dhidden[:, block:])
        hidden[rows, :block] = share[0].astype(jnp.bfloat16)
        hidden[rows, block:] = jnp.where(low, rest_share[0], 0.0).astype(jnp.bfloat16)
        dgate[rows, :block] = share[1].astype(jnp.bfloat16)
        dgate[rows, block : 2 * block] = share[2].astype(jnp.bfloat16)
        dgate[rows, 2 * block :] = jnp.where(low, rest_share[1], rest_share[2]).astype(jnp.bfloat16)
    copies.store(hidden, hidden_out)
    copies.store(dgate, dgate_out)
    for step, start in enumerate(range(0, width, ROW_BLOCK)):
        lanes = pl.ds(start, ROW_BLOCK)
        gate_up = dot_tn(normed[:, lanes], dgate[...]).astype(jnp.bfloat16)
        down = dot_tn(dout[:, lanes], hidden[...])[:, : block + HEAD_DIM].astype(jnp.bfloat16)
        for owner in range(owners):
            for slot in range(slots):
                piece = (owner * slots + slot) * rows_each
                grads[slot, step * owners + owner, :, :units] = gate_up[piece : piece + rows_each]
                grads[slot, step * owners + owner, :, units:] = down[piece : piece + rows_each]
        done = pl.ds(step * owners, owners)
        copies.store(grads.at[:, done], grads_out.at[:, done])
    copies.finish()


def second_units_kernel(
    me_ref, normed_ref, dout_ref, first_ref, second_ref, dgate_up_first_ref, hidden_ref, dgate_up_ref, own_ref, other_ref
):
    total = normed_ref.shape[0]
    block = hidden_ref.shape[1]
    units = dgate_up_first_ref.shape[1]
    for start in range(0, total, ROW_BLOCK):
        rows = pl.ds(start, ROW_BLOCK)
        both = dot_nn(normed_ref[rows, :], second_ref[:, : 2 * block])
        dhidden = dot_nn(dout_ref[rows, :], second_ref[:, 2 * block :])
        hidden, dgate, dup = unit_share(both[:, :block], both[:, block:], dhidden)
        hidden_ref[rows, :] = hidden.astype(jnp.bfloat16)
        dgate_up = jnp.concatenate([dgate, dup], axis=1).astype(jnp.bfloat16)
        dgate_up_ref[rows, :] = dgate_up
        dnormed = dot_nt(dgate_up, second_ref[:, : 2 * block]) + dot_nt(dgate_up_first_ref[rows, :], first_ref[:, :units])
        store_pair(me_ref, start // ROW_BLOCK, dnormed, own_ref, other_ref)


def unit_grads_kernel(normed_ref, dout_ref, hidden_ref, dgate_up_ref, grads_ref):
    slots, _, rows_each, cols = grads_ref.shape
    units = dgate_up_ref.shape[1]
    for start in range(0, normed_ref.shape[1], ROW_BLOCK):
        rows = pl.ds(start, ROW_BLOCK)
        gate_up = dot_tn(normed_ref[:, rows], dgate_up_ref[...]).astype(jnp.bfloat16)
        down = dot_tn(dout_ref[:, rows], hidden_ref[...])[:, : cols - units].astype(jnp.bfloat16)
        for piece in range(0, ROW_BLOCK, rows_each):
            owner, slot = divmod((start + piece) // rows_each, slots)
            grads_ref[slot, owner, :, :units] = gate_up[piece : piece + rows_each]
            grads_ref[slot, owner, :, units:] = down[piece : piece + rows_each]


def mixed_kernel(me_ref, hidden_first_ref, hidden_second_ref, first_ref, second_ref, own_ref, other_ref):
    total = hidden_first_ref.shape[0]
    block = hidden_second_ref.shape[1]
    units = 2 * block + LANES
    for start in range(0, total, ROW_BLOCK):
        rows = pl.ds(start, ROW_BLOCK)
        part = dot_nt(hidden_first_ref[rows, :], first_ref[:, units:]) + dot_nt(
            hidden_second_ref[rows, :], second_ref[:, 2 * block :]
        )
        store_pair(me_ref, start // ROW_BLOCK, part, own_ref, other_ref)


def add_kernel(me_ref, own_ref, other_ref, *part_refs):
    chip = lax.shift_right_logical(me_ref[0], 1)
    for i, part_ref in enumerate(part_refs):
        place = jnp.bitwise_xor(chip, i)
        part_ref[...] = (own_ref[place].astype(jnp.float32) + other_ref[place].astype(jnp.float32)).astype(jnp.bfloat16)


def add_blocks_kernel(own_ref, other_ref, sum_ref):
    sum_ref[...] = (own_ref[...].astype(jnp.float32) + other_ref[...].astype(jnp.float32)).astype(sum_ref.dtype)


def four_sum(parts):
    first, second, third, fourth = (part.astype(jnp.float32) for part in parts)
    return (first + second) + (third + fourth)


def tile_rows_kernel(head_ref, sums_ref, joined_ref):
    count, rows, cols = sums_ref.shape
    start = head_ref.shape[1]
    joined_ref[:, :start, :] = head_ref[...]
    for tile in range(0, cols, LANES):
        size = min(LANES, cols - tile)
        joined_ref[:, start : start + rows, :size] = sums_ref[:, :, tile : tile + size]
        if size < LANES:
            joined_ref[:, start : start + rows, size:] = jnp.zeros((count, rows, LANES - size), joined_ref.dtype)
        start += rows


def join_kernel(*refs):
    joined_ref, place = refs[8], 0
    for parts in (refs[:4], refs[4:8]):
        cols = parts[0].shape[2]
        joined_ref[:, :, place : place + cols] = four_sum([ref[...] for ref in parts]).astype(joined_ref.dtype)
        place += cols


def residual_back_kernel(
    parts_ref, residual_ref, upstream_ref, gain_ref, out_weight_ref,
    residual_grad_ref, low_ref, dattn_ref, terms_ref,
):
    values = residual_ref[...]
    factor = lax.rsqrt(jnp.mean(values * values, axis=-1, keepdims=True) + EPSILON)
    part, terms = rms_back(values, factor, gain_ref[...], four_sum([parts_ref[i] for i in range(4)]))
    residual_grad = upstream_ref[...].astype(jnp.float32) + part
    residual_grad_ref[...] = residual_grad
    low = residual_grad.astype(jnp.bfloat16)
    low_ref[...] = low
    dattn = dot_nn(low, out_weight_ref[...]).astype(jnp.bfloat16)
    for index in range(KV_HEADS):
        dattn_ref[index] = dattn[:, index * LANES : (index + 1) * LANES]
    terms_ref[...] = jnp.sum(terms, axis=0, keepdims=True)


def input_back_kernel(
    part_a_ref, part_b_ref, part_c_ref, part_d_ref, tokens_ref, residual_grad_ref, gain_ref, input_grad_ref,
):
    values = tokens_ref[...].astype(jnp.float32)
    factor = lax.rsqrt(jnp.mean(values * values, axis=-1, keepdims=True) + EPSILON)
    part, _ = rms_back(values, factor, gain_ref[...], four_sum([ref[...] for ref in (part_a_ref, part_b_ref, part_c_ref, part_d_ref)]))
    input_grad_ref[...] = (residual_grad_ref[...] + part).astype(jnp.bfloat16)


def attention_gain_kernel(me_ref, x_ref, own_ref, other_ref, terms_ref):
    rows = own_ref.shape[1]
    core = jnp.bitwise_and(me_ref[0], 1)
    terms = jnp.zeros(terms_ref.shape, jnp.float32)
    for chip in range(own_ref.shape[0]):
        for place, ref in ((core, own_ref), (1 - core, other_ref)):
            x = x_ref[pl.ds(pl.multiple_of(chip * 2 * rows + place * rows, rows), rows), :].astype(jnp.float32)
            factor = lax.rsqrt(jnp.mean(x * x, axis=-1, keepdims=True) + EPSILON)
            terms += jnp.sum(ref[chip].astype(jnp.float32) * (x * factor), axis=0, keepdims=True)
    terms_ref[...] = terms


def out_grads_kernel(me_ref, slot_ref, attn_low_ref, *refs):
    dbranch_refs, quarters, grads, dbranch = refs[:KV_HEADS], refs[KV_HEADS:-2], refs[-2], refs[-1]
    tok_rows = dbranch_refs[0].shape[0]
    for partner in range(KV_HEADS):
        dbranch[block_rows(me_ref, partner, tok_rows), :] = dbranch_refs[partner][...]
    quarter_rows(slot_ref, dbranch, attn_low_ref[...], grads, quarters)


def first_rows_kernel(first_ref, *refs):
    out_refs, stages, rest_stages, sems = refs[:3], refs[3:6], refs[6:9], refs[9]
    copies = Copies(sems)
    f32 = jnp.float32
    block = stages[0].shape[1] // KV_HEADS
    cut = KV_HEADS * block
    rows_each = out_refs[0].shape[0] // first_ref.shape[0]
    low = lane_is_low((rows_each, LANES))

    def tile(slot, index, place):
        return first_ref[slot, index, place * rows_each : (place + 1) * rows_each, :].astype(f32)

    tiles = block // LANES
    for slot in range(first_ref.shape[0]):
        rows = pl.ds(slot * rows_each, rows_each)
        for index in range(KV_HEADS):
            for place, stage in enumerate(stages):
                for step in range(tiles):
                    source = place * tiles + step + (1 if place == 2 else 0)
                    stage[rows, pl.ds(index * block + step * LANES, LANES)] = tile(slot, index, source)
        for index in range(0, KV_HEADS, 2):
            lanes = pl.ds(index * HEAD_DIM, LANES)
            even, odd = tile(slot, index, 2 * tiles), tile(slot, index + 1, 2 * tiles)
            rest_stages[0][rows, lanes] = jnp.where(low, even, pair_swap(odd))
            rest_stages[1][rows, lanes] = jnp.where(low, pair_swap(even), odd)
            even, odd = tile(slot, index, 3 * tiles + 1), tile(slot, index + 1, 3 * tiles + 1)
            rest_stages[2][rows, lanes] = jnp.where(low, even, pair_swap(odd))
        for out_ref, stage, rest_stage in zip(out_refs, stages, rest_stages):
            copies.store(stage.at[rows, :], out_ref.at[rows, pl.ds(0, cut)])
            copies.store(rest_stage.at[rows, :], out_ref.at[rows, pl.ds(2 * cut, rest_stage.shape[1])])
    copies.finish()


def second_rows_kernel(second_ref, *refs):
    out_refs, stages, sems = refs[3:6], refs[6:9], refs[9]
    copies = Copies(sems)
    block = second_ref.shape[3] // 3
    cut = KV_HEADS * block
    rows_each = second_ref.shape[2]
    for slot in range(second_ref.shape[0]):
        rows = pl.ds(slot * rows_each, rows_each)
        for index in range(KV_HEADS):
            for place, stage in enumerate(stages):
                columns = second_ref[slot, index, :, place * block : (place + 1) * block]
                stage[rows, pl.ds(index * block, block)] = columns.astype(jnp.float32)
        for out_ref, stage in zip(out_refs, stages):
            copies.store(stage.at[rows, :], out_ref.at[rows, pl.ds(cut, cut)])
    copies.finish()


def attention_rows_kernel(slot_ref, *refs):
    parts, (query, key, value, out) = refs[:-4], refs[-4:]
    f32 = jnp.float32
    rows_each = parts[0].shape[1]
    low = lane_is_low((rows_each, LANES))
    for partner, part in enumerate(parts):
        rows = block_rows(slot_ref, partner, rows_each)
        for index in range(KV_HEADS):
            lanes = pl.ds(index * LANES, LANES)
            query[rows, lanes] = part[index, :, :LANES].astype(f32)
            out[rows, lanes] = part[index, :, 2 * LANES :].astype(f32)
        for index in range(0, KV_HEADS, 2):
            lanes = pl.ds(index * HEAD_DIM, LANES)
            even = part[index, :, LANES : 2 * LANES].astype(f32)
            odd = part[index + 1, :, LANES : 2 * LANES].astype(f32)
            key[rows, lanes] = jnp.where(low, even, pair_swap(odd))
            value[rows, lanes] = jnp.where(low, pair_swap(even), odd)


def rotary_pair_tables(total):
    half = HEAD_DIM // 2
    exponent = np.arange(half, dtype=np.float32) * np.float32(2.0 / HEAD_DIM)
    inverse = np.float32(THETA_BASE) ** (-exponent)
    angles = np.arange(total, dtype=np.float32)[:, None] * inverse[None, :]
    cosine, sine = np.cos(angles), np.sin(angles)
    return (
        jnp.asarray(np.concatenate([cosine] * 4, axis=1), jnp.float32),
        jnp.asarray(np.concatenate([-sine, sine, -sine, sine], axis=1), jnp.float32),
    )


def to_partner(block, partner):
    return lax.ppermute(block, "seq", [(i, i ^ partner) for i in range(KV_HEADS)])


def gather_chips(block):
    return [block] + [to_partner(block, partner) for partner in (2, 4, 6)]


def gather_cores(parts):
    return [part for pair in zip(parts, [to_partner(part, 1) for part in parts]) for part in pair]


def swap_chips(blocks):
    cores = [list(range(core, KV_HEADS, 2)) for core in range(2)]
    return lax.all_to_all(blocks, "seq", 0, 0, axis_index_groups=cores, tiled=True)


def sum_partners(me, own, other, *tokens):
    *parts, added = call(add_kernel, (array(own.dtype, *own.shape[1:]),) * own.shape[0], token=True)(
        me, own, to_partner(other, 1), smem=1, tokens=tokens
    )
    return [parts[0]] + [to_partner(parts[i], 2 * i) for i in (1, 2, 3)], added


def to_slot(block, partner):
    return lax.ppermute(block, "slot", [(i, i ^ partner) for i in range(SLOTS_BY_HEADS)])


def send_quarters(quarters):
    return [quarters[0]] + [to_slot(quarters[partner], partner) for partner in (1, 2, 3)]


def sum_chips(values):
    for partner in (1, 2, 4):
        values = values + to_partner(values, partner)
    return values


def sum_slots(values):
    def turn(block, steps):
        slots = SLOTS_BY_HEADS
        return lax.ppermute(block, "slot", [(i, (i + steps) % slots) for i in range(slots)])

    lower, upper = turn(values, 1), turn(values, 3)
    return (values + turn(lower, 1)) + (lower + upper)


def heads_body(
    tokens, lengths, query_weight, key_weight, value_weight, out_weight, gate_weight, up_weight, down_weight,
    attn_norm, query_norm, key_norm, ffn_norm, out_grad,
):
    f32, bf16 = jnp.float32, jnp.bfloat16
    count = KV_HEADS
    tok_rows, width = tokens.shape[1:]
    depth = query_weight.shape[0]
    total = tok_rows * count
    units = gate_weight.shape[1] // count
    block = (units - HEAD_DIM) // 2
    length = lengths[0]
    index = lax.axis_index("seq")
    me = index[None]
    slot = lax.axis_index("slot")[None]
    position = index * tok_rows + jnp.arange(tok_rows, dtype=jnp.int32)
    row_valid = (position < length)[:, None]

    def swap(blocks):
        return lax.all_to_all(blocks, "seq", 0, 0, tiled=True)

    x_parts = gather_cores(gather_chips(tokens[0]))
    attn_owned, packed = call(pack_attention_kernel, array(bf16, count, depth, 2 * LANES), token=True)(
        query_weight, key_weight, value_weight
    )
    attn_weight = swap(attn_owned).reshape(width, 2 * LANES)
    first_owned, second_owned = call(
        pack_units_kernel,
        (array(bf16, count, depth // 2, 3 * block + 2 * LANES), array(bf16, count, depth, 3 * block)),
    )(slot, gate_weight, up_weight, down_weight, smem=1, tokens=(packed,))
    upstream = jnp.where(row_valid, out_grad[0], jnp.zeros_like(out_grad[0]))
    (first_owned,) = after((first_owned,), *x_parts, attn_weight)
    first_own = swap(first_owned)
    out_full = lax.all_gather(out_weight, "seq", axis=0, tiled=True)

    cosine, sine = rotary_pair_tables(total)
    q_gain = jnp.concatenate([query_norm, query_norm])[None]
    k_gain = jnp.concatenate([key_norm, jnp.ones_like(key_norm)])[None]
    x_all, normed, q_proj, kv_proj, q_low, k_pair, v_pair, attn, attn_low, weight_inv, attended = call(
        attention_forward_kernel,
        (
            array(bf16, total, width), array(bf16, total, width), array(f32, total, LANES), array(f32, total, LANES),
            array(bf16, total, LANES), array(bf16, total, LANES), array(bf16, total, LANES), array(f32, total, LANES),
            array(bf16, total, LANES), array(f32, total, LANES),
        ),
        token=True,
    )(lengths, me, *x_parts, attn_weight, attn_norm[None], q_gain, k_gain, cosine, sine, smem=2)

    attn_parts = gather_chips(attn_low)
    (second_owned,) = after((second_owned,), attended)
    second_weight = swap(second_owned).reshape(width, -1)
    first_own, upstream = after((first_own, upstream), *attn_parts[1:])
    first_other = to_slot(first_own, 1)
    dout_parts = gather_chips(upstream)
    attn_parts = gather_cores(attn_parts)
    residual, normed_two, normed_ready = call(
        residual_kernel,
        (array(f32, tok_rows, width), array(bf16, total, width)),
        scratch_shapes=[pltpu.VMEM((total, width), bf16), pltpu.VMEM((total, width), f32)],
        token=True,
    )(me, x_all, *attn_parts, out_full, ffn_norm[None], smem=1, tokens=(second_owned,))

    dout_parts = gather_cores(after(tuple(dout_parts), normed_ready, first_other))
    first_cols, second_cols = 3 * block + 2 * LANES, 3 * block
    units_first, units_second = 2 * block + LANES, 2 * block
    halves = (array(bf16, count // 2, tok_rows, width),) * 2
    quarter = depth // SLOTS_BY_HEADS
    first_arrays = (
        array(bf16, total, width), array(bf16, width, first_cols), array(bf16, total, block + LANES),
        array(bf16, total, units_first), array(bf16, SLOTS_BY_HEADS, count, quarter, first_cols - HEAD_DIM),
    )
    dout_all, first_weight, hidden_first, dgate_up_first, first_grads, first_done = moving(
        first_units_kernel,
        first_arrays,
        [pltpu.VMEM((total, width), bf16)] + [pltpu.VMEM(shape.shape, shape.dtype) for shape in first_arrays],
        64,
        token=True,
    )(me, slot, normed_two, *dout_parts, first_own, first_other, smem=2, tokens=(second_weight,))
    first_sums = lax.psum_scatter(
        first_grads.reshape(width, first_cols - HEAD_DIM), "slot", scatter_dimension=0, tiled=True
    )
    hidden_second, dgate_up_second, *normed_two_grad, summed = call(
        second_units_kernel,
        (array(bf16, total, block), array(bf16, total, units_second), *halves),
        token=True,
    )(
        me, normed_two, dout_all, first_weight, second_weight, dgate_up_first, smem=1,
        tokens=(first_done,),
    )

    def unit_grads(hidden, dgate_up, cols, *tokens):
        grads, done = call(unit_grads_kernel, array(bf16, SLOTS_BY_HEADS, count, depth // SLOTS_BY_HEADS, cols), token=True)(
            normed_two, dout_all, hidden, dgate_up, tokens=tokens
        )
        return done, lax.psum_scatter(grads.reshape(width, cols), "slot", scatter_dimension=0, tiled=True)

    def to_owners(sums):
        return swap(sums.reshape(count, -1, sums.shape[1]))

    normed_two_sum = call(add_blocks_kernel, halves[0])(
        normed_two_grad[0], to_partner(normed_two_grad[1], 1)
    )
    residual_grad, attn_out_low, dattn, ffn_terms, branched = call(
        residual_back_kernel,
        (
            array(f32, tok_rows, width), array(bf16, tok_rows, width), array(bf16, count, tok_rows, LANES),
            array(f32, 1, width),
        ),
        token=True,
    )(swap_chips(normed_two_sum), residual, upstream, ffn_norm[None], out_full)
    second_grads, second_sums = unit_grads(hidden_second, dgate_up_second, 3 * block, branched)
    quarter_tiles = quarter * (-(-(first_cols - HEAD_DIM) // LANES))
    swapped = swap(
        call(tile_rows_kernel, array(bf16, count, tok_rows + quarter_tiles, LANES))(
            dattn, first_sums.reshape(count, quarter, -1), tokens=(second_grads,)
        )
    )
    dattn, first_rows = swapped[:, :tok_rows], swapped[:, tok_rows:]
    first_all = lax.all_gather(first_rows, "slot", axis=0)
    dbranch_parts = gather_chips(*after((attn_out_low,), dattn))
    late = (
        (bf16, width, 2 * LANES), (f32, total, LANES), (f32, total, LANES), (f32, total, LANES), (f32, total, LANES),
        (bf16, total, width),
    )
    slots = SLOTS_BY_HEADS
    terms, *quarters, dnormed_own, dnormed_other, passed = call(
        attention_backward_kernel,
        (array(f32, 2, LANES), *(array(bf16, count, quarter, 2 * LANES),) * slots, *halves),
        scratch_shapes=[pltpu.VMEM((total, LANES), f32)] * 3
        + [pltpu.VMEM(shape.shape, bf16) for shape in halves]
        + [pltpu.VMEM((total, 2 * LANES), bf16), pltpu.VMEM((slots, count, quarter, 2 * LANES), bf16)]
        + [pltpu.VMEM(shape, kind) for kind, *shape in late]
        + [pltpu.SemaphoreType.DMA((len(late) + count,))],
        token=True,
        late=len(late),
        kept=2,
    )(
        lengths, me, slot, dattn.reshape(total, LANES), q_gain, k_gain, q_low, k_pair, v_pair, attn, weight_inv,
        attn_weight, cosine, sine, q_proj, kv_proj, normed, smem=3, tokens=(second_grads,),
    )
    proj_parts = send_quarters(quarters)
    second_owned = swap(after((second_sums,), *proj_parts[1:3])[0].reshape(count, quarter, second_cols))
    second_all = lax.all_gather(second_owned, "slot", axis=0)
    *mixed_halves, mixed_done = call(mixed_kernel, halves, token=True)(
        me, hidden_first, hidden_second, first_weight, second_weight, smem=1, tokens=tuple(proj_parts[1:3])
    )
    dbranch_parts = gather_cores(after(tuple(dbranch_parts), passed))
    *quarters, projected = call(
        out_grads_kernel,
        (array(bf16, count, quarter, LANES),) * slots,
        scratch_shapes=[pltpu.VMEM((slots, count, quarter, LANES), bf16), pltpu.VMEM((total, width), bf16)],
        token=True,
    )(me, slot, attn_low, *dbranch_parts, smem=2, tokens=(*proj_parts[1:], second_owned, mixed_done))
    out_parts = send_quarters(quarters)

    dnormed_own, dnormed_other = after((dnormed_own, dnormed_other), projected)
    dnormed_parts, added = sum_partners(me, dnormed_own, dnormed_other)
    attn_terms, gained = call(attention_gain_kernel, array(f32, 1, width), token=True)(
        me, x_all, dnormed_own, dnormed_other, smem=1, tokens=(added,)
    )
    mixed_parts, mixed_added = sum_partners(me, *mixed_halves, gained)
    joined = call(join_kernel, array(bf16, count, quarter, 3 * LANES))(
        *proj_parts, *out_parts, tokens=(mixed_added,)
    )
    half = HEAD_DIM
    attention_owned = swap(joined)
    attention_parts = [attention_owned] + [to_slot(attention_owned, partner) for partner in (1, 2, 3)]
    gains = jnp.concatenate([attn_terms[0], ffn_terms[0], terms[0, :half] + terms[0, half:], terms[1, :half]])
    gains = sum_slots(after((gains.reshape(-1, LANES),), attention_owned)[0])
    gains = sum_chips(after((gains,), *mixed_parts[1:])[0])
    input_grad = call(input_back_kernel, array(bf16, tok_rows, width))(
        *dnormed_parts, tokens[0], residual_grad, attn_norm[None]
    )
    result = residual + sum(part.astype(f32) for part in mixed_parts)
    mixed = jnp.where(row_valid, result, 0.0).astype(bf16)[None]
    stages = [pltpu.VMEM((depth, count * block), f32)] * 3
    unit_shapes = (array(f32, *gate_weight.shape),) * 3
    unit_rows = write_columns(
        first_rows_kernel, unit_shapes, stages + [pltpu.VMEM((depth, count * HEAD_DIM), f32)] * 3, 24
    )(first_all)
    unit_rows = write_columns(second_rows_kernel, unit_shapes, stages, 12)(second_all, *unit_rows)
    query_rows, key_rows, value_rows, out_rows = call(
        attention_rows_kernel,
        tuple(array(f32, *weight.shape) for weight in (query_weight, key_weight, value_weight, out_weight)),
    )(slot, *attention_parts, smem=1, tokens=(unit_rows[0], mixed, input_grad))

    gains = gains.reshape(-1)
    return (
        mixed, input_grad[None], query_rows, key_rows, value_rows, out_rows, *unit_rows, gains[:width], gains[2 * width : 2 * width + half],
        gains[2 * width + half :], gains[width : 2 * width],
    )


def solution(mesh):
    in_specs = (
        P("slot", "seq", None),
        P("slot"),
        P("seq", None),
        P("seq", None),
        P("seq", None),
        P("seq", None),
        P("seq", None),
        P("seq", None),
        P("seq", None),
        P(),
        P(),
        P(),
        P(),
        P("slot", "seq", None),
    )
    out_specs = (
        P("slot", "seq", None),
        P("slot", "seq", None),
        P("seq", None),
        P("seq", None),
        P("seq", None),
        P("seq", None),
        P("seq", None),
        P("seq", None),
        P("seq", None),
        P(),
        P(),
        P(),
        P(),
    )
    by_heads = mesh.shape["seq"] == KV_HEADS and mesh.shape["slot"] == SLOTS_BY_HEADS
    body = heads_body if by_heads else general_body
    return jax.shard_map(body, mesh=mesh, in_specs=in_specs, out_specs=out_specs, check_vma=False)
```
